256 devices in a mesh: space: 128 (over x_lo, z, y, core), dp: 2 (over x_hi).
Axes of the slice: x: 4 (x_hi: 2, x_lo: 2; x = x_hi * 2 + x_lo), y: 4, z: 8, core: 2. Of those that a mesh axis runs over, the one named last changes fastest.
Arguments:
- cell_state: bfloat16 [2, 256, 32, 32, 128], P('dp', 'space'), may hold values from -6 to 6
- cotangent: bfloat16 [2, 256, 32, 32, 128], P('dp', 'space'), may hold values from -6 to 6
- kernels: bfloat16 [2, 3, 3, 128, 128], replicated, may hold values from -0.1875 to 0.1875
- slot_of_tile: int32 [192], replicated, may hold values from 0 to 255, as said below
- neighbours: int32 [192, 8], replicated, may hold values from 0 to 191, as said below
- rotations: int32 [192, 8], replicated, may hold values from 0 to 3
- corner_flags: int32 [192, 4], replicated, may hold values 0 or 1
Outputs:
- next_state: bfloat16 [2, 256, 32, 32, 128], P('dp', 'space')
- cell_grad: bfloat16 [2, 256, 32, 32, 128], P('dp', 'space')
- kernel_grads: float32 [2, 3, 3, 128, 128], replicated
The draws below stay inside these ranges and needn't reach their ends.
Inputs may be any that keep to these rules, and one draw needn't show every extreme that they name: `slot_of_tile`: distinct tiles take distinct slots; slot s lies on space index s // 2; space indices 2p and 2p + 1 together hold three tiles: one of the two indices holds two of them, the other one. neighbours[t, k] for k < 4 is the tile across edge k of tile t, for k >= 4 the tile across corner k - 4, in the tile's own frame; each lies on a space index at most 3 away from tile t's, counted cyclically, and that distance occurs in every draw.
All inputs are finite; a program needn't handle non-finite values.
Results may differ from the reference program's by a relative error of at most 0.011.
Values may be sent and summed in bfloat16 or wider, within the bound.
A program may use at most 128 MiB of HBM per device.

```python
import math
import jax
import jax.numpy as jnp
from jax import lax

CHANNELS = 128
TILE_SIDE = 32
SLOT_DEV = 2
RES_BLOCKS = 1
DILATION_ONE = 2
DILATION_TWO = 4
SAMPLES = 2
TILE_COUNT = 192
SLOT_TOTAL = 256
CONV_LAYERS = 2


def tile_layout(key):
    rows_total = TILE_COUNT // 3
    heavy_first = jax.random.randint(jax.random.fold_in(key, 11), (rows_total,), 0, 2).astype(jnp.int32)
    heavy_first = heavy_first.at[rows_total - 1].set(0)
    ordering = jax.random.permutation(jax.random.fold_in(key, 12), TILE_COUNT).astype(jnp.int32)
    frames = jax.random.randint(jax.random.fold_in(key, 13), (TILE_COUNT,), 0, 4).astype(jnp.int32)
    position = jnp.arange(TILE_COUNT, dtype=jnp.int32)
    row_of = position // 3
    column = position % 3
    heavy = jnp.take(heavy_first, row_of)
    first_dev = jnp.where(heavy == 1, column <= 1, column == 0)
    device = 2 * row_of + jnp.where(first_dev, 0, 1)
    local_slot = jnp.where(heavy == 1, jnp.where(column == 1, 1, 0), jnp.where(column == 2, 1, 0))
    slot_pos = (device * SLOT_DEV + local_slot).astype(jnp.int32)
    row_step = jnp.array([-1, 0, 1, 0, -1, 1, 1, -1], jnp.int32)
    col_step = jnp.array([0, 1, 0, -1, 1, 1, -1, -1], jnp.int32)
    entry = jnp.arange(8, dtype=jnp.int32)
    physical = 4 * (entry // 4)[None, :] + (entry[None, :] % 4 + frames[:, None]) % 4
    near_row = (row_of[:, None] + jnp.take(row_step, physical) + rows_total) % rows_total
    near_col = (column[:, None] + jnp.take(col_step, physical) + 3) % 3
    near_pos = near_row * 3 + near_col
    codes = (frames[:, None] - jnp.take(frames, near_pos) + 4) % 4
    slot_table = jnp.zeros((TILE_COUNT,), jnp.int32).at[ordering].set(slot_pos)
    neighbour_table = jnp.zeros((TILE_COUNT, 8), jnp.int32).at[ordering].set(jnp.take(ordering, near_pos))
    rotation_table = jnp.zeros((TILE_COUNT, 8), jnp.int32).at[ordering].set(codes.astype(jnp.int32))
    return (slot_table, neighbour_table, rotation_table)


def draw_slot_of_tile(key, part):
    return tile_layout(key)[0]


def draw_neighbours(key, part):
    return tile_layout(key)[1]


def draw_rotations(key, part):
    return tile_layout(key)[2]


def with_ends(entries, own_key, smallest, top_value):
    shape = entries.shape
    spot = [jax.random.randint(jax.random.fold_in(own_key, axis), (), 0, shape[axis]) for axis in range(len(shape))]
    entries = entries.at[tuple(spot)].set(smallest)
    longest = shape.index(max(shape))
    spot[longest] = (spot[longest] + 1) % shape[longest]
    return entries.at[tuple(spot)].set(top_value)


def levels(own_key, shape, cuts, low, top_value):
    def one(dim, shards_of):
        heights = jax.random.uniform(jax.random.fold_in(jax.random.fold_in(own_key, 6), dim), (shards_of,), jnp.float32, low / len(cuts), top_value / len(cuts))
        return jnp.repeat(jnp.exp(heights), shape[dim] // shards_of).reshape((-1,) + (1,) * (len(shape) - dim - 1))

    level = one(*cuts[0])
    for cut in cuts[1:]:
        level = level * one(*cut)
    return level


def normal_values(key, dims, width, limit, pieces=(), kind=jnp.bfloat16):
    factor_of = levels(key, dims, pieces, -0.22, 0.18) if pieces else 1.0
    drawn = jax.random.normal(key, dims, jnp.float32) * width * factor_of
    return jnp.minimum(jnp.maximum(drawn, -limit), limit).astype(kind)


def setup_inputs(seed: int = 0) -> dict:
    seeds = jax.random.split(jax.random.key(seed), 8)
    return {
        "cell_state": normal_values(seeds[0], (SAMPLES, SLOT_TOTAL, TILE_SIDE, TILE_SIDE, CHANNELS), 1.0, 6.0, ((0, 2), (1, 128))),
        "cotangent": normal_values(seeds[1], (SAMPLES, SLOT_TOTAL, TILE_SIDE, TILE_SIDE, CHANNELS), 1.0, 6.0, ((0, 2), (1, 128))),
        "kernels": normal_values(seeds[2], (CONV_LAYERS, 3, 3, CHANNELS, CHANNELS), (9 * CHANNELS) ** -0.5, 0.1875),
        "slot_of_tile": draw_slot_of_tile(jax.random.fold_in(seeds[7], 71), 0),
        "neighbours": draw_neighbours(jax.random.fold_in(seeds[7], 71), 0),
        "rotations": draw_rotations(jax.random.fold_in(seeds[7], 71), 0),
        "corner_flags": with_ends((jax.random.randint(seeds[6], (TILE_COUNT, 4), 0, 8) < 1).astype(jnp.int32), jax.random.fold_in(seeds[6], 1), 0, 1),
    }


CONV_AXES = ('NHWC', 'HWIO', 'NHWC')

def boundary(tile_data, rim_depth):
    extent = tile_data.shape[3]
    far = extent - rim_depth
    sides = [tile_data[:, :, :rim_depth], tile_data[:, :, :, far:], tile_data[:, :, far:], tile_data[:, :, :, :rim_depth]]
    blocks = [tile_data[:, :, :rim_depth, far:], tile_data[:, :, far:, far:], tile_data[:, :, far:, :rim_depth], tile_data[:, :, :rim_depth, :rim_depth]]
    strips = jnp.stack([jnp.rot90(sides[quarter], quarter, axes=(2, 3)) for quarter in range(4)], axis=2)
    corners = jnp.stack([jnp.rot90(blocks[quarter], quarter, axes=(2, 3))[:, :, :, ::-1] for quarter in range(4)], axis=2)
    return (strips, corners)

def assemble(tile_data, strips, corners):
    edge_parts = [jnp.rot90(strips[:, :, quarter, ::-1, ::-1], -quarter, axes=(2, 3)) for quarter in range(4)]
    corner_parts = [jnp.rot90(corners[:, :, quarter, ::-1], -quarter, axes=(2, 3)) for quarter in range(4)]
    top_row = jnp.concatenate([corner_parts[3], edge_parts[0], corner_parts[0]], axis=3)
    middle = jnp.concatenate([edge_parts[3], tile_data, edge_parts[1]], axis=3)
    bottom = jnp.concatenate([corner_parts[2], edge_parts[2], corner_parts[1]], axis=3)
    return jnp.concatenate([top_row, middle, bottom], axis=2)

def conv_apply(padded, kernel, spread):
    merged = padded.reshape((-1,) + padded.shape[2:])
    result = lax.conv_general_dilated(merged, kernel, (1, 1), 'VALID', rhs_dilation=(spread, spread), dimension_numbers=CONV_AXES, precision=lax.Precision.HIGHEST, preferred_element_type=jnp.float32)
    return result.reshape(padded.shape[:2] + result.shape[1:])

def widen_tiles(tile_data, rim_depth, neighbours, rotations, corner_keep):
    strips, corners = boundary(tile_data, rim_depth)
    samples_all, tile_total = (tile_data.shape[0], tile_data.shape[1])
    facing = (jnp.arange(8, dtype=jnp.int32)[None, :] % 4 + 2 + rotations) % 4
    select = (neighbours * 4 + facing).astype(jnp.int32)
    flat_strips = strips.reshape((samples_all, tile_total * 4) + strips.shape[3:])
    flat_corners = corners.reshape((samples_all, tile_total * 4) + corners.shape[3:])
    picked = jnp.take(flat_strips, select[:, :4].reshape(-1), axis=1).reshape(strips.shape)
    corner_picked = jnp.take(flat_corners, select[:, 4:].reshape(-1), axis=1).reshape(corners.shape)
    corner_picked = corner_picked * corner_keep[None, :, :, None, None, None]
    return assemble(tile_data, picked, corner_picked)

def reference(cell_state, cotangent, kernels, slot_of_tile, neighbours, rotations, corner_flags):
    corner_keep = (1 - corner_flags).astype(jnp.float32)
    weights = kernels.astype(jnp.float32)
    current = jnp.take(cell_state, slot_of_tile, axis=1)
    stored = []
    for block_at in range(RES_BLOCKS):
        current_wide = current.astype(jnp.float32)
        widened = widen_tiles(current_wide, DILATION_ONE, neighbours, rotations, corner_keep)
        before = conv_apply(widened, weights[2 * block_at], DILATION_ONE)
        hidden = jax.nn.gelu(before).astype(jnp.bfloat16)
        hidden_wide = hidden.astype(jnp.float32)
        widened_two = widen_tiles(hidden_wide, DILATION_TWO, neighbours, rotations, corner_keep)
        branch = conv_apply(widened_two, weights[2 * block_at + 1], DILATION_TWO)
        stored.append((current_wide, before, hidden_wide))
        current = (current_wide + branch).astype(jnp.bfloat16)
    gradient = jnp.take(cotangent, slot_of_tile, axis=1)
    kernel_terms = [None] * (2 * RES_BLOCKS)
    for block_at in reversed(range(RES_BLOCKS)):
        current_wide, before, hidden_wide = stored[block_at]
        gradient_wide = gradient.astype(jnp.float32)
        outer_map = lambda tile_data, kernel: conv_apply(widen_tiles(tile_data, DILATION_TWO, neighbours, rotations, corner_keep), kernel, DILATION_TWO)
        _, back_two = jax.vjp(outer_map, hidden_wide, weights[2 * block_at + 1])
        grad_hidden, kernel_terms[2 * block_at + 1] = back_two(gradient_wide)
        grad_hidden = grad_hidden.astype(jnp.bfloat16)
        _, gelu_back = jax.vjp(jax.nn.gelu, before)
        grad_before = gelu_back(grad_hidden.astype(jnp.float32))[0].astype(jnp.bfloat16)
        inner_map = lambda tile_data, kernel: conv_apply(widen_tiles(tile_data, DILATION_ONE, neighbours, rotations, corner_keep), kernel, DILATION_ONE)
        _, back_one = jax.vjp(inner_map, current_wide, weights[2 * block_at])
        grad_state, kernel_terms[2 * block_at] = back_one(grad_before.astype(jnp.float32))
        gradient = (gradient_wide + grad_state).astype(jnp.bfloat16)
    norm_scale = 1.0 / math.sqrt(SAMPLES * TILE_COUNT * TILE_SIDE * TILE_SIDE)
    blank = jnp.zeros((SAMPLES, SLOT_TOTAL, TILE_SIDE, TILE_SIDE, CHANNELS), jnp.bfloat16)
    next_state = blank.at[:, slot_of_tile].set(current)
    cell_grad = blank.at[:, slot_of_tile].set(gradient)
    kernel_grads = jnp.stack(kernel_terms) * norm_scale
    return (next_state, cell_grad, kernel_grads)
```

```python
import functools
import math

import jax
import jax.numpy as jnp
import numpy as np
from jax import lax
from jax.experimental import pallas as pl
from jax.experimental.pallas import tpu as pltpu
from jax.sharding import PartitionSpec as P

RES_BLOCKS = 1
DILATION_ONE = 2
DILATION_TWO = 4
REACH_DEV = 3


CONV_AXES = ("NHWC", "HWIO", "NHWC")


def as_sent(shard):

    def short(part):
        return part.astype(jnp.bfloat16) if part.dtype == jnp.float32 else part

    return jax.tree.map(short, shard)


def shifted(value, axis, steps):
    count = lax.axis_size(axis)
    pairs = [(source, (source + steps) % count) for source in range(count)]
    return lax.ppermute(value, axis, pairs)


def boundary(tile_data, rim_depth):
    extent = tile_data.shape[3]
    far = extent - rim_depth
    sides = [
        tile_data[:, :, :rim_depth],
        tile_data[:, :, :, far:],
        tile_data[:, :, far:],
        tile_data[:, :, :, :rim_depth],
    ]
    blocks = [
        tile_data[:, :, :rim_depth, far:],
        tile_data[:, :, far:, far:],
        tile_data[:, :, far:, :rim_depth],
        tile_data[:, :, :rim_depth, :rim_depth],
    ]
    strips = jnp.stack(
        [jnp.rot90(sides[quarter], quarter, axes=(2, 3)) for quarter in range(4)], axis=2
    )
    corners = jnp.stack(
        [jnp.rot90(blocks[quarter], quarter, axes=(2, 3))[:, :, :, ::-1] for quarter in range(4)],
        axis=2,
    )
    return (strips, corners)


def assemble(tile_data, strips, corners):
    edge_parts = [
        jnp.rot90(strips[:, :, quarter, ::-1, ::-1], -quarter, axes=(2, 3)) for quarter in range(4)
    ]
    corner_parts = [
        jnp.rot90(corners[:, :, quarter, ::-1], -quarter, axes=(2, 3)) for quarter in range(4)
    ]
    top_row = jnp.concatenate([corner_parts[3], edge_parts[0], corner_parts[0]], axis=3)
    middle = jnp.concatenate([edge_parts[3], tile_data, edge_parts[1]], axis=3)
    bottom = jnp.concatenate([corner_parts[2], edge_parts[2], corner_parts[1]], axis=3)
    return jnp.concatenate([top_row, middle, bottom], axis=2)


def rim_pieces(tile_data, rim_depth):
    strips, corners = boundary(tile_data, rim_depth)
    joined = jnp.concatenate([strips, corners], axis=4)
    return joined.reshape((joined.shape[0], joined.shape[1] * 4) + joined.shape[3:])


def conv_apply(padded, kernel, spread):
    merged = padded.reshape((-1,) + padded.shape[2:])
    result = lax.conv_general_dilated(
        merged,
        kernel,
        (1, 1),
        "VALID",
        rhs_dilation=(spread, spread),
        dimension_numbers=CONV_AXES,
        preferred_element_type=jnp.float32,
    )
    return result.reshape(padded.shape[:2] + result.shape[1:])


def conv_back(grad_out, kernel, spread):
    merged = grad_out.reshape((-1,) + grad_out.shape[2:])
    flipped = jnp.swapaxes(kernel[::-1, ::-1], 2, 3)
    margin = 2 * spread
    result = lax.conv_general_dilated(
        merged,
        flipped,
        (1, 1),
        ((margin, margin), (margin, margin)),
        rhs_dilation=(spread, spread),
        dimension_numbers=CONV_AXES,
        preferred_element_type=jnp.float32,
    )
    return result.reshape(grad_out.shape[:2] + result.shape[1:])


def kernel_grad(padded, grad_out, spread):
    extent = grad_out.shape[2]
    tap_terms = []
    for row_tap in range(3):
        for col_tap in range(3):
            window = padded[
                :,
                :,
                row_tap * spread : row_tap * spread + extent,
                col_tap * spread : col_tap * spread + extent,
            ]
            tap_terms.append(
                lax.dot_general(
                    window,
                    grad_out,
                    (((0, 1, 2, 3), (0, 1, 2, 3)), ((), ())),
                    preferred_element_type=jnp.float32,
                )
            )
    stacked = jnp.stack(tap_terms)
    return stacked.reshape((3, 3) + stacked.shape[1:])


def halo_plan(slot_of_tile, neighbours, rotations, corner_flags, slot_count):
    span_count = lax.axis_size("space")
    myself = lax.axis_index("space")
    tile_count = slot_of_tile.shape[0]
    owned = myself * slot_count + jnp.arange(slot_count, dtype=jnp.int32)
    matches = slot_of_tile[None, :] == owned[:, None]
    present = jnp.any(matches, axis=1)
    tile_here = jnp.sum(
        jnp.where(matches, jnp.arange(tile_count, dtype=jnp.int32)[None, :], 0), axis=1
    )
    nearby = jnp.take(neighbours, tile_here, axis=0)
    turn_code = jnp.take(rotations, tile_here, axis=0)
    facing = (jnp.arange(8, dtype=jnp.int32)[None, :] % 4 + 2 + turn_code) % 4
    source = jnp.take(slot_of_tile, nearby)
    holder = source // slot_count
    within = source % slot_count
    offset = jnp.clip(
        (myself - holder + span_count + REACH_DEV) % span_count - REACH_DEV, -REACH_DEV, REACH_DEV
    )
    select = ((offset + REACH_DEV) * slot_count + within) * 4 + facing
    keep_corner = jnp.take(corner_flags, tile_here, axis=0) == 0
    return (select[:, :4].reshape(-1), select[:, 4:].reshape(-1), keep_corner.reshape(-1), present)


def fetch_near(bundle):
    arrived = {0: bundle}
    for offset in list(range(-REACH_DEV, 0)) + list(range(1, REACH_DEV + 1)):
        arrived[offset] = shifted(as_sent(bundle), "space", offset).astype(bundle.dtype)
    return [arrived[offset] for offset in range(-REACH_DEV, REACH_DEV + 1)]


def return_near(parts):
    total = parts[0]
    for offset in list(range(-REACH_DEV, 0)) + list(range(1, REACH_DEV + 1)):
        total = total + shifted(parts[offset].astype(jnp.bfloat16), "space", -offset).astype(
            jnp.float32
        )
    return total


def halo_forward(tile_data, rim_depth, plan):
    pick_edge, pick_corner, keep_corner = plan[:3]
    samples_here, slot_count, extent = (tile_data.shape[0], tile_data.shape[1], tile_data.shape[2])
    channels = tile_data.shape[4]
    gathered = jnp.concatenate(fetch_near(rim_pieces(tile_data, rim_depth)), axis=1)
    edge_part = jnp.take(gathered, pick_edge, axis=1)[:, :, :, :extent]
    corner_part = jnp.take(gathered, pick_corner, axis=1)[:, :, :, extent:]
    corner_part = jnp.where(
        keep_corner[None, :, None, None, None], corner_part, jnp.zeros((), corner_part.dtype)
    )
    strips = edge_part.reshape(samples_here, slot_count, 4, rim_depth, extent, channels)
    corners = corner_part.reshape(samples_here, slot_count, 4, rim_depth, rim_depth, channels)
    return assemble(tile_data, strips, corners)


def halo_backward(grad_wide, rim_depth, plan):
    pick_edge, pick_corner, keep_corner = plan[:3]
    samples_here, slot_count = (grad_wide.shape[0], grad_wide.shape[1])
    extent = grad_wide.shape[2] - 2 * rim_depth
    channels = grad_wide.shape[4]
    tile_zero = jnp.zeros((samples_here, slot_count, extent, extent, channels), jnp.float32)
    strip_zero = jnp.zeros((samples_here, slot_count, 4, rim_depth, extent, channels), jnp.float32)
    corner_zero = jnp.zeros(
        (samples_here, slot_count, 4, rim_depth, rim_depth, channels), jnp.float32
    )
    _, assemble_back = jax.vjp(assemble, tile_zero, strip_zero, corner_zero)
    grad_tiles, grad_strips, grad_corners = assemble_back(grad_wide)
    pieces = slot_count * 4
    grad_corners = grad_corners.reshape(samples_here, pieces, rim_depth, rim_depth, channels)
    grad_corners = jnp.where(keep_corner[None, :, None, None, None], grad_corners, 0.0)
    spread_out = jnp.zeros(
        (samples_here, (2 * REACH_DEV + 1) * pieces, rim_depth, extent + rim_depth, channels),
        jnp.float32,
    )
    spread_out = spread_out.at[:, pick_edge, :, :extent].add(
        grad_strips.reshape(samples_here, pieces, rim_depth, extent, channels)
    )
    spread_out = spread_out.at[:, pick_corner, :, extent:].add(grad_corners)
    parts = {
        offset: spread_out[:, (offset + REACH_DEV) * pieces : (offset + REACH_DEV + 1) * pieces]
        for offset in range(-REACH_DEV, REACH_DEV + 1)
    }
    returned = return_near(parts)
    _, rim_back = jax.vjp(lambda tile_part: rim_pieces(tile_part, rim_depth), tile_zero)
    return grad_tiles + rim_back(returned)[0]


def shards(cell_state, cotangent, kernels, slot_of_tile, neighbours, rotations, corner_flags):
    plan = halo_plan(slot_of_tile, neighbours, rotations, corner_flags, cell_state.shape[1])
    keep_slot = plan[3][None, :, None, None, None]
    current = cell_state
    block_at = 0
    widened = halo_forward(current, DILATION_ONE, plan)
    before = conv_apply(widened, kernels[2 * block_at], DILATION_ONE)
    hidden = jax.nn.gelu(before).astype(jnp.bfloat16)
    widened_two = halo_forward(hidden, DILATION_TWO, plan)
    branch = conv_apply(widened_two, kernels[2 * block_at + 1], DILATION_TWO)
    stored = [(widened, before, widened_two)]
    current = (current.astype(jnp.float32) + branch).astype(jnp.bfloat16)
    next_state = jnp.where(keep_slot, current, jnp.zeros((), jnp.bfloat16))
    gradient = jnp.where(keep_slot, cotangent, jnp.zeros((), jnp.bfloat16))
    kernel_terms = [None] * (2 * RES_BLOCKS)
    extent = cell_state.shape[2]
    norm_scale = 1.0 / math.sqrt(
        cell_state.shape[0] * lax.axis_size("dp") * slot_of_tile.shape[0] * extent * extent
    )
    for block_at in reversed(range(RES_BLOCKS)):
        widened, before, widened_two = stored[block_at]
        outer_term = kernel_grad(widened_two, gradient, DILATION_TWO)
        kernel_terms[2 * block_at + 1] = outer_term
        grad_hidden = halo_backward(
            conv_back(gradient, kernels[2 * block_at + 1], DILATION_TWO), DILATION_TWO, plan
        ).astype(jnp.bfloat16)
        _, gelu_back = jax.vjp(jax.nn.gelu, before)
        grad_before = gelu_back(grad_hidden.astype(jnp.float32))[0].astype(jnp.bfloat16)
        inner_term = kernel_grad(widened, grad_before, DILATION_ONE)
        kernel_terms[2 * block_at] = inner_term
        returned = halo_backward(
            conv_back(grad_before, kernels[2 * block_at], DILATION_ONE), DILATION_ONE, plan
        )
        gradient = (gradient.astype(jnp.float32) + returned).astype(jnp.bfloat16)
    stacked = jnp.stack(kernel_terms)
    stacked = lax.psum(stacked, ("space", "dp"))
    return (next_state, gradient, stacked * norm_scale)


MESH_ID = pl.DeviceIdType.MESH
SPAN = 128
STRIP_CAP = (1, 2, 2, 2, 2, 1)
CORNER_CAP = 4
PART = 20
MESSAGE = 2 * PART
OFFSETS = (-3, -2, -1, 1, 2, 3)
SELF = 6
T_STRIPS, T_CORNERS, T_STRIP_LIST, T_CORNER_LIST = 0, 6, 12, 26
T_PIECES, T_PRESENT, T_SPARE, T_SIZE = 56, 152, 160, 176
VMEM_BYTES = 56 * 1024 * 1024
F32 = jnp.float32
BF16 = jnp.bfloat16


def cell_order():
    rows, cols = np.meshgrid(np.arange(4), np.arange(4), indexing="ij")
    return ((cols // 2) * 8 + (rows // 2) * 4 + (rows % 2) * 2 + cols % 2).astype(np.int64)


def permutations():
    order = cell_order()
    to_blocks = np.zeros((128, 128), np.float32)
    for row in range(4):
        for col in range(32):
            to_blocks[(col // 4) * 16 + order[row, col % 4], row * 32 + col] = 1
    mats = [to_blocks, to_blocks.T]
    for turn in range(4):
        turned = np.rot90(order, turn)
        small = np.zeros((16, 16), np.float32)
        small[order.reshape(-1), turned.reshape(-1)] = 1
        for flip in range(2):
            line = np.eye(8)[::-1] if flip else np.eye(8)
            mats.append(np.kron(line, small))
    return np.stack(mats)


def turn_matrix(turn, flip):
    return 2 + 2 * turn + flip


def flips(edge, turn):
    side = (edge + 2 + turn) & 1
    once = jnp.where((turn == 1) & (side == 0), 1, 0)
    thrice = jnp.where((turn == 3) & (side == 1), 1, 0)
    return jnp.where(turn == 2, 1, once + thrice)


def ranges_fit(slot_of_tile, neighbours):
    tiles = jnp.arange(slot_of_tile.shape[0], dtype=jnp.int32)
    holder = slot_of_tile // 2
    near = jnp.sum(jnp.where(neighbours[:, :, None] == tiles, holder[None, None, :], 0), axis=2)
    offset = (near - holder[:, None] + 3 + SPAN) % SPAN
    onehot = (offset[:, :, None] == jnp.arange(7, dtype=jnp.int32)).astype(F32)
    counts = jnp.concatenate([onehot[:, :4].sum(axis=1), onehot[:, 4:].sum(axis=1)], axis=1)
    owner = (holder[None, :] == jnp.arange(SPAN, dtype=jnp.int32)[:, None]).astype(F32)
    per_device = jnp.dot(owner, counts, preferred_element_type=F32)
    caps = list(STRIP_CAP[:3]) + [8] + list(STRIP_CAP[3:]) + [CORNER_CAP] * 3 + [8] + [CORNER_CAP] * 3
    return jnp.all(per_device <= jnp.asarray(caps, F32))


def make_plan(me, slot_ref, near_ref, turn_ref, flag_ref, table, tile_at):
    for entry in range(T_SIZE):
        table[entry] = 0
    for rel in range(14):
        tile_at[(me + rel // 2 - 3 + SPAN) % SPAN * 2 + rel % 2] = -1

    def place(step, carry):
        for inner in range(8):
            tile = step * 8 + inner
            tile_at[slot_ref[tile]] = tile
        return carry

    lax.fori_loop(0, slot_ref.shape[0] // 8, place, 0)
    for where, offset in enumerate(OFFSETS):
        strips, corners = jnp.int32(0), jnp.int32(0)
        for slot in range(2):
            tile = tile_at[(me + offset + SPAN) % SPAN * 2 + slot]
            row = jnp.maximum(tile, 0) * 8
            for piece in range(8):
                source = slot_ref[near_ref[row + piece]]
                hit = (tile >= 0) & (source // 2 == me)
                entry = source % 2 * 4 + ((piece + 2 + turn_ref[row + piece]) & 3)
                if piece < 4:
                    table[jnp.where(hit, T_STRIP_LIST + where * 2 + jnp.minimum(strips, 1), T_SPARE)] = entry
                    strips = strips + jnp.where(hit, 1, 0)
                else:
                    table[jnp.where(hit, T_CORNER_LIST + where * 4 + jnp.minimum(corners, 3), T_SPARE)] = entry
                    corners = corners + jnp.where(hit, 1, 0)
        table[T_STRIPS + where] = jnp.minimum(strips, STRIP_CAP[where])
        table[T_CORNERS + where] = jnp.minimum(corners, CORNER_CAP)
    seen = [[jnp.int32(0)] * 7, [jnp.int32(0)] * 7]
    for slot in range(2):
        tile = tile_at[me * 2 + slot]
        row = jnp.maximum(tile, 0)
        valid = jnp.where(tile >= 0, 1, 0)
        table[T_PRESENT + slot] = valid
        for piece in range(8):
            kind = piece // 4
            source = slot_ref[near_ref[row * 8 + piece]]
            turn = turn_ref[row * 8 + piece] & 3
            offset = (source // 2 - me + 3 + SPAN) % SPAN
            offset = jnp.clip(offset, 0, 6)
            where = jnp.where(offset == 3, SELF, jnp.where(offset < 3, offset, offset - 1))
            rank = jnp.int32(0)
            for choice in range(7):
                match = jnp.where(offset == choice, valid, 0)
                rank = rank + match * seen[kind][choice]
                seen[kind][choice] = seen[kind][choice] + match
            keep = valid
            if kind:
                keep = valid * jnp.where(flag_ref[row * 4 + piece - 4] == 0, 1, 0)
            base = T_PIECES + (slot * 8 + piece) * 6
            table[base] = valid
            table[base + 1] = where
            table[base + 2] = jnp.minimum(rank, 3 if kind else 1)
            table[base + 3] = turn
            table[base + 4] = source % 2 * 4 + ((piece + 2 + turn) & 3)
            table[base + 5] = keep


def piece_of(table, slot, piece):
    base = T_PIECES + (slot * 8 + piece) * 6
    return [table[base + field] for field in range(6)]


def blocks(value):
    return value.reshape((-1, 16, 128))


def cells(value):
    return value.reshape((-1, 128))


def product(left, right):
    return jnp.dot(left, right, preferred_element_type=F32)


EDGE_OF = ((0, slice(None)), (slice(None), 7), (7, slice(None)), (slice(None), 0))
CORNER_OF = ((0, 7), (7, 7), (7, 0), (0, 0))
BAND_OF = ((0, slice(1, 9)), (slice(1, 9), 9), (9, slice(1, 9)), (slice(1, 9), 0))
BLOCK_OF = ((0, 9), (9, 9), (9, 0), (0, 0))


def take_rims(tile_ref, strips, corners):
    for slot in range(2):
        for side in range(4):
            strips[slot * 4 + side] = blocks(tile_ref[(slot,) + EDGE_OF[side]])
            corners[slot * 4 + side] = tile_ref[(slot,) + CORNER_OF[side]]


def send_rims(table, strips, corners, send):
    for where in range(6):
        for rank in range(STRIP_CAP[where]):
            entry = table[T_STRIP_LIST + where * 2 + rank]
            send[where, 4 + rank * 8 : 12 + rank * 8] = strips[entry]
        for rank in range(CORNER_CAP):
            send[where, rank] = corners[table[T_CORNER_LIST + where * 4 + rank]]


def corner_turns(table, turns, back):
    parts = []
    for slot in range(2):
        for side in range(4):
            fields = piece_of(table, slot, 4 + side)
            turn = (4 - fields[3]) & 3 if back else fields[3]
            rows = turns[turn_matrix(turn, 0)]
            at = (slot * 4 + side) * 16
            parts.append(rows[at : at + 16] * jnp.where(fields[5] > 0, 1.0, 0.0).astype(BF16))
    return jnp.concatenate(parts, axis=0)


def widen(table, tile_ref, strips, corners, arrived, turns, padded):
    for slot in range(2):
        padded[slot, 1:9, 1:9] = tile_ref[slot]
        for edge in range(4):
            valid, where, rank, turn, entry, keep = piece_of(table, slot, edge)
            own = strips[entry]
            other = arrived[jnp.minimum(where, 5), pl.ds(4 + rank * 8, 8)]
            strip = jnp.where(where == SELF, own, other)
            strip = jnp.where(valid > 0, strip, jnp.zeros_like(strip))
            turned = product(turns[turn_matrix(turn, flips(edge, turn))], cells(strip))
            padded[(slot,) + BAND_OF[edge]] = blocks(turned.astype(BF16))
    stack = []
    for slot in range(2):
        for side in range(4):
            valid, where, rank, turn, entry, keep = piece_of(table, slot, 4 + side)
            block = jnp.where(where == SELF, corners[entry], arrived[jnp.minimum(where, 5), rank])
            stack.append(jnp.where(valid > 0, block, jnp.zeros_like(block)))
    turned = product(corner_turns(table, turns, False), jnp.concatenate(stack, axis=0))
    turned = blocks(turned.astype(BF16))
    for slot in range(2):
        for side in range(4):
            padded[(slot,) + BLOCK_OF[side]] = turned[slot * 4 + side]


def give_back(table, wide, turns, send, strip_sums, corner_sums):
    strip_sums[...] = jnp.zeros_like(strip_sums)
    corner_sums[...] = jnp.zeros_like(corner_sums)
    for slot in range(2):
        for edge in range(4):
            valid, where, rank, turn, entry, keep = piece_of(table, slot, edge)
            band = cells(blocks(wide[(slot,) + BAND_OF[edge]])).astype(BF16)
            turned = product(turns[turn_matrix((4 - turn) & 3, flips(edge, turn))], band)

            @pl.when((valid > 0) & (where == SELF))
            def _():
                strip_sums[entry] += blocks(turned)

            @pl.when((valid > 0) & (where != SELF))
            def _():
                send[jnp.minimum(where, 5), pl.ds(PART + 4 + rank * 8, 8)] = blocks(turned.astype(BF16))

    stack = [wide[(slot,) + BLOCK_OF[side]].astype(BF16) for slot in range(2) for side in range(4)]
    turned = blocks(product(corner_turns(table, turns, True), jnp.concatenate(stack, axis=0)))
    for slot in range(2):
        for side in range(4):
            valid, where, rank, turn, entry, keep = piece_of(table, slot, 4 + side)
            block = turned[slot * 4 + side]

            @pl.when((valid > 0) & (where == SELF))
            def _():
                corner_sums[entry] += block

            @pl.when((valid > 0) & (where != SELF))
            def _():
                send[jnp.minimum(where, 5), PART + rank] = block.astype(BF16)


def take_back(table, arrived, strip_sums, corner_sums):
    for where in range(6):
        for rank in range(STRIP_CAP[where]):

            @pl.when(rank < table[T_STRIPS + where])
            def _():
                entry = table[T_STRIP_LIST + where * 2 + rank]
                strip_sums[entry] += arrived[where, PART + 4 + rank * 8 : PART + 12 + rank * 8].astype(F32)

        for rank in range(CORNER_CAP):

            @pl.when(rank < table[T_CORNERS + where])
            def _():
                entry = table[T_CORNER_LIST + where * 4 + rank]
                corner_sums[entry] += arrived[where, PART + rank].astype(F32)


def add_sums(total, strip_sums, corner_sums):
    for slot in range(2):
        for side in range(4):
            at = (slot,) + EDGE_OF[side]
            total[at] = total[at] + strip_sums[slot * 4 + side]
            at = (slot,) + CORNER_OF[side]
            total[at] = total[at] + corner_sums[slot * 4 + side]


def back_two(
    slot_ref, near_ref, turn_ref, flag_ref, state, cotangent, flipped, turns,
    send, state_blocks, grad_blocks, total, strip_sums, corner_sums, table,
    tile_at, strips, corners, grad_wide, wide,
):
    me = lax.axis_index("space")
    make_plan(me, slot_ref, near_ref, turn_ref, flag_ref, table, tile_at)
    grad_wide[...] = jnp.zeros_like(grad_wide)
    for slot in range(2):
        present = jnp.where(table[T_PRESENT + slot] > 0, 1.0, 0.0)
        for row in range(8):
            moved = product(turns[0], state[slot, row])
            state_blocks[slot, row] = blocks(moved.astype(BF16))
            moved = blocks((product(turns[0], cotangent[slot, row]) * present).astype(BF16))
            grad_blocks[slot, row] = moved
            grad_wide[slot, 2 + row, 2:10] = moved
    take_rims(state_blocks, strips, corners)
    send_rims(table, strips, corners, send)
    for slot in range(2):

        def rows(step, carry):
            taps = [
                cells(grad_wide[slot, pl.ds(step * 2 + 2 - up, 2), 2 - across : 12 - across])
                for up in range(3)
                for across in range(3)
            ]
            result = product(jnp.concatenate(taps, axis=1), flipped[...])
            wide[slot, pl.ds(step * 2, 2)] = result.reshape(2, 10, 16, 128)
            return carry

        lax.fori_loop(0, 5, rows, 0)
        total[slot] = wide[slot, 1:9, 1:9]
    give_back(table, wide, turns, send, strip_sums, corner_sums)


def halves(value):
    return value.astype(F32).reshape(value.shape[0], value.shape[1] * 2, 8, 128)


def shifted_up(upper, lower):
    low = lax.broadcasted_iota(jnp.int32, upper.shape, upper.ndim - 2) < 4
    mixed = jnp.where(low, lower, upper)
    return jnp.concatenate([mixed[..., 4:, :], mixed[..., :4, :]], axis=mixed.ndim - 2)


def gelu_parts(value):
    root = math.sqrt(2.0 / math.pi)
    square = value * value
    bent = jnp.tanh(root * (value + 0.044715 * (value * square)))
    half = 0.5 * (1.0 + bent)
    slope = half + 0.5 * value * (1.0 - bent * bent) * (root * (1.0 + 3 * 0.044715 * square))
    return (value * half, slope)


def middle(
    table, arrived, state_blocks, total, strip_in, corner_in, forward, flipped, turns,
    send, hidden_blocks, total_out, strip_sums, corner_sums, kernel_term,
    strips, corners, padded, even, odd, before, grad_even, grad_odd, grad_turned, wide,
):
    take_rims(state_blocks, strips, corners)
    widen(table, state_blocks, strips, corners, arrived, turns, padded)
    for row in range(10):
        both = [halves(padded[slot, row : row + 1])[0] for slot in range(2)]
        even[row] = jnp.concatenate(both, axis=1).astype(BF16)
    for row in range(9):
        both = [
            shifted_up(halves(padded[slot, row : row + 1])[0], halves(padded[slot, row + 1 : row + 2])[0])
            for slot in range(2)
        ]
        odd[row] = jnp.concatenate(both, axis=1).astype(BF16)

    def window(row, up, across, count):
        source, at = ((odd, row), (even, row + 1), (odd, row + 1))[up]
        return cells(source[pl.ds(at, count), 1 + across : 17 + across])

    def first(row, carry):
        taps = [window(row, up, across, 1) for up in range(3) for across in range(3)]
        result = product(jnp.concatenate(taps, axis=1), forward[...]).reshape(16, 16, 128)
        before[row] = result
        hidden = gelu_parts(result)[0]
        for slot in range(2):
            part = hidden[:, slot * 8 : slot * 8 + 8].reshape(8, 16, 128)
            hidden_blocks[slot, row] = part.astype(BF16)
        return carry

    lax.fori_loop(0, 8, first, 0)
    take_rims(hidden_blocks, strips, corners)
    send_rims(table, strips, corners, send)

    strip_sums[...] = strip_in[...]
    corner_sums[...] = corner_in[...]
    take_back(table, arrived, strip_sums, corner_sums)
    total_out[...] = total[...]
    add_sums(total_out, strip_sums, corner_sums)

    grad_even[...] = jnp.zeros_like(grad_even)
    grad_odd[...] = jnp.zeros_like(grad_odd)

    def pointwise(row, carry):
        both = [
            total_out[slot, row].astype(BF16).astype(F32).reshape(16, 8, 128) for slot in range(2)
        ]
        grad = jnp.concatenate(both, axis=1) * gelu_parts(before[row])[1]
        grad = grad.astype(BF16)
        grad_even[row + 1, 2:18] = grad
        grad_turned[:, pl.ds(pl.multiple_of(row * 256, 256), 256)] = cells(grad).astype(F32).T.astype(BF16)
        return carry

    lax.fori_loop(0, 8, pointwise, 0)
    for row in range(9):
        low = grad_even[row, 2:18].astype(F32)
        high = grad_even[row + 1, 2:18].astype(F32)
        both = [
            shifted_up(low[:, slot * 8 : slot * 8 + 8], high[:, slot * 8 : slot * 8 + 8])
            for slot in range(2)
        ]
        grad_odd[row + 1, 2:18] = jnp.concatenate(both, axis=1).astype(BF16)

    for up in range(3):
        for across in range(3):
            term = product(grad_turned[...], window(0, up, across, 8))
            kernel_term[up * 3 + across] = term.T.reshape(8, 16, 128)

    def returned(row, carry):
        taps = []
        for up in range(3):
            source, at = ((grad_odd, row + 1), (grad_even, row), (grad_odd, row))[up]
            for across in range(3):
                taps.append(cells(source[at, 2 - across : 20 - across]))
        result = product(jnp.concatenate(taps, axis=1), flipped[...]).reshape(18, 16, 128)
        blank = jnp.zeros((1, 8, 128), F32)
        for slot in range(2):
            part = jnp.concatenate([blank, result[:, slot * 8 : slot * 8 + 8], blank], axis=0)
            wide[slot, row] = part.reshape(10, 16, 128)
        return carry

    lax.fori_loop(0, 10, returned, 0)
    give_back(table, wide, turns, send, strip_sums, corner_sums)
    for slot in range(2):
        total_out[slot] = wide[slot, 1:9, 1:9]


def last(
    table, arrived, hidden_blocks, state_blocks, grad_blocks, total, strip_in, corner_in, forward, turns,
    next_state, cell_grad, kernel_term,
    strips, corners, padded, grad_turned, strip_sums, corner_sums, total_out,
):
    take_rims(hidden_blocks, strips, corners)
    widen(table, hidden_blocks, strips, corners, arrived, turns, padded)
    strip_sums[...] = strip_in[...]
    corner_sums[...] = corner_in[...]
    take_back(table, arrived, strip_sums, corner_sums)
    total_out[...] = total[...]
    add_sums(total_out, strip_sums, corner_sums)
    for slot in range(2):
        present = jnp.where(table[T_PRESENT + slot] > 0, 1.0, 0.0)

        def rows(step, carry):
            taps = [
                cells(padded[slot, pl.ds(step * 2 + up, 2), across : across + 8])
                for up in range(3)
                for across in range(3)
            ]
            result = product(jnp.concatenate(taps, axis=1), forward[...])
            fresh = cells(state_blocks[slot, pl.ds(step * 2, 2)]).astype(F32) + result
            fresh = (fresh * present).astype(BF16)
            grad = cells(grad_blocks[slot, pl.ds(step * 2, 2)])
            summed = (grad.astype(F32) + cells(total_out[slot, pl.ds(step * 2, 2)])) * present
            summed = summed.astype(BF16)
            for half in range(2):
                part = slice(half * 128, half * 128 + 128)
                next_state[slot, step * 2 + half] = product(turns[1], fresh[part]).astype(BF16)
                cell_grad[slot, step * 2 + half] = product(turns[1], summed[part]).astype(BF16)
            at = pl.multiple_of(slot * 1024 + step * 256, 256)
            grad_turned[:, pl.ds(at, 256)] = grad.astype(F32).T.astype(BF16)
            return carry

        lax.fori_loop(0, 4, rows, 0)
    for up in range(3):
        for across in range(3):
            term = sum(
                product(
                    grad_turned[:, slot * 1024 : slot * 1024 + 1024],
                    cells(padded[slot, up : up + 8, across : across + 8]),
                )
                for slot in range(2)
            )
            kernel_term[up * 3 + across] = term.T.reshape(8, 16, 128)


def exchange(send, arrived, send_sem, recv_sem):
    me = lax.axis_index("space")
    barrier = pltpu.get_barrier_semaphore()
    peers = [lax.rem(me + offset + SPAN, SPAN) for offset in OFFSETS]
    for peer in peers:
        pl.semaphore_signal(barrier, inc=1, device_id={"space": peer}, device_id_type=MESH_ID)
    pl.semaphore_wait(barrier, 6)
    copies = []
    for where in (2, 3, 1, 4, 0, 5):
        size = 4 + 8 * STRIP_CAP[where]
        for part in range(2):
            copies.append(
                pltpu.make_async_remote_copy(
                    src_ref=send.at[where, pl.ds(part * PART, size)],
                    dst_ref=arrived.at[5 - where, pl.ds(part * PART, size)],
                    send_sem=send_sem.at[where, part],
                    recv_sem=recv_sem.at[5 - where, part],
                    device_id={"space": peers[where]},
                    device_id_type=MESH_ID,
                )
            )
    for copy in copies:
        copy.start()
    for copy in copies:
        copy.wait()


UNITS = 144
HALF = 72
CHUNK = 5


def chunk_start(index):
    return (index * (HALF - CHUNK)) // 15


def reduce_all(
    scale, parts_one, parts_two, out,
    half_send, half_in, plane_send, plane_in, line_in, wide_send, wide_in, pair_send, pair_in, acc, chunk,
    half_sems, plane_sems, line_sems, wide_sems, pair_sems,
):
    me = lax.axis_index("space")
    x_hi = lax.axis_index("dp")
    core, y, z, x_lo = me % 2, me // 2 % 4, me // 8 % 8, me // 64
    plane = (x_hi * 2 + x_lo) * 4 + y

    def at_plane(index):
        return {
            "dp": index // 8,
            "space": ((index // 4 % 2) * 8 + z) * 8 + index % 4 * 2 + core,
        }

    def at_line(index):
        return {"space": (x_lo * 8 + index) * 8 + y * 2 + core}

    mate = {"space": me + 1 - 2 * core}
    barrier = pltpu.get_barrier_semaphore()

    def signal(where):
        pl.semaphore_signal(barrier, inc=1, device_id=where, device_id_type=MESH_ID)

    signal(mate)
    for step in range(1, 16):
        signal(at_plane(lax.rem(plane + step, 16)))
    for step in range(1, 8):
        signal(at_line(lax.rem(z + step, 8)))

    for index in range(9):
        both = (parts_one[index], parts_two[index])
        for half in range(2):
            half_send[half, index * 8 : index * 8 + 8] = both[half].astype(BF16)
    pl.semaphore_wait(barrier, 23)

    def copy(source, target, sems, index, where):
        return pltpu.make_async_remote_copy(
            src_ref=source,
            dst_ref=target,
            send_sem=sems.at[0, index],
            recv_sem=sems.at[1, index],
            device_id=where,
            device_id_type=MESH_ID,
        )

    to_mate = copy(half_send.at[1 - core], half_in, half_sems, 0, mate)
    to_mate.start()
    to_mate.wait()
    for index in range(9):
        mine = jnp.where(core == 0, parts_one[index], parts_two[index])
        got = half_in[index * 8 : index * 8 + 8].astype(F32)
        acc[index * 8 : index * 8 + 8] = mine + got
    plane_send[...] = acc[...].astype(BF16)
    copies = []
    for step in range(1, 16):
        peer = lax.rem(plane + step, 16)
        copies.append(
            copy(plane_send.at[pl.ds(chunk_start(peer), CHUNK)], plane_in.at[step - 1], plane_sems, step - 1, at_plane(peer))
        )
    for one in copies:
        one.start()
    chunk[...] = acc[pl.ds(chunk_start(plane), CHUNK)]
    for step in range(1, 16):
        copies[step - 1].wait()
        chunk[...] += plane_in[step - 1].astype(F32)
    line_in[z] = chunk[...].astype(BF16)
    copies = []
    for step in range(1, 8):
        peer = lax.rem(z + step, 8)
        copies.append(copy(line_in.at[z], line_in.at[z], line_sems, step - 1, at_line(peer)))
    for one in copies:
        one.start()
    for one in copies:
        one.wait()
    total = line_in[0].astype(F32)
    for index in range(1, 8):
        total = total + line_in[index].astype(F32)
    wide_in[plane] = total.astype(BF16)
    copies = []
    for step in range(1, 16):
        peer = lax.rem(plane + step, 16)
        copies.append(copy(wide_in.at[plane], wide_in.at[plane], wide_sems, step - 1, at_plane(peer)))
    for one in copies:
        one.start()
    for one in copies:
        one.wait()
    for index in range(16):
        pair_send[chunk_start(index) : chunk_start(index) + CHUNK] = wide_in[index]
    to_mate = copy(pair_send, pair_in, pair_sems, 0, mate)
    to_mate.start()
    to_mate.wait()
    mine, other = pair_send[...].astype(F32) * scale, pair_in[...].astype(F32) * scale
    out[0] = jnp.where(core == 0, mine, other)
    out[1] = jnp.where(core == 0, other, mine)


def vmem(shape, kind):
    return pltpu.VMEM(shape, kind)


def specs(kinds):
    return [
        pl.BlockSpec(memory_space=pltpu.SMEM if kind == "s" else pltpu.VMEM if kind == "v" else pl.ANY)
        for kind in kinds
    ]


def shape(dims, kind):
    return jax.ShapeDtypeStruct(dims, kind)


def params(**extra):
    return pltpu.CompilerParams(vmem_limit_bytes=VMEM_BYTES, **extra)


TILES = (2, 8, 8, 16, 128)
STRIPS = (8, 8, 16, 128)
CORNERS = (8, 16, 128)
SENT = (6, MESSAGE, 16, 128)


def swap(send, ident):
    return pl.pallas_call(
        exchange,
        out_shape=shape(SENT, BF16),
        in_specs=specs("a"),
        out_specs=specs("a")[0],
        scratch_shapes=[pltpu.SemaphoreType.DMA((6, 2)), pltpu.SemaphoreType.DMA((6, 2))],
        compiler_params=pltpu.CompilerParams(collective_id=ident, has_side_effects=True),
    )(send)


def fast_shards(cell_state, cotangent, kernels, slot_of_tile, neighbours, rotations, corner_flags):
    turns = jnp.asarray(permutations(), BF16)
    forward = kernels.reshape(2, 1152, 128)
    flipped = jnp.swapaxes(kernels, 3, 4).reshape(2, 1152, 128)
    state = cell_state.reshape(2, 8, 128, 128)
    grad = cotangent.reshape(2, 8, 128, 128)
    send, state_blocks, grad_blocks, total, strip_sums, corner_sums, table = pl.pallas_call(
        back_two,
        out_shape=[
            shape(SENT, BF16), shape(TILES, BF16), shape(TILES, BF16), shape(TILES, F32),
            shape(STRIPS, F32), shape(CORNERS, F32), shape((T_SIZE,), jnp.int32),
        ],
        in_specs=specs("ssssvvvv"),
        out_specs=specs("vvvvvvs"),
        scratch_shapes=[
            pltpu.SMEM((2 * SPAN,), jnp.int32),
            vmem(STRIPS, BF16), vmem(CORNERS, BF16),
            vmem((2, 12, 12, 16, 128), BF16), vmem((2, 10, 10, 16, 128), F32),
        ],
        compiler_params=params(),
    )(
        slot_of_tile, neighbours.reshape(-1), rotations.reshape(-1), corner_flags.reshape(-1),
        state, grad, flipped[1], turns,
    )
    arrived = swap(send, 1)
    send, hidden_blocks, total, strip_sums, corner_sums, kernel_one = pl.pallas_call(
        middle,
        out_shape=[
            shape(SENT, BF16), shape(TILES, BF16), shape(TILES, F32),
            shape(STRIPS, F32), shape(CORNERS, F32), shape((9, 8, 16, 128), F32),
        ],
        in_specs=specs("svvvvvvvv"),
        out_specs=specs("vvvvvv"),
        scratch_shapes=[
            vmem(STRIPS, BF16), vmem(CORNERS, BF16),
            vmem((2, 10, 10, 16, 128), BF16),
            vmem((10, 20, 16, 128), BF16), vmem((9, 20, 16, 128), BF16),
            vmem((8, 16, 16, 128), F32),
            vmem((10, 20, 16, 128), BF16), vmem((11, 20, 16, 128), BF16),
            vmem((128, 2048), BF16), vmem((2, 10, 10, 16, 128), F32),
        ],
        compiler_params=params(),
    )(table, arrived, state_blocks, total, strip_sums, corner_sums, forward[0], flipped[0], turns)
    arrived = swap(send, 2)
    next_state, cell_grad, kernel_two = pl.pallas_call(
        last,
        out_shape=[shape((2, 8, 128, 128), BF16), shape((2, 8, 128, 128), BF16), shape((9, 8, 16, 128), F32)],
        in_specs=specs("svvvvvvvvv"),
        out_specs=specs("vvv"),
        scratch_shapes=[
            vmem(STRIPS, BF16), vmem(CORNERS, BF16),
            vmem((2, 10, 10, 16, 128), BF16), vmem((128, 2048), BF16),
            vmem(STRIPS, F32), vmem(CORNERS, F32), vmem(TILES, F32),
        ],
        compiler_params=params(),
    )(table, arrived, hidden_blocks, state_blocks, grad_blocks, total, strip_sums, corner_sums, forward[1], turns)
    scale = 1.0 / math.sqrt(
        cell_state.shape[0] * lax.axis_size("dp") * slot_of_tile.shape[0] * cell_state.shape[2] ** 2
    )
    sums = pl.pallas_call(
        functools.partial(reduce_all, scale),
        out_shape=shape((2, HALF, 16, 128), F32),
        in_specs=specs("vv"),
        out_specs=specs("v")[0],
        scratch_shapes=[
            vmem((2, HALF, 16, 128), BF16), vmem((HALF, 16, 128), BF16),
            vmem((HALF, 16, 128), BF16), vmem((15, CHUNK, 16, 128), BF16),
            vmem((8, CHUNK, 16, 128), BF16),
            vmem((CHUNK, 16, 128), BF16), vmem((16, CHUNK, 16, 128), BF16),
            vmem((HALF, 16, 128), BF16), vmem((HALF, 16, 128), BF16),
            vmem((HALF, 16, 128), F32), vmem((CHUNK, 16, 128), F32),
            pltpu.SemaphoreType.DMA((2, 1)), pltpu.SemaphoreType.DMA((2, 15)),
            pltpu.SemaphoreType.DMA((2, 7)), pltpu.SemaphoreType.DMA((2, 15)),
            pltpu.SemaphoreType.DMA((2, 1)),
        ],
        compiler_params=params(collective_id=3, has_side_effects=True),
    )(kernel_one, kernel_two)
    return (
        next_state.reshape(cell_state.shape),
        cell_grad.reshape(cell_state.shape),
        sums.reshape(kernels.shape),
    )


def routed(*arrays):
    fits = ranges_fit(arrays[3], arrays[4])
    return lax.cond(fits, fast_shards, shards, *arrays)


def solution(mesh):
    in_specs = (
        P("dp", "space", None, None, None),
        P("dp", "space", None, None, None),
        P(),
        P(),
        P(),
        P(),
        P(),
    )
    out_specs = (P("dp", "space", None, None, None), P("dp", "space", None, None, None), P())
    return jax.shard_map(routed, mesh=mesh, in_specs=in_specs, out_specs=out_specs, check_vma=False)
```

```python
import functools
import math

import jax
import jax.numpy as jnp
import numpy as np
from jax import lax
from jax.experimental import pallas as pl
from jax.experimental.pallas import tpu as pltpu
from jax.sharding import PartitionSpec as P

RES_BLOCKS = 1
DILATION_ONE = 2
DILATION_TWO = 4
REACH_DEV = 3


CONV_AXES = ("NHWC", "HWIO", "NHWC")


def as_sent(shard):

    def short(part):
        return part.astype(jnp.bfloat16) if part.dtype == jnp.float32 else part

    return jax.tree.map(short, shard)


def shifted(value, axis, steps):
    count = lax.axis_size(axis)
    pairs = [(source, (source + steps) % count) for source in range(count)]
    return lax.ppermute(value, axis, pairs)


def boundary(tile_data, rim_depth):
    extent = tile_data.shape[3]
    far = extent - rim_depth
    sides = [
        tile_data[:, :, :rim_depth],
        tile_data[:, :, :, far:],
        tile_data[:, :, far:],
        tile_data[:, :, :, :rim_depth],
    ]
    blocks = [
        tile_data[:, :, :rim_depth, far:],
        tile_data[:, :, far:, far:],
        tile_data[:, :, far:, :rim_depth],
        tile_data[:, :, :rim_depth, :rim_depth],
    ]
    strips = jnp.stack(
        [jnp.rot90(sides[quarter], quarter, axes=(2, 3)) for quarter in range(4)], axis=2
    )
    corners = jnp.stack(
        [jnp.rot90(blocks[quarter], quarter, axes=(2, 3))[:, :, :, ::-1] for quarter in range(4)],
        axis=2,
    )
    return (strips, corners)


def assemble(tile_data, strips, corners):
    edge_parts = [
        jnp.rot90(strips[:, :, quarter, ::-1, ::-1], -quarter, axes=(2, 3)) for quarter in range(4)
    ]
    corner_parts = [
        jnp.rot90(corners[:, :, quarter, ::-1], -quarter, axes=(2, 3)) for quarter in range(4)
    ]
    top_row = jnp.concatenate([corner_parts[3], edge_parts[0], corner_parts[0]], axis=3)
    middle = jnp.concatenate([edge_parts[3], tile_data, edge_parts[1]], axis=3)
    bottom = jnp.concatenate([corner_parts[2], edge_parts[2], corner_parts[1]], axis=3)
    return jnp.concatenate([top_row, middle, bottom], axis=2)


def rim_pieces(tile_data, rim_depth):
    strips, corners = boundary(tile_data, rim_depth)
    joined = jnp.concatenate([strips, corners], axis=4)
    return joined.reshape((joined.shape[0], joined.shape[1] * 4) + joined.shape[3:])


def conv_apply(padded, kernel, spread):
    merged = padded.reshape((-1,) + padded.shape[2:])
    result = lax.conv_general_dilated(
        merged,
        kernel,
        (1, 1),
        "VALID",
        rhs_dilation=(spread, spread),
        dimension_numbers=CONV_AXES,
        preferred_element_type=jnp.float32,
    )
    return result.reshape(padded.shape[:2] + result.shape[1:])


def conv_back(grad_out, kernel, spread):
    merged = grad_out.reshape((-1,) + grad_out.shape[2:])
    flipped = jnp.swapaxes(kernel[::-1, ::-1], 2, 3)
    margin = 2 * spread
    result = lax.conv_general_dilated(
        merged,
        flipped,
        (1, 1),
        ((margin, margin), (margin, margin)),
        rhs_dilation=(spread, spread),
        dimension_numbers=CONV_AXES,
        preferred_element_type=jnp.float32,
    )
    return result.reshape(grad_out.shape[:2] + result.shape[1:])


def kernel_grad(padded, grad_out, spread):
    extent = grad_out.shape[2]
    tap_terms = []
    for row_tap in range(3):
        for col_tap in range(3):
            window = padded[
                :,
                :,
                row_tap * spread : row_tap * spread + extent,
                col_tap * spread : col_tap * spread + extent,
            ]
            tap_terms.append(
                lax.dot_general(
                    window,
                    grad_out,
                    (((0, 1, 2, 3), (0, 1, 2, 3)), ((), ())),
                    preferred_element_type=jnp.float32,
                )
            )
    stacked = jnp.stack(tap_terms)
    return stacked.reshape((3, 3) + stacked.shape[1:])


def halo_plan(slot_of_tile, neighbours, rotations, corner_flags, slot_count):
    span_count = lax.axis_size("space")
    myself = lax.axis_index("space")
    tile_count = slot_of_tile.shape[0]
    owned = myself * slot_count + jnp.arange(slot_count, dtype=jnp.int32)
    matches = slot_of_tile[None, :] == owned[:, None]
    present = jnp.any(matches, axis=1)
    tile_here = jnp.sum(
        jnp.where(matches, jnp.arange(tile_count, dtype=jnp.int32)[None, :], 0), axis=1
    )
    nearby = jnp.take(neighbours, tile_here, axis=0)
    turn_code = jnp.take(rotations, tile_here, axis=0)
    facing = (jnp.arange(8, dtype=jnp.int32)[None, :] % 4 + 2 + turn_code) % 4
    source = jnp.take(slot_of_tile, nearby)
    holder = source // slot_count
    within = source % slot_count
    offset = jnp.clip(
        (myself - holder + span_count + REACH_DEV) % span_count - REACH_DEV, -REACH_DEV, REACH_DEV
    )
    select = ((offset + REACH_DEV) * slot_count + within) * 4 + facing
    keep_corner = jnp.take(corner_flags, tile_here, axis=0) == 0
    return (select[:, :4].reshape(-1), select[:, 4:].reshape(-1), keep_corner.reshape(-1), present)


def fetch_near(bundle):
    arrived = {0: bundle}
    for offset in list(range(-REACH_DEV, 0)) + list(range(1, REACH_DEV + 1)):
        arrived[offset] = shifted(as_sent(bundle), "space", offset).astype(bundle.dtype)
    return [arrived[offset] for offset in range(-REACH_DEV, REACH_DEV + 1)]


def return_near(parts):
    total = parts[0]
    for offset in list(range(-REACH_DEV, 0)) + list(range(1, REACH_DEV + 1)):
        total = total + shifted(parts[offset].astype(jnp.bfloat16), "space", -offset).astype(
            jnp.float32
        )
    return total


def halo_forward(tile_data, rim_depth, plan):
    pick_edge, pick_corner, keep_corner = plan[:3]
    samples_here, slot_count, extent = (tile_data.shape[0], tile_data.shape[1], tile_data.shape[2])
    channels = tile_data.shape[4]
    gathered = jnp.concatenate(fetch_near(rim_pieces(tile_data, rim_depth)), axis=1)
    edge_part = jnp.take(gathered, pick_edge, axis=1)[:, :, :, :extent]
    corner_part = jnp.take(gathered, pick_corner, axis=1)[:, :, :, extent:]
    corner_part = jnp.where(
        keep_corner[None, :, None, None, None], corner_part, jnp.zeros((), corner_part.dtype)
    )
    strips = edge_part.reshape(samples_here, slot_count, 4, rim_depth, extent, channels)
    corners = corner_part.reshape(samples_here, slot_count, 4, rim_depth, rim_depth, channels)
    return assemble(tile_data, strips, corners)


def halo_backward(grad_wide, rim_depth, plan):
    pick_edge, pick_corner, keep_corner = plan[:3]
    samples_here, slot_count = (grad_wide.shape[0], grad_wide.shape[1])
    extent = grad_wide.shape[2] - 2 * rim_depth
    channels = grad_wide.shape[4]
    tile_zero = jnp.zeros((samples_here, slot_count, extent, extent, channels), jnp.float32)
    strip_zero = jnp.zeros((samples_here, slot_count, 4, rim_depth, extent, channels), jnp.float32)
    corner_zero = jnp.zeros(
        (samples_here, slot_count, 4, rim_depth, rim_depth, channels), jnp.float32
    )
    _, assemble_back = jax.vjp(assemble, tile_zero, strip_zero, corner_zero)
    grad_tiles, grad_strips, grad_corners = assemble_back(grad_wide)
    pieces = slot_count * 4
    grad_corners = grad_corners.reshape(samples_here, pieces, rim_depth, rim_depth, channels)
    grad_corners = jnp.where(keep_corner[None, :, None, None, None], grad_corners, 0.0)
    spread_out = jnp.zeros(
        (samples_here, (2 * REACH_DEV + 1) * pieces, rim_depth, extent + rim_depth, channels),
        jnp.float32,
    )
    spread_out = spread_out.at[:, pick_edge, :, :extent].add(
        grad_strips.reshape(samples_here, pieces, rim_depth, extent, channels)
    )
    spread_out = spread_out.at[:, pick_corner, :, extent:].add(grad_corners)
    parts = {
        offset: spread_out[:, (offset + REACH_DEV) * pieces : (offset + REACH_DEV + 1) * pieces]
        for offset in range(-REACH_DEV, REACH_DEV + 1)
    }
    returned = return_near(parts)
    _, rim_back = jax.vjp(lambda tile_part: rim_pieces(tile_part, rim_depth), tile_zero)
    return grad_tiles + rim_back(returned)[0]


def shards(cell_state, cotangent, kernels, slot_of_tile, neighbours, rotations, corner_flags):
    plan = halo_plan(slot_of_tile, neighbours, rotations, corner_flags, cell_state.shape[1])
    keep_slot = plan[3][None, :, None, None, None]
    current = cell_state
    block_at = 0
    widened = halo_forward(current, DILATION_ONE, plan)
    before = conv_apply(widened, kernels[2 * block_at], DILATION_ONE)
    hidden = jax.nn.gelu(before).astype(jnp.bfloat16)
    widened_two = halo_forward(hidden, DILATION_TWO, plan)
    branch = conv_apply(widened_two, kernels[2 * block_at + 1], DILATION_TWO)
    stored = [(widened, before, widened_two)]
    current = (current.astype(jnp.float32) + branch).astype(jnp.bfloat16)
    next_state = jnp.where(keep_slot, current, jnp.zeros((), jnp.bfloat16))
    gradient = jnp.where(keep_slot, cotangent, jnp.zeros((), jnp.bfloat16))
    kernel_terms = [None] * (2 * RES_BLOCKS)
    extent = cell_state.shape[2]
    norm_scale = 1.0 / math.sqrt(
        cell_state.shape[0] * lax.axis_size("dp") * slot_of_tile.shape[0] * extent * extent
    )
    for block_at in reversed(range(RES_BLOCKS)):
        widened, before, widened_two = stored[block_at]
        outer_term = kernel_grad(widened_two, gradient, DILATION_TWO)
        kernel_terms[2 * block_at + 1] = outer_term
        grad_hidden = halo_backward(
            conv_back(gradient, kernels[2 * block_at + 1], DILATION_TWO), DILATION_TWO, plan
        ).astype(jnp.bfloat16)
        _, gelu_back = jax.vjp(jax.nn.gelu, before)
        grad_before = gelu_back(grad_hidden.astype(jnp.float32))[0].astype(jnp.bfloat16)
        inner_term = kernel_grad(widened, grad_before, DILATION_ONE)
        kernel_terms[2 * block_at] = inner_term
        returned = halo_backward(
            conv_back(grad_before, kernels[2 * block_at], DILATION_ONE), DILATION_ONE, plan
        )
        gradient = (gradient.astype(jnp.float32) + returned).astype(jnp.bfloat16)
    stacked = jnp.stack(kernel_terms)
    stacked = lax.psum(stacked, ("space", "dp"))
    return (next_state, gradient, stacked * norm_scale)


MESH_ID = pl.DeviceIdType.MESH
SPAN = 128
STRIP_CAP = (1, 2, 2, 2, 2, 1)
CORNER_CAP = 4
PART = 20
OFFSETS = (-3, -2, -1, 1, 2, 3)
ORDER = (2, 3, 1, 4, 0, 5)
SELF = 6
NOT_STRIP, NOT_CORNER = 20, 32
T_STRIP_LIST, T_CORNER_LIST, T_GIVE_STRIP, T_GIVE_CORNER = 0, 12, 36, 48
T_ADD_STRIP, T_ADD_CORNER, T_PIECES, T_PRESENT = 72, 88, 104, 200
T_OVER, T_SPARE, T_COUNT, T_SIZE = 202, 203, 208, 224
VMEM_BYTES = 56 * 1024 * 1024
F32 = jnp.float32
BF16 = jnp.bfloat16


def cell_order():
    rows, cols = np.meshgrid(np.arange(4), np.arange(4), indexing="ij")
    return ((cols // 2) * 8 + (rows // 2) * 4 + (rows % 2) * 2 + cols % 2).astype(np.int64)


def permutations():
    order = cell_order()
    to_blocks = np.zeros((128, 128), np.float32)
    for row in range(4):
        for col in range(32):
            to_blocks[(col // 4) * 16 + order[row, col % 4], row * 32 + col] = 1
    mats = [to_blocks, to_blocks.T]
    for turn in range(4):
        turned = np.rot90(order, turn)
        small = np.zeros((16, 16), np.float32)
        small[order.reshape(-1), turned.reshape(-1)] = 1
        for flip in range(2):
            line = np.eye(8)[::-1] if flip else np.eye(8)
            mats.append(np.kron(line, small))
    return np.stack(mats)


def turn_matrix(turn, flip):
    return 2 + 2 * turn + flip


def flips(edge, turn):
    side = (edge + 2 + turn) & 1
    once = jnp.where((turn == 1) & (side == 0), 1, 0)
    thrice = jnp.where((turn == 3) & (side == 1), 1, 0)
    return jnp.where(turn == 2, 1, once + thrice)


def plan_kernel(slot_ref, near_ref, turn_ref, flag_ref, table, tile_at):
    me = lax.axis_index("space")
    for entry in range(T_SIZE):
        table[entry] = 0
    for entry in range(16):
        table[T_ADD_STRIP + entry] = NOT_STRIP
        table[T_ADD_CORNER + entry] = NOT_CORNER
    for rel in range(14):
        tile_at[(me + rel // 2 - 3 + SPAN) % SPAN * 2 + rel % 2] = -1

    def place(step, carry):
        for inner in range(16):
            tile = step * 16 + inner
            tile_at[slot_ref[tile]] = tile
        return carry

    lax.fori_loop(0, slot_ref.shape[0] // 16, place, 0)
    over = jnp.int32(0)

    def contribute(hit, kind, entry, code):
        counter = T_COUNT + kind * 8 + entry
        count = table[counter]
        table[jnp.where(hit, counter, T_SPARE)] = count + 1
        place_at = (T_ADD_CORNER if kind else T_ADD_STRIP) + entry * 2 + jnp.minimum(count, 1)
        table[jnp.where(hit, place_at, T_SPARE)] = code
        return jnp.where(hit & (count > 1), 1, 0)

    for where, offset in enumerate(OFFSETS):
        seen = [jnp.int32(0), jnp.int32(0)]
        for slot in range(2):
            tile = tile_at[(me + offset + SPAN) % SPAN * 2 + slot]
            row = jnp.maximum(tile, 0)
            for piece in range(8):
                kind = piece // 4
                source = slot_ref[near_ref[row, piece]]
                hit = (tile >= 0) & (source // 2 == me)
                entry = source % 2 * 4 + ((piece + 2 + turn_ref[row, piece]) & 3)
                cap = CORNER_CAP if kind else STRIP_CAP[where]
                rank = jnp.minimum(seen[kind], cap - 1)
                over = over + jnp.where(hit & (seen[kind] >= cap), 1, 0)
                seen[kind] = seen[kind] + jnp.where(hit, 1, 0)
                width = 4 if kind else 2
                place_at = (T_CORNER_LIST if kind else T_STRIP_LIST) + where * width + rank
                table[jnp.where(hit, place_at, T_SPARE)] = entry
                over = over + contribute(hit, kind, entry, where * width + rank)
    seen = [[jnp.int32(0)] * 7, [jnp.int32(0)] * 7]
    for slot in range(2):
        tile = tile_at[me * 2 + slot]
        row = jnp.maximum(tile, 0)
        valid = jnp.where(tile >= 0, 1, 0)
        table[T_PRESENT + slot] = valid
        for piece in range(8):
            kind = piece // 4
            source = slot_ref[near_ref[row, piece]]
            turn = turn_ref[row, piece] & 3
            offset = jnp.clip((source // 2 - me + 3 + SPAN) % SPAN, 0, 6)
            where = jnp.where(offset == 3, SELF, jnp.where(offset < 3, offset, offset - 1))
            rank = jnp.int32(0)
            for choice in range(7):
                match = jnp.where(offset == choice, valid, 0)
                rank = rank + match * seen[kind][choice]
                seen[kind][choice] = seen[kind][choice] + match
            rank = jnp.minimum(rank, 3 if kind else 1)
            keep = valid
            if kind:
                keep = valid * jnp.where(flag_ref[row, piece - 4] == 0, 1, 0)
            entry = source % 2 * 4 + ((piece + 2 + turn) & 3)
            base = T_PIECES + (slot * 8 + piece) * 6
            table[base] = valid
            table[base + 1] = where
            table[base + 2] = rank
            table[base + 3] = turn
            table[base + 4] = entry
            table[base + 5] = keep
            mine = slot * 4 + piece % 4
            own = (valid > 0) & (where == SELF)
            away = (valid > 0) & (where != SELF)
            place_at = (T_GIVE_CORNER if kind else T_GIVE_STRIP) + where * (4 if kind else 2) + rank
            table[jnp.where(away, place_at, T_SPARE)] = mine
            over = over + contribute(own, kind, entry, (24 if kind else 12) + mine)
    table[T_OVER] = over


def piece_of(table, slot, piece):
    base = T_PIECES + (slot * 8 + piece) * 6
    return [table[base + field] for field in range(6)]


def blocks(value):
    return value.reshape((-1, 16, 128))


def cells(value):
    return value.reshape((-1, 128))


def product(left, right):
    return jnp.dot(left, right, preferred_element_type=F32)


EDGE_OF = ((0, slice(None)), (slice(None), 7), (7, slice(None)), (slice(None), 0))
CORNER_OF = ((0, 7), (7, 7), (7, 0), (0, 0))
BAND_OF = ((0, slice(1, 9)), (slice(1, 9), 9), (9, slice(1, 9)), (slice(1, 9), 0))
BLOCK_OF = ((0, 9), (9, 9), (9, 0), (0, 0))


def take_rims(tile_ref, strips, corners):
    for slot in range(2):
        for side in range(4):
            strips[slot * 4 + side] = blocks(tile_ref[(slot,) + EDGE_OF[side]])
            corners[slot * 4 + side] = tile_ref[(slot,) + CORNER_OF[side]]


def send_rims(table, strips, corners, send, strip_list=T_STRIP_LIST, corner_list=T_CORNER_LIST):
    for where in range(6):
        for rank in range(STRIP_CAP[where]):
            send[where, 4 + rank * 8 : 12 + rank * 8] = strips[table[strip_list + where * 2 + rank]]
        for rank in range(CORNER_CAP):
            send[where, rank] = corners[table[corner_list + where * 4 + rank]]


def corner_turns(table, turns, back):
    parts = []
    for slot in range(2):
        for side in range(4):
            fields = piece_of(table, slot, 4 + side)
            turn = (4 - fields[3]) & 3 if back else fields[3]
            rows = turns[turn_matrix(turn, 0)]
            at = (slot * 4 + side) * 16
            parts.append(rows[at : at + 16] * jnp.where(fields[5] > 0, 1.0, 0.0).astype(BF16))
    return jnp.concatenate(parts, axis=0)


def widen(table, tile_ref, strips, corners, arrived, turns, padded):
    for slot in range(2):
        padded[slot, 1:9, 1:9] = tile_ref[slot]
        for edge in range(4):
            valid, where, rank, turn, entry, keep = piece_of(table, slot, edge)
            own = strips[entry]
            other = arrived[jnp.minimum(where, 5), pl.ds(4 + rank * 8, 8)]
            strip = jnp.where(where == SELF, own, other)
            strip = jnp.where(valid > 0, strip, jnp.zeros_like(strip))
            turned = product(turns[turn_matrix(turn, flips(edge, turn))], cells(strip))
            padded[(slot,) + BAND_OF[edge]] = blocks(turned.astype(BF16))
    stack = []
    for slot in range(2):
        for side in range(4):
            valid, where, rank, turn, entry, keep = piece_of(table, slot, 4 + side)
            block = jnp.where(where == SELF, corners[entry], arrived[jnp.minimum(where, 5), rank])
            stack.append(jnp.where(valid > 0, block, jnp.zeros_like(block)))
    turned = product(corner_turns(table, turns, False), jnp.concatenate(stack, axis=0))
    turned = blocks(turned.astype(BF16))
    for slot in range(2):
        for side in range(4):
            padded[(slot,) + BLOCK_OF[side]] = turned[slot * 4 + side]


def give_back(table, wide, turns, send, strips, corners):
    for slot in range(2):
        for edge in range(4):
            valid, where, rank, turn, entry, keep = piece_of(table, slot, edge)
            band = cells(blocks(wide[(slot,) + BAND_OF[edge]])).astype(BF16)
            turned = product(turns[turn_matrix((4 - turn) & 3, flips(edge, turn))], band)
            strips[slot * 4 + edge] = blocks(turned.astype(BF16))
    stack = [wide[(slot,) + BLOCK_OF[side]].astype(BF16) for slot in range(2) for side in range(4)]
    turned = product(corner_turns(table, turns, True), jnp.concatenate(stack, axis=0))
    corners[...] = blocks(turned.astype(BF16))
    send_rims(table, strips, corners, send, T_GIVE_STRIP, T_GIVE_CORNER)


def take_back(table, arrived, strips, corners, total):
    for slot in range(2):
        for side in range(4):
            at = (slot,) + EDGE_OF[side]
            value = total[at]
            for extra in range(2):
                code = table[T_ADD_STRIP + (slot * 4 + side) * 2 + extra]
                far = jnp.minimum(code, 11)
                near = jnp.clip(code - 12, 0, 7)
                part = jnp.where(code < 12, arrived[far // 2, pl.ds(4 + far % 2 * 8, 8)], strips[near])
                part = jnp.where(code == NOT_STRIP, jnp.zeros_like(part), part)
                value = value + part.astype(F32)
            total[at] = value
    for slot in range(2):
        for side in range(4):
            at = (slot,) + CORNER_OF[side]
            value = total[at]
            for extra in range(2):
                code = table[T_ADD_CORNER + (slot * 4 + side) * 2 + extra]
                far = jnp.minimum(code, 23)
                near = jnp.clip(code - 24, 0, 7)
                part = jnp.where(code < 24, arrived[far // 4, far % 4], corners[near])
                part = jnp.where(code == NOT_CORNER, jnp.zeros_like(part), part)
                value = value + part.astype(F32)
            total[at] = value


def halves(value):
    return value.astype(F32).reshape(value.shape[0], value.shape[1] * 2, 8, 128)


def shifted_up(upper, lower):
    low = lax.broadcasted_iota(jnp.int32, upper.shape, upper.ndim - 2) < 4
    mixed = jnp.where(low, lower, upper)
    return jnp.concatenate([mixed[..., 4:, :], mixed[..., :4, :]], axis=mixed.ndim - 2)


def gelu_parts(value):
    root = math.sqrt(2.0 / math.pi)
    square = value * value
    bent = jnp.tanh(root * (value + 0.044715 * (value * square)))
    half = 0.5 * (1.0 + bent)
    slope = half + 0.5 * value * (1.0 - bent * bent) * (root * (1.0 + 3 * 0.044715 * square))
    return (value * half, slope)


UNITS = 72
HALF = 37
CHUNK = 3


def chunk_start(index):
    return (index * (HALF - CHUNK)) // 15


class Swap:
    def __init__(self, me, send, arrived, sems):
        self.copies = []
        for where in ORDER:
            size = 4 + 8 * STRIP_CAP[where]
            self.copies.append(
                pltpu.make_async_remote_copy(
                    src_ref=send.at[where, pl.ds(0, size)],
                    dst_ref=arrived.at[5 - where, pl.ds(0, size)],
                    send_sem=sems.at[0, where],
                    recv_sem=sems.at[1, 5 - where],
                    device_id={"space": lax.rem(me + OFFSETS[where] + SPAN, SPAN)},
                    device_id_type=MESH_ID,
                )
            )

    def start(self):
        for copy in self.copies:
            copy.start()

    def wait(self):
        for copy in self.copies:
            copy.wait()


class Place:
    def __init__(self):
        me = lax.axis_index("space")
        self.me = me
        self.core, self.y, self.z, self.x_lo = me % 2, me // 2 % 4, me // 8 % 8, me // 64
        self.plane = (lax.axis_index("dp") * 2 + self.x_lo) * 4 + self.y
        self.mate = {"space": me + 1 - 2 * self.core}

    def at_plane(self, index):
        return {
            "dp": index // 8,
            "space": ((index // 4 % 2) * 8 + self.z) * 8 + index % 4 * 2 + self.core,
        }

    def at_line(self, index):
        return {"space": (self.x_lo * 8 + index) * 8 + self.y * 2 + self.core}


class Sum:
    def __init__(self, place, buffers, sems):
        self.place = place
        self.half_send, self.half_in, self.plane_send, self.plane_in, self.line_in = buffers[:5]
        self.wide_in, self.pair_send, self.pair_in, self.acc = buffers[5:]
        self.sems = sems
        self.copies = []

    def copy(self, source, target, index, where):
        one = pltpu.make_async_remote_copy(
            src_ref=source,
            dst_ref=target,
            send_sem=self.sems.at[0, index],
            recv_sem=self.sems.at[1, index],
            device_id=where,
            device_id_type=MESH_ID,
        )
        one.start()
        self.copies.append(one)

    def put(self, index, value):
        half, at = index // 36, index % 36
        size = value.shape[0]
        self.half_send[half, at : at + size] = value.astype(BF16)

    def wait(self):
        for one in self.copies:
            one.wait()
        self.copies = []

    def one(self):
        place = self.place
        self.copy(self.half_send.at[1 - place.core], self.half_in, 0, place.mate)

    def two(self):
        place = self.place
        self.wait()
        self.acc[...] = self.half_send[place.core].astype(F32) + self.half_in[...].astype(F32)
        self.plane_send[...] = self.acc[...].astype(BF16)
        for step in range(1, 16):
            peer = lax.rem(place.plane + step, 16)
            source = self.plane_send.at[pl.ds(chunk_start(peer), CHUNK)]
            self.copy(source, self.plane_in.at[step - 1], step, place.at_plane(peer))

    def three(self):
        place = self.place
        self.wait()
        total = self.acc[pl.ds(chunk_start(place.plane), CHUNK)]
        for step in range(15):
            total = total + self.plane_in[step].astype(F32)
        self.line_in[place.z] = total.astype(BF16)
        for step in range(1, 8):
            peer = lax.rem(place.z + step, 8)
            self.copy(self.line_in.at[place.z], self.line_in.at[place.z], 15 + step, place.at_line(peer))

    def four(self):
        place = self.place
        self.wait()
        total = self.line_in[0].astype(F32)
        for index in range(1, 8):
            total = total + self.line_in[index].astype(F32)
        self.wide_in[place.plane] = total.astype(BF16)
        for step in range(1, 16):
            peer = lax.rem(place.plane + step, 16)
            here = self.wide_in.at[place.plane]
            self.copy(here, here, 22 + step, place.at_plane(peer))

    def five(self):
        self.wait()
        for index in range(16):
            at = chunk_start(index)
            self.pair_send[at : at + CHUNK] = self.wide_in[index]
        self.copy(self.pair_send, self.pair_in, 38, self.place.mate)

    def end(self, out, layer, scale, over):
        self.wait()
        core = self.place.core
        mine, other = self.pair_send[...].astype(F32), self.pair_in[...].astype(F32)
        out[layer, :36] = jnp.where(core == 0, mine[:36], other[:36]) * scale
        out[layer, 36:] = jnp.where(core == 0, other[:36], mine[:36]) * scale
        if over is not None:
            over[...] = mine[36]


def whole(
    scale, table, state, cotangent, kernels, turns, next_state, cell_grad, sums, over,
    state_blocks, grad_blocks, hidden_blocks, strips, corners, given_strips, given_corners,
    send_a, send_b, send_c, send_d, in_a, in_b, in_c, in_d,
    forward, flipped, grad_wide, wide, total, padded, even, odd, before, grad_even, grad_odd, grad_turned,
    *rest,
):
    sum_one, sum_two = rest[:9], rest[9:18]
    swap_sems, one_sems, two_sems = rest[18:]
    place = Place()
    me = place.me
    barrier = pltpu.get_barrier_semaphore()

    def greet(where):
        pl.semaphore_signal(barrier, inc=1, device_id=where, device_id_type=MESH_ID)

    for offset in OFFSETS:
        greet({"space": lax.rem(me + offset + SPAN, SPAN)})
    greet(place.mate)
    for step in range(1, 16):
        greet(place.at_plane(lax.rem(place.plane + step, 16)))
    for step in range(1, 8):
        greet(place.at_line(lax.rem(place.z + step, 8)))

    rims_one = Swap(me, send_a, in_a, swap_sems.at[0])
    back_two = Swap(me, send_b, in_b, swap_sems.at[1])
    rims_two = Swap(me, send_c, in_c, swap_sems.at[2])
    back_one = Swap(me, send_d, in_d, swap_sems.at[3])
    reduce_one = Sum(place, sum_one, one_sems)
    reduce_two = Sum(place, sum_two, two_sems)

    for slot in range(2):
        for row in range(8):
            moved = product(turns[0], state[slot, row])
            state_blocks[slot, row] = blocks(moved.astype(BF16))
    take_rims(state_blocks, strips, corners)
    send_rims(table, strips, corners, send_a)
    pl.semaphore_wait(barrier, 29)
    rims_one.start()

    for layer in range(2):
        for tap in range(9):
            weight = kernels[layer, tap // 3, tap % 3]
            forward[layer, tap * 128 : tap * 128 + 128] = weight
            flipped[layer, tap * 128 : tap * 128 + 128] = weight.astype(F32).T.astype(BF16)
    grad_wide[...] = jnp.zeros_like(grad_wide)
    for slot in range(2):
        present = jnp.where(table[T_PRESENT + slot] > 0, 1.0, 0.0)
        for row in range(8):
            moved = blocks((product(turns[0], cotangent[slot, row]) * present).astype(BF16))
            grad_blocks[slot, row] = moved
            grad_wide[slot, 2 + row, 2:10] = moved
    for slot in range(2):

        def rows_back(step, carry):
            taps = [
                cells(grad_wide[slot, pl.ds(step * 2 + 2 - up, 2), 2 - across : 12 - across])
                for up in range(3)
                for across in range(3)
            ]
            result = product(jnp.concatenate(taps, axis=1), flipped[1])
            wide[slot, pl.ds(step * 2, 2)] = result.reshape(2, 10, 16, 128)
            return carry

        lax.fori_loop(0, 5, rows_back, 0)
        total[slot] = wide[slot, 1:9, 1:9]
    give_back(table, wide, turns, send_b, given_strips, given_corners)
    back_two.start()

    rims_one.wait()
    widen(table, state_blocks, strips, corners, in_a, turns, padded)
    for row in range(10):
        both = [halves(padded[slot, row : row + 1])[0] for slot in range(2)]
        even[row] = jnp.concatenate(both, axis=1).astype(BF16)
    for row in range(9):
        both = [
            shifted_up(halves(padded[slot, row : row + 1])[0], halves(padded[slot, row + 1 : row + 2])[0])
            for slot in range(2)
        ]
        odd[row] = jnp.concatenate(both, axis=1).astype(BF16)

    def window(row, up, across, count):
        source, at = ((odd, row), (even, row + 1), (odd, row + 1))[up]
        return cells(source[pl.ds(at, count), 1 + across : 17 + across])

    def first(row, carry):
        taps = [window(row, up, across, 1) for up in range(3) for across in range(3)]
        result = product(jnp.concatenate(taps, axis=1), forward[0]).reshape(16, 16, 128)
        before[row] = result
        hidden = gelu_parts(result)[0]
        for slot in range(2):
            part = hidden[:, slot * 8 : slot * 8 + 8].reshape(8, 16, 128)
            hidden_blocks[slot, row] = part.astype(BF16)
        return carry

    lax.fori_loop(0, 8, first, 0)
    take_rims(hidden_blocks, strips, corners)
    send_rims(table, strips, corners, send_c)
    rims_two.start()

    back_two.wait()
    take_back(table, in_b, given_strips, given_corners, total)
    grad_even[...] = jnp.zeros_like(grad_even)
    grad_odd[...] = jnp.zeros_like(grad_odd)

    def pointwise(row, carry):
        both = [total[slot, row].astype(BF16).astype(F32).reshape(16, 8, 128) for slot in range(2)]
        grad = jnp.concatenate(both, axis=1) * gelu_parts(before[row])[1]
        grad = grad.astype(BF16)
        grad_even[row + 1, 2:18] = grad
        at = pl.multiple_of(row * 256, 256)
        grad_turned[:, pl.ds(at, 256)] = cells(grad).astype(F32).T.astype(BF16)
        return carry

    lax.fori_loop(0, 8, pointwise, 0)
    for row in range(9):
        low = grad_even[row, 2:18].astype(F32)
        high = grad_even[row + 1, 2:18].astype(F32)
        both = [
            shifted_up(low[:, slot * 8 : slot * 8 + 8], high[:, slot * 8 : slot * 8 + 8])
            for slot in range(2)
        ]
        grad_odd[row + 1, 2:18] = jnp.concatenate(both, axis=1).astype(BF16)

    def returned(row, carry):
        taps = []
        for up in range(3):
            source, at = ((grad_odd, row + 1), (grad_even, row), (grad_odd, row))[up]
            for across in range(3):
                taps.append(cells(source[at, 2 - across : 20 - across]))
        result = product(jnp.concatenate(taps, axis=1), flipped[0]).reshape(18, 16, 128)
        blank = jnp.zeros((1, 8, 128), F32)
        for slot in range(2):
            part = jnp.concatenate([blank, result[:, slot * 8 : slot * 8 + 8], blank], axis=0)
            wide[slot, row] = part.reshape(10, 16, 128)
        return carry

    lax.fori_loop(0, 10, returned, 0)
    give_back(table, wide, turns, send_d, given_strips, given_corners)
    back_one.start()
    for slot in range(2):
        total[slot] = wide[slot, 1:9, 1:9]

    for up in range(3):
        for across in range(3):
            term = product(grad_turned[...], window(0, up, across, 8))
            reduce_one.put((up * 3 + across) * 8, term.T.reshape(8, 16, 128)[:4])
            reduce_one.put((up * 3 + across) * 8 + 4, term.T.reshape(8, 16, 128)[4:])
    blank = jnp.zeros((1, 16, 128), F32)
    broken = blank + table[T_OVER].astype(F32)
    for half in range(2):
        reduce_one.half_send[half, 36:37] = blank.astype(BF16)
        reduce_two.half_send[half, 36:37] = broken.astype(BF16)
    reduce_one.one()

    rims_two.wait()
    widen(table, hidden_blocks, strips, corners, in_c, turns, padded)
    for slot in range(2):
        for step in range(4):
            grad = cells(grad_blocks[slot, step * 2 : step * 2 + 2])
            at = slot * 1024 + step * 256
            grad_turned[:, at : at + 256] = grad.astype(F32).T.astype(BF16)
    reduce_one.two()
    for up in range(3):
        for across in range(3):
            term = sum(
                product(
                    grad_turned[:, slot * 1024 : slot * 1024 + 1024],
                    cells(padded[slot, up : up + 8, across : across + 8]),
                )
                for slot in range(2)
            )
            reduce_two.put((up * 3 + across) * 8, term.T.reshape(8, 16, 128)[:4])
            reduce_two.put((up * 3 + across) * 8 + 4, term.T.reshape(8, 16, 128)[4:])
    reduce_two.one()
    reduce_one.three()

    def finish(slot):
        present = jnp.where(table[T_PRESENT + slot] > 0, 1.0, 0.0)

        def rows(step, carry):
            taps = [
                cells(padded[slot, pl.ds(step * 2 + up, 2), across : across + 8])
                for up in range(3)
                for across in range(3)
            ]
            result = product(jnp.concatenate(taps, axis=1), forward[1])
            fresh = cells(state_blocks[slot, pl.ds(step * 2, 2)]).astype(F32) + result
            fresh = (fresh * present).astype(BF16)
            for half in range(2):
                part = slice(half * 128, half * 128 + 128)
                next_state[slot, step * 2 + half] = product(turns[1], fresh[part]).astype(BF16)
            return carry

        lax.fori_loop(0, 4, rows, 0)

    def close(slot):
        present = jnp.where(table[T_PRESENT + slot] > 0, 1.0, 0.0)

        def rows(step, carry):
            grad = cells(grad_blocks[slot, step])
            summed = (grad.astype(F32) + cells(total[slot, step])) * present
            cell_grad[slot, step] = product(turns[1], summed.astype(BF16)).astype(BF16)
            return carry

        lax.fori_loop(0, 8, rows, 0)

    reduce_two.two()
    reduce_one.four()
    finish(0)
    reduce_two.three()
    finish(1)
    reduce_one.five()
    reduce_two.four()
    back_one.wait()
    take_back(table, in_d, given_strips, given_corners, total)
    close(0)
    close(1)
    reduce_two.five()
    reduce_one.end(sums, 0, scale, None)
    reduce_two.end(sums, 1, scale, over)


def vmem(shape, kind):
    return pltpu.VMEM(shape, kind)


def specs(kinds):
    return [pl.BlockSpec(memory_space=pltpu.SMEM if kind == "s" else pltpu.VMEM) for kind in kinds]


def shape(dims, kind):
    return jax.ShapeDtypeStruct(dims, kind)


TILES = (2, 8, 8, 16, 128)
STRIPS = (8, 8, 16, 128)
CORNERS = (8, 16, 128)
SENT = (6, PART, 16, 128)
NATURAL = (2, 8, 128, 128)


def sum_buffers():
    return [
        vmem((2, HALF, 16, 128), BF16), vmem((HALF, 16, 128), BF16), vmem((HALF, 16, 128), BF16),
        vmem((15, CHUNK, 16, 128), BF16), vmem((8, CHUNK, 16, 128), BF16), vmem((16, CHUNK, 16, 128), BF16),
        vmem((HALF, 16, 128), BF16), vmem((HALF, 16, 128), BF16), vmem((HALF, 16, 128), F32),
    ]


def routed(cell_state, cotangent, kernels, slot_of_tile, neighbours, rotations, corner_flags):
    table = pl.pallas_call(
        plan_kernel,
        out_shape=shape((T_SIZE,), jnp.int32),
        in_specs=specs("ssss"),
        out_specs=specs("s")[0],
        scratch_shapes=[pltpu.SMEM((2 * SPAN,), jnp.int32)],
    )(slot_of_tile, neighbours, rotations, corner_flags)
    scale = 1.0 / math.sqrt(
        cell_state.shape[0] * lax.axis_size("dp") * slot_of_tile.shape[0] * cell_state.shape[2] ** 2
    )
    next_state, cell_grad, sums, over = pl.pallas_call(
        functools.partial(whole, scale),
        out_shape=[
            shape(NATURAL, BF16), shape(NATURAL, BF16), shape((2, UNITS, 16, 128), F32), shape((16, 128), F32)
        ],
        in_specs=specs("svvvv"),
        out_specs=specs("vvvv"),
        scratch_shapes=[
            vmem(TILES, BF16), vmem(TILES, BF16), vmem(TILES, BF16),
            vmem(STRIPS, BF16), vmem(CORNERS, BF16), vmem(STRIPS, BF16), vmem(CORNERS, BF16),
        ]
        + [vmem(SENT, BF16)] * 8
        + [
            vmem((2, 1152, 128), BF16), vmem((2, 1152, 128), BF16),
            vmem((2, 12, 12, 16, 128), BF16), vmem((2, 10, 10, 16, 128), F32), vmem(TILES, F32),
            vmem((2, 10, 10, 16, 128), BF16), vmem((10, 20, 16, 128), BF16), vmem((9, 20, 16, 128), BF16),
            vmem((8, 16, 16, 128), F32), vmem((10, 20, 16, 128), BF16), vmem((11, 20, 16, 128), BF16),
            vmem((128, 2048), BF16),
        ]
        + sum_buffers()
        + sum_buffers()
        + [
            pltpu.SemaphoreType.DMA((4, 2, 6)),
            pltpu.SemaphoreType.DMA((2, 39)),
            pltpu.SemaphoreType.DMA((2, 39)),
        ],
        compiler_params=pltpu.CompilerParams(
            vmem_limit_bytes=VMEM_BYTES, collective_id=1, has_side_effects=True
        ),
    )(
        table, cell_state.reshape(NATURAL), cotangent.reshape(NATURAL), kernels,
        jnp.asarray(permutations(), BF16),
    )
    done = (next_state.reshape(cell_state.shape), cell_grad.reshape(cell_state.shape), sums.reshape(kernels.shape))
    arrays = (cell_state, cotangent, kernels, slot_of_tile, neighbours, rotations, corner_flags)
    return lax.cond(over[0, 0] == 0, lambda *_: done, shards, *arrays)


def solution(mesh):
    in_specs = (
        P("dp", "space", None, None, None),
        P("dp", "space", None, None, None),
        P(),
        P(),
        P(),
        P(),
        P(),
    )
    out_specs = (P("dp", "space", None, None, None), P("dp", "space", None, None, None), P())
    return jax.shard_map(routed, mesh=mesh, in_specs=in_specs, out_specs=out_specs, check_vma=False)
```

```python
import functools
import math

import jax
import jax.numpy as jnp
import numpy as np
from jax import lax
from jax.experimental import pallas as pl
from jax.experimental.pallas import tpu as pltpu
from jax.sharding import PartitionSpec as P

RES_BLOCKS = 1
DILATION_ONE = 2
DILATION_TWO = 4
REACH_DEV = 3


CONV_AXES = ("NHWC", "HWIO", "NHWC")


def as_sent(shard):

    def short(part):
        return part.astype(jnp.bfloat16) if part.dtype == jnp.float32 else part

    return jax.tree.map(short, shard)


def shifted(value, axis, steps):
    count = lax.axis_size(axis)
    pairs = [(source, (source + steps) % count) for source in range(count)]
    return lax.ppermute(value, axis, pairs)


def boundary(tile_data, rim_depth):
    extent = tile_data.shape[3]
    far = extent - rim_depth
    sides = [
        tile_data[:, :, :rim_depth],
        tile_data[:, :, :, far:],
        tile_data[:, :, far:],
        tile_data[:, :, :, :rim_depth],
    ]
    blocks = [
        tile_data[:, :, :rim_depth, far:],
        tile_data[:, :, far:, far:],
        tile_data[:, :, far:, :rim_depth],
        tile_data[:, :, :rim_depth, :rim_depth],
    ]
    strips = jnp.stack(
        [jnp.rot90(sides[quarter], quarter, axes=(2, 3)) for quarter in range(4)], axis=2
    )
    corners = jnp.stack(
        [jnp.rot90(blocks[quarter], quarter, axes=(2, 3))[:, :, :, ::-1] for quarter in range(4)],
        axis=2,
    )
    return (strips, corners)


def assemble(tile_data, strips, corners):
    edge_parts = [
        jnp.rot90(strips[:, :, quarter, ::-1, ::-1], -quarter, axes=(2, 3)) for quarter in range(4)
    ]
    corner_parts = [
        jnp.rot90(corners[:, :, quarter, ::-1], -quarter, axes=(2, 3)) for quarter in range(4)
    ]
    top_row = jnp.concatenate([corner_parts[3], edge_parts[0], corner_parts[0]], axis=3)
    middle = jnp.concatenate([edge_parts[3], tile_data, edge_parts[1]], axis=3)
    bottom = jnp.concatenate([corner_parts[2], edge_parts[2], corner_parts[1]], axis=3)
    return jnp.concatenate([top_row, middle, bottom], axis=2)


def rim_pieces(tile_data, rim_depth):
    strips, corners = boundary(tile_data, rim_depth)
    joined = jnp.concatenate([strips, corners], axis=4)
    return joined.reshape((joined.shape[0], joined.shape[1] * 4) + joined.shape[3:])


def conv_apply(padded, kernel, spread):
    merged = padded.reshape((-1,) + padded.shape[2:])
    result = lax.conv_general_dilated(
        merged,
        kernel,
        (1, 1),
        "VALID",
        rhs_dilation=(spread, spread),
        dimension_numbers=CONV_AXES,
        preferred_element_type=jnp.float32,
    )
    return result.reshape(padded.shape[:2] + result.shape[1:])


def conv_back(grad_out, kernel, spread):
    merged = grad_out.reshape((-1,) + grad_out.shape[2:])
    flipped = jnp.swapaxes(kernel[::-1, ::-1], 2, 3)
    margin = 2 * spread
    result = lax.conv_general_dilated(
        merged,
        flipped,
        (1, 1),
        ((margin, margin), (margin, margin)),
        rhs_dilation=(spread, spread),
        dimension_numbers=CONV_AXES,
        preferred_element_type=jnp.float32,
    )
    return result.reshape(grad_out.shape[:2] + result.shape[1:])


def kernel_grad(padded, grad_out, spread):
    extent = grad_out.shape[2]
    tap_terms = []
    for row_tap in range(3):
        for col_tap in range(3):
            window = padded[
                :,
                :,
                row_tap * spread : row_tap * spread + extent,
                col_tap * spread : col_tap * spread + extent,
            ]
            tap_terms.append(
                lax.dot_general(
                    window,
                    grad_out,
                    (((0, 1, 2, 3), (0, 1, 2, 3)), ((), ())),
                    preferred_element_type=jnp.float32,
                )
            )
    stacked = jnp.stack(tap_terms)
    return stacked.reshape((3, 3) + stacked.shape[1:])


def halo_plan(slot_of_tile, neighbours, rotations, corner_flags, slot_count):
    span_count = lax.axis_size("space")
    myself = lax.axis_index("space")
    tile_count = slot_of_tile.shape[0]
    owned = myself * slot_count + jnp.arange(slot_count, dtype=jnp.int32)
    matches = slot_of_tile[None, :] == owned[:, None]
    present = jnp.any(matches, axis=1)
    tile_here = jnp.sum(
        jnp.where(matches, jnp.arange(tile_count, dtype=jnp.int32)[None, :], 0), axis=1
    )
    nearby = jnp.take(neighbours, tile_here, axis=0)
    turn_code = jnp.take(rotations, tile_here, axis=0)
    facing = (jnp.arange(8, dtype=jnp.int32)[None, :] % 4 + 2 + turn_code) % 4
    source = jnp.take(slot_of_tile, nearby)
    holder = source // slot_count
    within = source % slot_count
    offset = jnp.clip(
        (myself - holder + span_count + REACH_DEV) % span_count - REACH_DEV, -REACH_DEV, REACH_DEV
    )
    select = ((offset + REACH_DEV) * slot_count + within) * 4 + facing
    keep_corner = jnp.take(corner_flags, tile_here, axis=0) == 0
    return (select[:, :4].reshape(-1), select[:, 4:].reshape(-1), keep_corner.reshape(-1), present)


def fetch_near(bundle):
    arrived = {0: bundle}
    for offset in list(range(-REACH_DEV, 0)) + list(range(1, REACH_DEV + 1)):
        arrived[offset] = shifted(as_sent(bundle), "space", offset).astype(bundle.dtype)
    return [arrived[offset] for offset in range(-REACH_DEV, REACH_DEV + 1)]


def return_near(parts):
    total = parts[0]
    for offset in list(range(-REACH_DEV, 0)) + list(range(1, REACH_DEV + 1)):
        total = total + shifted(parts[offset].astype(jnp.bfloat16), "space", -offset).astype(
            jnp.float32
        )
    return total


def halo_forward(tile_data, rim_depth, plan):
    pick_edge, pick_corner, keep_corner = plan[:3]
    samples_here, slot_count, extent = (tile_data.shape[0], tile_data.shape[1], tile_data.shape[2])
    channels = tile_data.shape[4]
    gathered = jnp.concatenate(fetch_near(rim_pieces(tile_data, rim_depth)), axis=1)
    edge_part = jnp.take(gathered, pick_edge, axis=1)[:, :, :, :extent]
    corner_part = jnp.take(gathered, pick_corner, axis=1)[:, :, :, extent:]
    corner_part = jnp.where(
        keep_corner[None, :, None, None, None], corner_part, jnp.zeros((), corner_part.dtype)
    )
    strips = edge_part.reshape(samples_here, slot_count, 4, rim_depth, extent, channels)
    corners = corner_part.reshape(samples_here, slot_count, 4, rim_depth, rim_depth, channels)
    return assemble(tile_data, strips, corners)


def halo_backward(grad_wide, rim_depth, plan):
    pick_edge, pick_corner, keep_corner = plan[:3]
    samples_here, slot_count = (grad_wide.shape[0], grad_wide.shape[1])
    extent = grad_wide.shape[2] - 2 * rim_depth
    channels = grad_wide.shape[4]
    tile_zero = jnp.zeros((samples_here, slot_count, extent, extent, channels), jnp.float32)
    strip_zero = jnp.zeros((samples_here, slot_count, 4, rim_depth, extent, channels), jnp.float32)
    corner_zero = jnp.zeros(
        (samples_here, slot_count, 4, rim_depth, rim_depth, channels), jnp.float32
    )
    _, assemble_back = jax.vjp(assemble, tile_zero, strip_zero, corner_zero)
    grad_tiles, grad_strips, grad_corners = assemble_back(grad_wide)
    pieces = slot_count * 4
    grad_corners = grad_corners.reshape(samples_here, pieces, rim_depth, rim_depth, channels)
    grad_corners = jnp.where(keep_corner[None, :, None, None, None], grad_corners, 0.0)
    spread_out = jnp.zeros(
        (samples_here, (2 * REACH_DEV + 1) * pieces, rim_depth, extent + rim_depth, channels),
        jnp.float32,
    )
    spread_out = spread_out.at[:, pick_edge, :, :extent].add(
        grad_strips.reshape(samples_here, pieces, rim_depth, extent, channels)
    )
    spread_out = spread_out.at[:, pick_corner, :, extent:].add(grad_corners)
    parts = {
        offset: spread_out[:, (offset + REACH_DEV) * pieces : (offset + REACH_DEV + 1) * pieces]
        for offset in range(-REACH_DEV, REACH_DEV + 1)
    }
    returned = return_near(parts)
    _, rim_back = jax.vjp(lambda tile_part: rim_pieces(tile_part, rim_depth), tile_zero)
    return grad_tiles + rim_back(returned)[0]


def sum_over(value, axis):
    count = lax.axis_size(axis)
    step = 1
    while step < count:
        pairs = [(source, source ^ step) for source in range(count)]
        value = value + lax.ppermute(value, axis, pairs)
        step *= 2
    return value


def shards(cell_state, cotangent, kernels, slot_of_tile, neighbours, rotations, corner_flags):
    plan = halo_plan(slot_of_tile, neighbours, rotations, corner_flags, cell_state.shape[1])
    keep_slot = plan[3][None, :, None, None, None]
    current = cell_state
    block_at = 0
    widened = halo_forward(current, DILATION_ONE, plan)
    before = conv_apply(widened, kernels[2 * block_at], DILATION_ONE)
    hidden = jax.nn.gelu(before).astype(jnp.bfloat16)
    widened_two = halo_forward(hidden, DILATION_TWO, plan)
    branch = conv_apply(widened_two, kernels[2 * block_at + 1], DILATION_TWO)
    stored = [(widened, before, widened_two)]
    current = (current.astype(jnp.float32) + branch).astype(jnp.bfloat16)
    next_state = jnp.where(keep_slot, current, jnp.zeros((), jnp.bfloat16))
    gradient = jnp.where(keep_slot, cotangent, jnp.zeros((), jnp.bfloat16))
    kernel_terms = [None] * (2 * RES_BLOCKS)
    extent = cell_state.shape[2]
    norm_scale = 1.0 / math.sqrt(
        cell_state.shape[0] * lax.axis_size("dp") * slot_of_tile.shape[0] * extent * extent
    )
    for block_at in reversed(range(RES_BLOCKS)):
        widened, before, widened_two = stored[block_at]
        outer_term = kernel_grad(widened_two, gradient, DILATION_TWO)
        kernel_terms[2 * block_at + 1] = outer_term
        grad_hidden = halo_backward(
            conv_back(gradient, kernels[2 * block_at + 1], DILATION_TWO), DILATION_TWO, plan
        ).astype(jnp.bfloat16)
        _, gelu_back = jax.vjp(jax.nn.gelu, before)
        grad_before = gelu_back(grad_hidden.astype(jnp.float32))[0].astype(jnp.bfloat16)
        inner_term = kernel_grad(widened, grad_before, DILATION_ONE)
        kernel_terms[2 * block_at] = inner_term
        returned = halo_backward(
            conv_back(grad_before, kernels[2 * block_at], DILATION_ONE), DILATION_ONE, plan
        )
        gradient = (gradient.astype(jnp.float32) + returned).astype(jnp.bfloat16)
    stacked = jnp.stack(kernel_terms)
    stacked = sum_over(sum_over(stacked, "space"), "dp")
    return (next_state, gradient, stacked * norm_scale)


MESH_ID = pl.DeviceIdType.MESH
SPAN = 128
STRIP_CAP = (1, 2, 2, 2, 2, 1)
CORNER_CAP = 4
PART = 20
OFFSETS = (-3, -2, -1, 1, 2, 3)
ORDER = (2, 3, 1, 4, 0, 5)
SELF = 6
NOT_STRIP, NOT_CORNER = 20, 32
T_STRIP_LIST, T_CORNER_LIST, T_GIVE_STRIP, T_GIVE_CORNER = 0, 12, 36, 48
T_ADD_STRIP, T_ADD_CORNER, T_PIECES, T_PRESENT = 72, 88, 104, 200
T_OVER, T_SPARE, T_COUNT, T_SIZE = 202, 203, 208, 224
VMEM_BYTES = 56 * 1024 * 1024
F32 = jnp.float32
BF16 = jnp.bfloat16


def cell_order():
    rows, cols = np.meshgrid(np.arange(4), np.arange(4), indexing="ij")
    return ((cols // 2) * 8 + (rows // 2) * 4 + (rows % 2) * 2 + cols % 2).astype(np.int64)


def permutations():
    order = cell_order()
    to_blocks = np.zeros((128, 128), np.float32)
    for row in range(4):
        for col in range(32):
            to_blocks[(col // 4) * 16 + order[row, col % 4], row * 32 + col] = 1
    mats = [to_blocks, to_blocks.T]
    for turn in range(4):
        turned = np.rot90(order, turn)
        small = np.zeros((16, 16), np.float32)
        small[order.reshape(-1), turned.reshape(-1)] = 1
        for flip in range(2):
            line = np.eye(8)[::-1] if flip else np.eye(8)
            mats.append(np.kron(line, small))
    return np.stack(mats)


def turn_matrix(turn, flip):
    return 2 + 2 * turn + flip


def flips(edge, turn):
    side = (edge + 2 + turn) & 1
    once = jnp.where((turn == 1) & (side == 0), 1, 0)
    thrice = jnp.where((turn == 3) & (side == 1), 1, 0)
    return jnp.where(turn == 2, 1, once + thrice)


def plan_kernel(slot_ref, near_ref, turn_ref, flag_ref, table, tile_at):
    me = lax.axis_index("space")
    for entry in range(T_SIZE):
        table[entry] = 0
    for entry in range(16):
        table[T_ADD_STRIP + entry] = NOT_STRIP
        table[T_ADD_CORNER + entry] = NOT_CORNER
    for rel in range(14):
        tile_at[(me + rel // 2 - 3 + SPAN) % SPAN * 2 + rel % 2] = -1

    def place(step, carry):
        for inner in range(16):
            tile = step * 16 + inner
            tile_at[slot_ref[tile]] = tile
        return carry

    lax.fori_loop(0, slot_ref.shape[0] // 16, place, 0)
    over = jnp.int32(0)

    def contribute(hit, kind, entry, code):
        counter = T_COUNT + kind * 8 + entry
        count = table[counter]
        table[jnp.where(hit, counter, T_SPARE)] = count + 1
        place_at = (T_ADD_CORNER if kind else T_ADD_STRIP) + entry * 2 + jnp.minimum(count, 1)
        table[jnp.where(hit, place_at, T_SPARE)] = code
        return jnp.where(hit & (count > 1), 1, 0)

    for where, offset in enumerate(OFFSETS):
        seen = [jnp.int32(0), jnp.int32(0)]
        for slot in range(2):
            tile = tile_at[(me + offset + SPAN) % SPAN * 2 + slot]
            row = jnp.maximum(tile, 0)
            for piece in range(8):
                kind = piece // 4
                source = slot_ref[near_ref[piece, row]]
                hit = (tile >= 0) & (source // 2 == me)
                entry = source % 2 * 4 + ((piece + 2 + turn_ref[piece, row]) & 3)
                cap = CORNER_CAP if kind else STRIP_CAP[where]
                rank = jnp.minimum(seen[kind], cap - 1)
                over = over + jnp.where(hit & (seen[kind] >= cap), 1, 0)
                seen[kind] = seen[kind] + jnp.where(hit, 1, 0)
                width = 4 if kind else 2
                place_at = (T_CORNER_LIST if kind else T_STRIP_LIST) + where * width + rank
                table[jnp.where(hit, place_at, T_SPARE)] = entry
                over = over + contribute(hit, kind, entry, where * width + rank)
    seen = [[jnp.int32(0)] * 7, [jnp.int32(0)] * 7]
    for slot in range(2):
        tile = tile_at[me * 2 + slot]
        row = jnp.maximum(tile, 0)
        valid = jnp.where(tile >= 0, 1, 0)
        table[T_PRESENT + slot] = valid
        for piece in range(8):
            kind = piece // 4
            source = slot_ref[near_ref[piece, row]]
            turn = turn_ref[piece, row] & 3
            offset = jnp.clip((source // 2 - me + 3 + SPAN) % SPAN, 0, 6)
            where = jnp.where(offset == 3, SELF, jnp.where(offset < 3, offset, offset - 1))
            rank = jnp.int32(0)
            for choice in range(7):
                match = jnp.where(offset == choice, valid, 0)
                rank = rank + match * seen[kind][choice]
                seen[kind][choice] = seen[kind][choice] + match
            rank = jnp.minimum(rank, 3 if kind else 1)
            keep = valid
            if kind:
                keep = valid * jnp.where(flag_ref[piece - 4, row] == 0, 1, 0)
            entry = source % 2 * 4 + ((piece + 2 + turn) & 3)
            base = T_PIECES + (slot * 8 + piece) * 6
            table[base] = valid
            table[base + 1] = where
            table[base + 2] = rank
            table[base + 3] = turn
            table[base + 4] = entry
            table[base + 5] = keep
            mine = slot * 4 + piece % 4
            own = (valid > 0) & (where == SELF)
            away = (valid > 0) & (where != SELF)
            place_at = (T_GIVE_CORNER if kind else T_GIVE_STRIP) + where * (4 if kind else 2) + rank
            table[jnp.where(away, place_at, T_SPARE)] = mine
            over = over + contribute(own, kind, entry, (24 if kind else 12) + mine)
    table[T_OVER] = over


def piece_of(table, slot, piece):
    base = T_PIECES + (slot * 8 + piece) * 6
    return [table[base + field] for field in range(6)]


def blocks(value):
    return value.reshape((-1, 16, 128))


def cells(value):
    return value.reshape((-1, 128))


def product(left, right):
    return jnp.dot(left, right, preferred_element_type=F32)


EDGE_OF = ((0, slice(None)), (slice(None), 7), (7, slice(None)), (slice(None), 0))
CORNER_OF = ((0, 7), (7, 7), (7, 0), (0, 0))
BAND_OF = ((0, slice(1, 9)), (slice(1, 9), 9), (9, slice(1, 9)), (slice(1, 9), 0))
BLOCK_OF = ((0, 9), (9, 9), (9, 0), (0, 0))


def take_rims(tile_ref, strips, corners):
    for slot in range(2):
        for side in range(4):
            strips[slot * 4 + side] = blocks(tile_ref[(slot,) + EDGE_OF[side]])
            corners[slot * 4 + side] = tile_ref[(slot,) + CORNER_OF[side]]


def send_rims(table, strips, corners, send, strip_list=T_STRIP_LIST, corner_list=T_CORNER_LIST):
    for where in range(6):
        for rank in range(STRIP_CAP[where]):
            send[where, 4 + rank * 8 : 12 + rank * 8] = strips[table[strip_list + where * 2 + rank]]
        for rank in range(CORNER_CAP):
            send[where, rank] = corners[table[corner_list + where * 4 + rank]]


def corner_turns(table, turns, back):
    parts = []
    for slot in range(2):
        for side in range(4):
            fields = piece_of(table, slot, 4 + side)
            turn = (4 - fields[3]) & 3 if back else fields[3]
            rows = turns[turn_matrix(turn, 0)]
            at = (slot * 4 + side) * 16
            parts.append(rows[at : at + 16] * jnp.where(fields[5] > 0, 1.0, 0.0).astype(BF16))
    return jnp.concatenate(parts, axis=0)


def widen(table, tile_ref, strips, corners, arrived, turns, padded):
    for slot in range(2):
        padded[slot, 1:9, 1:9] = tile_ref[slot]
        for edge in range(4):
            valid, where, rank, turn, entry, keep = piece_of(table, slot, edge)
            own = strips[entry]
            other = arrived[jnp.minimum(where, 5), pl.ds(4 + rank * 8, 8)]
            strip = jnp.where(where == SELF, own, other)
            strip = jnp.where(valid > 0, strip, jnp.zeros_like(strip))
            turned = product(turns[turn_matrix(turn, flips(edge, turn))], cells(strip))
            padded[(slot,) + BAND_OF[edge]] = blocks(turned.astype(BF16))
    stack = []
    for slot in range(2):
        for side in range(4):
            valid, where, rank, turn, entry, keep = piece_of(table, slot, 4 + side)
            block = jnp.where(where == SELF, corners[entry], arrived[jnp.minimum(where, 5), rank])
            stack.append(jnp.where(valid > 0, block, jnp.zeros_like(block)))
    turned = product(corner_turns(table, turns, False), jnp.concatenate(stack, axis=0))
    turned = blocks(turned.astype(BF16))
    for slot in range(2):
        for side in range(4):
            padded[(slot,) + BLOCK_OF[side]] = turned[slot * 4 + side]


def give_back(table, wide, turns, send, strips, corners):
    for slot in range(2):
        for edge in range(4):
            valid, where, rank, turn, entry, keep = piece_of(table, slot, edge)
            band = cells(blocks(wide[(slot,) + BAND_OF[edge]])).astype(BF16)
            turned = product(turns[turn_matrix((4 - turn) & 3, flips(edge, turn))], band)
            strips[slot * 4 + edge] = blocks(turned.astype(BF16))
    stack = [wide[(slot,) + BLOCK_OF[side]].astype(BF16) for slot in range(2) for side in range(4)]
    turned = product(corner_turns(table, turns, True), jnp.concatenate(stack, axis=0))
    corners[...] = blocks(turned.astype(BF16))
    send_rims(table, strips, corners, send, T_GIVE_STRIP, T_GIVE_CORNER)


def take_back(table, arrived, strips, corners, total):
    for slot in range(2):
        for side in range(4):
            at = (slot,) + EDGE_OF[side]
            value = total[at]
            for extra in range(2):
                code = table[T_ADD_STRIP + (slot * 4 + side) * 2 + extra]
                far = jnp.minimum(code, 11)
                near = jnp.clip(code - 12, 0, 7)
                part = jnp.where(code < 12, arrived[far // 2, pl.ds(4 + far % 2 * 8, 8)], strips[near])
                part = jnp.where(code == NOT_STRIP, jnp.zeros_like(part), part)
                value = value + part.astype(F32)
            total[at] = value
    for slot in range(2):
        for side in range(4):
            at = (slot,) + CORNER_OF[side]
            value = total[at]
            for extra in range(2):
                code = table[T_ADD_CORNER + (slot * 4 + side) * 2 + extra]
                far = jnp.minimum(code, 23)
                near = jnp.clip(code - 24, 0, 7)
                part = jnp.where(code < 24, arrived[far // 4, far % 4], corners[near])
                part = jnp.where(code == NOT_CORNER, jnp.zeros_like(part), part)
                value = value + part.astype(F32)
            total[at] = value


def halves(value):
    return value.astype(F32).reshape(value.shape[0], value.shape[1] * 2, 8, 128)


def shifted_up(upper, lower):
    low = lax.broadcasted_iota(jnp.int32, upper.shape, upper.ndim - 2) < 4
    mixed = jnp.where(low, lower, upper)
    return jnp.concatenate([mixed[..., 4:, :], mixed[..., :4, :]], axis=mixed.ndim - 2)


def gelu_parts(value):
    root = math.sqrt(2.0 / math.pi)
    square = value * value
    bent = jnp.tanh(root * (value + 0.044715 * (value * square)))
    half = 0.5 * (1.0 + bent)
    slope = half + 0.5 * value * (1.0 - bent * bent) * (root * (1.0 + 3 * 0.044715 * square))
    return (value * half, slope)


UNITS = 72
HALF = 37
CHUNK = 3


def chunk_start(index):
    return (index * (HALF - CHUNK)) // 15


class Swap:
    def __init__(self, me, send, arrived, sems):
        self.copies = []
        for where in ORDER:
            size = 4 + 8 * STRIP_CAP[where]
            self.copies.append(
                pltpu.make_async_remote_copy(
                    src_ref=send.at[where, pl.ds(0, size)],
                    dst_ref=arrived.at[5 - where, pl.ds(0, size)],
                    send_sem=sems.at[0, where],
                    recv_sem=sems.at[1, 5 - where],
                    device_id={"space": lax.rem(me + OFFSETS[where] + SPAN, SPAN)},
                    device_id_type=MESH_ID,
                )
            )

    def start(self):
        for copy in self.copies:
            copy.start()

    def wait(self):
        for copy in self.copies:
            copy.wait()


class Place:
    def __init__(self):
        me = lax.axis_index("space")
        self.me = me
        self.core, self.y, self.z, self.x_lo = me % 2, me // 2 % 4, me // 8 % 8, me // 64
        self.plane = (lax.axis_index("dp") * 2 + self.x_lo) * 4 + self.y
        self.mate = {"space": me + 1 - 2 * self.core}

    def at_plane(self, index):
        return {
            "dp": index // 8,
            "space": ((index // 4 % 2) * 8 + self.z) * 8 + index % 4 * 2 + self.core,
        }

    def at_line(self, index):
        return {"space": (self.x_lo * 8 + index) * 8 + self.y * 2 + self.core}


class Sum:
    def __init__(self, place, buffers, sems):
        self.place = place
        self.half_send, self.half_in, self.plane_send, self.plane_in, self.line_in = buffers[:5]
        self.wide_in, self.pair_send, self.pair_in, self.acc = buffers[5:]
        self.sems = sems
        self.copies = []

    def copy(self, source, target, index, where):
        one = pltpu.make_async_remote_copy(
            src_ref=source,
            dst_ref=target,
            send_sem=self.sems.at[0, index],
            recv_sem=self.sems.at[1, index],
            device_id=where,
            device_id_type=MESH_ID,
        )
        one.start()
        self.copies.append(one)

    def put(self, index, value):
        half, at = index // 36, index % 36
        size = value.shape[0]
        self.half_send[half, at : at + size] = value.astype(BF16)

    def wait(self):
        for one in self.copies:
            one.wait()
        self.copies = []

    def one(self):
        place = self.place
        self.copy(self.half_send.at[1 - place.core], self.half_in, 0, place.mate)

    def two(self):
        place = self.place
        self.wait()
        self.acc[...] = self.half_send[place.core].astype(F32) + self.half_in[...].astype(F32)
        self.plane_send[...] = self.acc[...].astype(BF16)
        for step in range(1, 16):
            peer = lax.rem(place.plane + step, 16)
            source = self.plane_send.at[pl.ds(chunk_start(peer), CHUNK)]
            self.copy(source, self.plane_in.at[step - 1], step, place.at_plane(peer))

    def three(self):
        place = self.place
        self.wait()
        total = self.acc[pl.ds(chunk_start(place.plane), CHUNK)]
        for step in range(15):
            total = total + self.plane_in[step].astype(F32)
        self.line_in[place.z] = total.astype(BF16)
        for step in range(1, 8):
            peer = lax.rem(place.z + step, 8)
            self.copy(self.line_in.at[place.z], self.line_in.at[place.z], 15 + step, place.at_line(peer))

    def four(self):
        place = self.place
        self.wait()
        total = self.line_in[0].astype(F32)
        for index in range(1, 8):
            total = total + self.line_in[index].astype(F32)
        self.wide_in[place.plane] = total.astype(BF16)
        for step in range(1, 16):
            peer = lax.rem(place.plane + step, 16)
            here = self.wide_in.at[place.plane]
            self.copy(here, here, 22 + step, place.at_plane(peer))

    def five(self):
        self.wait()
        for index in range(16):
            at = chunk_start(index)
            self.pair_send[at : at + CHUNK] = self.wide_in[index]
        self.copy(self.pair_send, self.pair_in, 38, self.place.mate)

    def end(self, out, layer, over):
        self.wait()
        core = self.place.core
        mine, other = self.pair_send[...], self.pair_in[...]
        out[layer, :36] = jnp.where(core == 0, mine[:36], other[:36])
        out[layer, 36:] = jnp.where(core == 0, other[:36], mine[:36])
        if over is not None:
            over[0] = jnp.where(jnp.max(mine[36].astype(F32)) > 0.0, 1, 0)


def columns(value, first, count):
    rows, wide = value.shape[:2]
    paired = value.reshape(rows, wide // 2, 2, 16, 128)
    return [
        cells(paired[:, (first + step) // 2 : (first + step) // 2 + count, (first + step) % 2])
        for step in range(4)
    ]


def split_pairs(result, rows, count):
    wide = result.reshape(rows, count, 16, 256)
    return jnp.stack([wide[..., :128], wide[..., 128:]], axis=2).reshape(rows, count * 2, 16, 128)


def paired_conv(sources, first, count, weight):
    taps = [tap for value in sources for tap in columns(value, first, count)]
    result = product(jnp.concatenate(taps, axis=1), weight)
    return split_pairs(result, sources[0].shape[0], count)


def gradient_terms(turned, windows):
    total = None
    for at, taps in windows:
        part = product(turned[:, at : at + taps[0].shape[0]], jnp.concatenate(taps, axis=1))
        total = part if total is None else total + part
    return [total[:, tap * 128 : tap * 128 + 128].T for tap in range(9)]


def whole(
    table, state, cotangent, kernels, turns, fresh, summed, sums, over,
    state_blocks, grad_blocks, hidden_blocks, strips, corners, given_strips, given_corners,
    send_a, send_b, send_c, send_d, in_a, in_b, in_c, in_d,
    forward, flipped, grad_wide, wide, total, padded, even, odd, slope, grad_even, grad_odd, grad_turned,
    *rest,
):
    sum_one, sum_two = rest[:9], rest[9:18]
    swap_sems, one_sems, two_sems = rest[18:]
    place = Place()
    me = place.me
    barrier = pltpu.get_barrier_semaphore()

    def greet(where):
        pl.semaphore_signal(barrier, inc=1, device_id=where, device_id_type=MESH_ID)

    for offset in OFFSETS:
        greet({"space": lax.rem(me + offset + SPAN, SPAN)})
    greet(place.mate)
    for step in range(1, 16):
        greet(place.at_plane(lax.rem(place.plane + step, 16)))
    for step in range(1, 8):
        greet(place.at_line(lax.rem(place.z + step, 8)))

    rims_one = Swap(me, send_a, in_a, swap_sems.at[0])
    back_two = Swap(me, send_b, in_b, swap_sems.at[1])
    rims_two = Swap(me, send_c, in_c, swap_sems.at[2])
    back_one = Swap(me, send_d, in_d, swap_sems.at[3])
    reduce_one = Sum(place, sum_one, one_sems)
    reduce_two = Sum(place, sum_two, two_sems)

    for slot in range(2):
        for row in range(8):
            moved = product(turns[0], state[slot, row])
            state_blocks[slot, row] = blocks(moved.astype(BF16))
    take_rims(state_blocks, strips, corners)
    send_rims(table, strips, corners, send_a)
    pl.semaphore_wait(barrier, 29)
    rims_one.start()

    forward[...] = jnp.zeros_like(forward)
    flipped[...] = jnp.zeros_like(flipped)
    for layer in range(2):
        for up in range(3):
            for across in range(3):
                weight = kernels[layer, up, across]
                turned = weight.T
                for side in range(2):
                    at = (up * 4 + side + across) * 128
                    forward[layer, at : at + 128, side * 128 : side * 128 + 128] = weight
                    at = (up * 4 + side + 2 - across) * 128
                    flipped[layer, at : at + 128, side * 128 : side * 128 + 128] = turned
    grad_wide[...] = jnp.zeros_like(grad_wide)
    for slot in range(2):
        present = jnp.where(table[T_PRESENT + slot] > 0, 1.0, 0.0)
        for row in range(8):
            moved = blocks((product(turns[0], cotangent[slot, row]) * present).astype(BF16))
            grad_blocks[slot, row] = moved
            grad_wide[slot, 2 + row, 2:10] = moved
    for slot in range(2):
        for row in (0, 5):
            sources = [grad_wide[slot, row + 2 - up : row + 7 - up] for up in range(3)]
            wide[slot, row : row + 5] = paired_conv(sources, 0, 5, flipped[1])
        total[slot] = wide[slot, 1:9, 1:9]
    give_back(table, wide, turns, send_b, given_strips, given_corners)
    back_two.start()

    rims_one.wait()
    widen(table, state_blocks, strips, corners, in_a, turns, padded)
    for row in range(10):
        both = [halves(padded[slot, row : row + 1])[0] for slot in range(2)]
        even[row] = jnp.concatenate(both, axis=1).astype(BF16)
    for row in range(9):
        both = [
            shifted_up(halves(padded[slot, row : row + 1])[0], halves(padded[slot, row + 1 : row + 2])[0])
            for slot in range(2)
        ]
        odd[row] = jnp.concatenate(both, axis=1).astype(BF16)
    for row in (0, 4):
        sources = [odd[row : row + 4], even[row + 1 : row + 5], odd[row + 1 : row + 5]]
        result = paired_conv(sources, 1, 8, forward[0])
        hidden, slopes = gelu_parts(result)
        slope[row : row + 4] = slopes
        for slot in range(2):
            part = hidden[:, :, slot * 8 : slot * 8 + 8].reshape(4, 8, 16, 128)
            hidden_blocks[slot, row : row + 4] = part.astype(BF16)
    take_rims(hidden_blocks, strips, corners)
    send_rims(table, strips, corners, send_c)
    rims_two.start()

    grad_even[...] = jnp.zeros_like(grad_even)
    grad_odd[...] = jnp.zeros_like(grad_odd)
    back_two.wait()
    take_back(table, in_b, given_strips, given_corners, total)
    for row in range(8):
        both = [total[slot, row].astype(BF16).astype(F32).reshape(16, 8, 128) for slot in range(2)]
        grad = (jnp.concatenate(both, axis=1) * slope[row]).astype(BF16)
        grad_even[row + 1, 2:18] = grad
        grad_turned[:, row * 256 : row * 256 + 256] = cells(grad).T
    for row in range(9):
        low = grad_even[row, 2:18].astype(F32)
        high = grad_even[row + 1, 2:18].astype(F32)
        both = [
            shifted_up(low[:, slot * 8 : slot * 8 + 8], high[:, slot * 8 : slot * 8 + 8])
            for slot in range(2)
        ]
        grad_odd[row + 1, 2:18] = jnp.concatenate(both, axis=1).astype(BF16)
    for row in (0, 5):
        sources = [grad_odd[row + 1 : row + 6], grad_even[row : row + 5], grad_odd[row : row + 5]]
        result = paired_conv(sources, 0, 9, flipped[0])
        blank = jnp.zeros((5, 1, 8, 128), F32)
        for slot in range(2):
            part = jnp.concatenate([blank, result[:, :, slot * 8 : slot * 8 + 8], blank], axis=1)
            wide[slot, row : row + 5] = part.reshape(5, 10, 16, 128)
    give_back(table, wide, turns, send_d, given_strips, given_corners)
    back_one.start()
    for slot in range(2):
        total[slot] = wide[slot, 1:9, 1:9]

    windows = []
    for row in range(0, 8, 2):
        taps = []
        for source, at in ((odd, row), (even, row + 1), (odd, row + 1)):
            for across in range(3):
                taps.append(cells(source[at : at + 2, 1 + across : 17 + across]))
        windows.append((row * 256, taps))
    for tap, term in enumerate(gradient_terms(grad_turned, windows)):
        reduce_one.put(tap * 8, blocks(term)[:4])
        reduce_one.put(tap * 8 + 4, blocks(term)[4:])
    blank = jnp.zeros((1, 16, 128), F32)
    broken = blank + table[T_OVER].astype(F32)
    for half in range(2):
        reduce_one.half_send[half, 36:37] = blank.astype(BF16)
        reduce_two.half_send[half, 36:37] = broken.astype(BF16)
    reduce_one.one()

    for slot in range(2):
        for step in range(4):
            at = slot * 1024 + step * 256
            grad_turned[:, at : at + 256] = cells(grad_blocks[slot, step * 2 : step * 2 + 2]).T
    rims_two.wait()
    widen(table, hidden_blocks, strips, corners, in_c, turns, padded)
    reduce_one.two()
    windows = []
    for slot in range(2):
        for row in (0, 4):
            taps = [
                cells(padded[slot, row + up : row + up + 4, across : across + 8])
                for up in range(3)
                for across in range(3)
            ]
            windows.append((slot * 1024 + row * 128, taps))
    for tap, term in enumerate(gradient_terms(grad_turned, windows)):
        reduce_two.put(tap * 8, blocks(term)[:4])
        reduce_two.put(tap * 8 + 4, blocks(term)[4:])
    reduce_two.one()
    reduce_one.three()

    def finish(slot):
        present = jnp.where(table[T_PRESENT + slot] > 0, 1.0, 0.0)
        for row in (0, 4):
            sources = [padded[slot, row + up : row + up + 4] for up in range(3)]
            result = paired_conv(sources, 0, 4, forward[1])
            value = state_blocks[slot, row : row + 4].astype(F32) + result
            fresh[slot, row : row + 4] = (value * present).astype(BF16)

    reduce_two.two()
    reduce_one.four()
    finish(0)
    reduce_two.three()
    finish(1)
    reduce_one.five()
    reduce_two.four()
    back_one.wait()
    take_back(table, in_d, given_strips, given_corners, total)
    for slot in range(2):
        present = jnp.where(table[T_PRESENT + slot] > 0, 1.0, 0.0)
        value = grad_blocks[slot].astype(F32) + total[slot]
        summed[slot] = (value * present).astype(BF16)
    reduce_two.five()
    reduce_one.end(sums, 0, None)
    reduce_two.end(sums, 1, over)


def settle(scale, fresh, summed, sums, back, next_state, cell_grad, kernel_grads):
    for row in range(fresh.shape[0]):
        next_state[row] = product(back[...], cells(fresh[row])).astype(BF16)
        cell_grad[row] = product(back[...], cells(summed[row])).astype(BF16)
    kernel_grads[...] = sums[...].astype(F32) * scale


def vmem(shape, kind):
    return pltpu.VMEM(shape, kind)


def specs(kinds):
    return [pl.BlockSpec(memory_space=pltpu.SMEM if kind == "s" else pltpu.VMEM) for kind in kinds]


def shape(dims, kind):
    return jax.ShapeDtypeStruct(dims, kind)


TILES = (2, 8, 8, 16, 128)
STRIPS = (8, 8, 16, 128)
CORNERS = (8, 16, 128)
SENT = (6, PART, 16, 128)
NATURAL = (2, 8, 128, 128)


def sum_buffers():
    return [
        vmem((2, HALF, 16, 128), BF16), vmem((HALF, 16, 128), BF16), vmem((HALF, 16, 128), BF16),
        vmem((15, CHUNK, 16, 128), BF16), vmem((8, CHUNK, 16, 128), BF16), vmem((16, CHUNK, 16, 128), BF16),
        vmem((HALF, 16, 128), BF16), vmem((HALF, 16, 128), BF16), vmem((HALF, 16, 128), F32),
    ]


def finished(scale, fresh, summed, sums, back):
    def rows(count, *tail):
        return pl.BlockSpec((count,) + tail, lambda step: (step,) + (0,) * len(tail))

    return pl.pallas_call(
        functools.partial(settle, scale),
        grid=(4,),
        out_shape=[
            shape((16, 128, 128), BF16), shape((16, 128, 128), BF16), shape((2 * UNITS, 16, 128), F32)
        ],
        in_specs=[
            rows(4, 8, 16, 128), rows(4, 8, 16, 128), rows(36, 16, 128),
            pl.BlockSpec((128, 128), lambda step: (0, 0)),
        ],
        out_specs=[rows(4, 128, 128), rows(4, 128, 128), rows(36, 16, 128)],
    )(
        fresh.reshape(16, 8, 16, 128), summed.reshape(16, 8, 16, 128),
        sums.reshape(2 * UNITS, 16, 128), back,
    )


def routed(cell_state, cotangent, kernels, slot_of_tile, neighbours, rotations, corner_flags):
    table = pl.pallas_call(
        plan_kernel,
        out_shape=shape((T_SIZE,), jnp.int32),
        in_specs=specs("ssss"),
        out_specs=specs("s")[0],
        scratch_shapes=[pltpu.SMEM((2 * SPAN,), jnp.int32)],
    )(slot_of_tile, neighbours.T, rotations.T, corner_flags.T)
    scale = 1.0 / math.sqrt(
        cell_state.shape[0] * lax.axis_size("dp") * slot_of_tile.shape[0] * cell_state.shape[2] ** 2
    )
    turns = permutations()
    fresh, summed, sums, over = pl.pallas_call(
        whole,
        out_shape=[
            shape(TILES, BF16), shape(TILES, BF16), shape((2, UNITS, 16, 128), BF16), shape((1,), jnp.int32)
        ],
        in_specs=specs("svvvv"),
        out_specs=specs("vvvs"),
        scratch_shapes=[
            vmem(TILES, BF16), vmem(TILES, BF16), vmem(TILES, BF16),
            vmem(STRIPS, BF16), vmem(CORNERS, BF16), vmem(STRIPS, BF16), vmem(CORNERS, BF16),
        ]
        + [vmem(SENT, BF16)] * 8
        + [
            vmem((2, 1536, 256), BF16), vmem((2, 1536, 256), BF16),
            vmem((2, 12, 12, 16, 128), BF16), vmem((2, 10, 10, 16, 128), F32), vmem(TILES, F32),
            vmem((2, 10, 10, 16, 128), BF16), vmem((10, 20, 16, 128), BF16), vmem((9, 20, 16, 128), BF16),
            vmem((8, 16, 16, 128), F32), vmem((10, 20, 16, 128), BF16), vmem((11, 20, 16, 128), BF16),
            vmem((128, 2048), BF16),
        ]
        + sum_buffers()
        + sum_buffers()
        + [
            pltpu.SemaphoreType.DMA((4, 2, 6)),
            pltpu.SemaphoreType.DMA((2, 39)),
            pltpu.SemaphoreType.DMA((2, 39)),
        ],
        compiler_params=pltpu.CompilerParams(
            vmem_limit_bytes=VMEM_BYTES, collective_id=1, has_side_effects=True
        ),
    )(
        table, cell_state.reshape(NATURAL), cotangent.reshape(NATURAL), kernels,
        jnp.asarray(turns, BF16),
    )
    back = jnp.asarray(turns[1], BF16)
    arrays = (cell_state, cotangent, kernels, slot_of_tile, neighbours, rotations, corner_flags)

    def fast(*_):
        outs = finished(scale, fresh, summed, sums, back)
        return tuple(out.reshape(like) for out, like in zip(outs, (cell_state.shape, cell_state.shape, kernels.shape)))

    return lax.cond(over[0] == 0, fast, shards, *arrays)


def solution(mesh):
    in_specs = (
        P("dp", "space", None, None, None),
        P("dp", "space", None, None, None),
        P(),
        P(),
        P(),
        P(),
        P(),
    )
    out_specs = (P("dp", "space", None, None, None), P("dp", "space", None, None, None), P())
    return jax.shard_map(routed, mesh=mesh, in_specs=in_specs, out_specs=out_specs, check_vma=False)
```

```python
import functools
import math

import jax
import jax.numpy as jnp
import numpy as np
from jax import lax
from jax.experimental import pallas as pl
from jax.experimental.pallas import tpu as pltpu
from jax.sharding import PartitionSpec as P

RES_BLOCKS = 1
DILATION_ONE = 2
DILATION_TWO = 4
REACH_DEV = 3


CONV_AXES = ("NHWC", "HWIO", "NHWC")


def as_sent(shard):

    def short(part):
        return part.astype(jnp.bfloat16) if part.dtype == jnp.float32 else part

    return jax.tree.map(short, shard)


def shifted(value, axis, steps):
    count = lax.axis_size(axis)
    pairs = [(source, (source + steps) % count) for source in range(count)]
    return lax.ppermute(value, axis, pairs)


def boundary(tile_data, rim_depth):
    extent = tile_data.shape[3]
    far = extent - rim_depth
    sides = [
        tile_data[:, :, :rim_depth],
        tile_data[:, :, :, far:],
        tile_data[:, :, far:],
        tile_data[:, :, :, :rim_depth],
    ]
    blocks = [
        tile_data[:, :, :rim_depth, far:],
        tile_data[:, :, far:, far:],
        tile_data[:, :, far:, :rim_depth],
        tile_data[:, :, :rim_depth, :rim_depth],
    ]
    strips = jnp.stack(
        [jnp.rot90(sides[quarter], quarter, axes=(2, 3)) for quarter in range(4)], axis=2
    )
    corners = jnp.stack(
        [jnp.rot90(blocks[quarter], quarter, axes=(2, 3))[:, :, :, ::-1] for quarter in range(4)],
        axis=2,
    )
    return (strips, corners)


def assemble(tile_data, strips, corners):
    edge_parts = [
        jnp.rot90(strips[:, :, quarter, ::-1, ::-1], -quarter, axes=(2, 3)) for quarter in range(4)
    ]
    corner_parts = [
        jnp.rot90(corners[:, :, quarter, ::-1], -quarter, axes=(2, 3)) for quarter in range(4)
    ]
    top_row = jnp.concatenate([corner_parts[3], edge_parts[0], corner_parts[0]], axis=3)
    middle = jnp.concatenate([edge_parts[3], tile_data, edge_parts[1]], axis=3)
    bottom = jnp.concatenate([corner_parts[2], edge_parts[2], corner_parts[1]], axis=3)
    return jnp.concatenate([top_row, middle, bottom], axis=2)


def rim_pieces(tile_data, rim_depth):
    strips, corners = boundary(tile_data, rim_depth)
    joined = jnp.concatenate([strips, corners], axis=4)
    return joined.reshape((joined.shape[0], joined.shape[1] * 4) + joined.shape[3:])


def conv_apply(padded, kernel, spread):
    merged = padded.reshape((-1,) + padded.shape[2:])
    result = lax.conv_general_dilated(
        merged,
        kernel,
        (1, 1),
        "VALID",
        rhs_dilation=(spread, spread),
        dimension_numbers=CONV_AXES,
        preferred_element_type=jnp.float32,
    )
    return result.reshape(padded.shape[:2] + result.shape[1:])


def conv_back(grad_out, kernel, spread):
    merged = grad_out.reshape((-1,) + grad_out.shape[2:])
    flipped = jnp.swapaxes(kernel[::-1, ::-1], 2, 3)
    margin = 2 * spread
    result = lax.conv_general_dilated(
        merged,
        flipped,
        (1, 1),
        ((margin, margin), (margin, margin)),
        rhs_dilation=(spread, spread),
        dimension_numbers=CONV_AXES,
        preferred_element_type=jnp.float32,
    )
    return result.reshape(grad_out.shape[:2] + result.shape[1:])


def kernel_grad(padded, grad_out, spread):
    extent = grad_out.shape[2]
    tap_terms = []
    for row_tap in range(3):
        for col_tap in range(3):
            window = padded[
                :,
                :,
                row_tap * spread : row_tap * spread + extent,
                col_tap * spread : col_tap * spread + extent,
            ]
            tap_terms.append(
                lax.dot_general(
                    window,
                    grad_out,
                    (((0, 1, 2, 3), (0, 1, 2, 3)), ((), ())),
                    preferred_element_type=jnp.float32,
                )
            )
    stacked = jnp.stack(tap_terms)
    return stacked.reshape((3, 3) + stacked.shape[1:])


def halo_plan(slot_of_tile, neighbours, rotations, corner_flags, slot_count):
    span_count = lax.axis_size("space")
    myself = lax.axis_index("space")
    tile_count = slot_of_tile.shape[0]
    owned = myself * slot_count + jnp.arange(slot_count, dtype=jnp.int32)
    matches = slot_of_tile[None, :] == owned[:, None]
    present = jnp.any(matches, axis=1)
    tile_here = jnp.sum(
        jnp.where(matches, jnp.arange(tile_count, dtype=jnp.int32)[None, :], 0), axis=1
    )
    nearby = jnp.take(neighbours, tile_here, axis=0)
    turn_code = jnp.take(rotations, tile_here, axis=0)
    facing = (jnp.arange(8, dtype=jnp.int32)[None, :] % 4 + 2 + turn_code) % 4
    source = jnp.take(slot_of_tile, nearby)
    holder = source // slot_count
    within = source % slot_count
    offset = jnp.clip(
        (myself - holder + span_count + REACH_DEV) % span_count - REACH_DEV, -REACH_DEV, REACH_DEV
    )
    select = ((offset + REACH_DEV) * slot_count + within) * 4 + facing
    keep_corner = jnp.take(corner_flags, tile_here, axis=0) == 0
    return (select[:, :4].reshape(-1), select[:, 4:].reshape(-1), keep_corner.reshape(-1), present)


def fetch_near(bundle):
    arrived = {0: bundle}
    for offset in list(range(-REACH_DEV, 0)) + list(range(1, REACH_DEV + 1)):
        arrived[offset] = shifted(as_sent(bundle), "space", offset).astype(bundle.dtype)
    return [arrived[offset] for offset in range(-REACH_DEV, REACH_DEV + 1)]


def return_near(parts):
    total = parts[0]
    for offset in list(range(-REACH_DEV, 0)) + list(range(1, REACH_DEV + 1)):
        total = total + shifted(parts[offset].astype(jnp.bfloat16), "space", -offset).astype(
            jnp.float32
        )
    return total


def halo_forward(tile_data, rim_depth, plan):
    pick_edge, pick_corner, keep_corner = plan[:3]
    samples_here, slot_count, extent = (tile_data.shape[0], tile_data.shape[1], tile_data.shape[2])
    channels = tile_data.shape[4]
    gathered = jnp.concatenate(fetch_near(rim_pieces(tile_data, rim_depth)), axis=1)
    edge_part = jnp.take(gathered, pick_edge, axis=1)[:, :, :, :extent]
    corner_part = jnp.take(gathered, pick_corner, axis=1)[:, :, :, extent:]
    corner_part = jnp.where(
        keep_corner[None, :, None, None, None], corner_part, jnp.zeros((), corner_part.dtype)
    )
    strips = edge_part.reshape(samples_here, slot_count, 4, rim_depth, extent, channels)
    corners = corner_part.reshape(samples_here, slot_count, 4, rim_depth, rim_depth, channels)
    return assemble(tile_data, strips, corners)


def halo_backward(grad_wide, rim_depth, plan):
    pick_edge, pick_corner, keep_corner = plan[:3]
    samples_here, slot_count = (grad_wide.shape[0], grad_wide.shape[1])
    extent = grad_wide.shape[2] - 2 * rim_depth
    channels = grad_wide.shape[4]
    tile_zero = jnp.zeros((samples_here, slot_count, extent, extent, channels), jnp.float32)
    strip_zero = jnp.zeros((samples_here, slot_count, 4, rim_depth, extent, channels), jnp.float32)
    corner_zero = jnp.zeros(
        (samples_here, slot_count, 4, rim_depth, rim_depth, channels), jnp.float32
    )
    _, assemble_back = jax.vjp(assemble, tile_zero, strip_zero, corner_zero)
    grad_tiles, grad_strips, grad_corners = assemble_back(grad_wide)
    pieces = slot_count * 4
    grad_corners = grad_corners.reshape(samples_here, pieces, rim_depth, rim_depth, channels)
    grad_corners = jnp.where(keep_corner[None, :, None, None, None], grad_corners, 0.0)
    spread_out = jnp.zeros(
        (samples_here, (2 * REACH_DEV + 1) * pieces, rim_depth, extent + rim_depth, channels),
        jnp.float32,
    )
    spread_out = spread_out.at[:, pick_edge, :, :extent].add(
        grad_strips.reshape(samples_here, pieces, rim_depth, extent, channels)
    )
    spread_out = spread_out.at[:, pick_corner, :, extent:].add(grad_corners)
    parts = {
        offset: spread_out[:, (offset + REACH_DEV) * pieces : (offset + REACH_DEV + 1) * pieces]
        for offset in range(-REACH_DEV, REACH_DEV + 1)
    }
    returned = return_near(parts)
    _, rim_back = jax.vjp(lambda tile_part: rim_pieces(tile_part, rim_depth), tile_zero)
    return grad_tiles + rim_back(returned)[0]


def sum_over(value, axis):
    count = lax.axis_size(axis)
    step = 1
    while step < count:
        pairs = [(source, source ^ step) for source in range(count)]
        value = value + lax.ppermute(value, axis, pairs)
        step *= 2
    return value


def shards(cell_state, cotangent, kernels, slot_of_tile, neighbours, rotations, corner_flags):
    plan = halo_plan(slot_of_tile, neighbours, rotations, corner_flags, cell_state.shape[1])
    keep_slot = plan[3][None, :, None, None, None]
    current = cell_state
    block_at = 0
    widened = halo_forward(current, DILATION_ONE, plan)
    before = conv_apply(widened, kernels[2 * block_at], DILATION_ONE)
    hidden = jax.nn.gelu(before).astype(jnp.bfloat16)
    widened_two = halo_forward(hidden, DILATION_TWO, plan)
    branch = conv_apply(widened_two, kernels[2 * block_at + 1], DILATION_TWO)
    stored = [(widened, before, widened_two)]
    current = (current.astype(jnp.float32) + branch).astype(jnp.bfloat16)
    next_state = jnp.where(keep_slot, current, jnp.zeros((), jnp.bfloat16))
    gradient = jnp.where(keep_slot, cotangent, jnp.zeros((), jnp.bfloat16))
    kernel_terms = [None] * (2 * RES_BLOCKS)
    extent = cell_state.shape[2]
    norm_scale = 1.0 / math.sqrt(
        cell_state.shape[0] * lax.axis_size("dp") * slot_of_tile.shape[0] * extent * extent
    )
    for block_at in reversed(range(RES_BLOCKS)):
        widened, before, widened_two = stored[block_at]
        outer_term = kernel_grad(widened_two, gradient, DILATION_TWO)
        kernel_terms[2 * block_at + 1] = outer_term
        grad_hidden = halo_backward(
            conv_back(gradient, kernels[2 * block_at + 1], DILATION_TWO), DILATION_TWO, plan
        ).astype(jnp.bfloat16)
        _, gelu_back = jax.vjp(jax.nn.gelu, before)
        grad_before = gelu_back(grad_hidden.astype(jnp.float32))[0].astype(jnp.bfloat16)
        inner_term = kernel_grad(widened, grad_before, DILATION_ONE)
        kernel_terms[2 * block_at] = inner_term
        returned = halo_backward(
            conv_back(grad_before, kernels[2 * block_at], DILATION_ONE), DILATION_ONE, plan
        )
        gradient = (gradient.astype(jnp.float32) + returned).astype(jnp.bfloat16)
    stacked = jnp.stack(kernel_terms)
    stacked = sum_over(sum_over(stacked, "space"), "dp")
    return (next_state, gradient, stacked * norm_scale)


MESH_ID = pl.DeviceIdType.MESH
SPAN = 128
STRIP_CAP = (1, 2, 2, 2, 2, 1)
CORNER_CAP = 4
PART = 20
OFFSETS = (-3, -2, -1, 1, 2, 3)
ORDER = (2, 3, 1, 4, 0, 5)
SELF = 6
NOT_THERE = 32
T_STRIP_LIST, T_CORNER_LIST, T_GIVE_STRIP, T_GIVE_CORNER = 0, 12, 36, 48
T_ADD, T_PIECES, T_PRESENT = 72, 104, 200
T_OVER, T_SPARE, T_SIZE = 202, 203, 208
VMEM_BYTES = 56 * 1024 * 1024
F32 = jnp.float32
BF16 = jnp.bfloat16


def cell_order():
    rows, cols = np.meshgrid(np.arange(4), np.arange(4), indexing="ij")
    return ((cols // 2) * 8 + (rows // 2) * 4 + (rows % 2) * 2 + cols % 2).astype(np.int64)


def permutations():
    order = cell_order()
    to_blocks = np.zeros((128, 128), np.float32)
    for row in range(4):
        for col in range(32):
            to_blocks[(col // 4) * 16 + order[row, col % 4], row * 32 + col] = 1
    mats = [to_blocks, to_blocks.T]
    for turn in range(4):
        turned = np.rot90(order, turn)
        small = np.zeros((16, 16), np.float32)
        small[order.reshape(-1), turned.reshape(-1)] = 1
        for flip in range(2):
            line = np.eye(8)[::-1] if flip else np.eye(8)
            mats.append(np.kron(line, small))
    return np.stack(mats)


def turn_matrix(turn, flip):
    return 2 + 2 * turn + flip


def flips(edge, turn):
    side = (edge + 2 + turn) & 1
    once = jnp.where((turn == 1) & (side == 0), 1, 0)
    thrice = jnp.where((turn == 3) & (side == 1), 1, 0)
    return jnp.where(turn == 2, 1, once + thrice)


def plan_kernel(slot_ref, near_ref, turn_ref, flag_ref, table, tile_at):
    me = lax.axis_index("space")
    for entry in range(T_SIZE):
        table[entry] = 0
    for entry in range(8):
        table[T_ADD + entry] = NOT_THERE
        table[T_ADD + 16 + entry] = NOT_THERE
    for rel in range(14):
        tile_at[(me + rel // 2 - 3 + SPAN) % SPAN * 2 + rel % 2] = -1

    def place(step, carry):
        for inner in range(16):
            tile = step * 16 + inner
            tile_at[slot_ref[tile]] = tile
        return carry

    lax.fori_loop(0, slot_ref.shape[0] // 16, place, 0)
    over = jnp.int32(0)
    core = me % 2

    def contribute(hit, kind, entry, code, turn):
        place_at = jnp.where(hit, T_ADD + kind * 16 + entry, T_SPARE)
        taken = jnp.where(hit & (table[place_at] != NOT_THERE), 1, 0)
        table[place_at] = code
        table[place_at + jnp.where(hit, 8, 0)] = jnp.where(hit, turn, code)
        return taken

    for where, offset in enumerate(OFFSETS):
        seen = [jnp.int32(0), jnp.int32(0)]
        for slot in range(2):
            tile = tile_at[(me + offset + SPAN) % SPAN * 2 + slot]
            row = jnp.maximum(tile, 0)
            for piece in range(8):
                kind = piece // 4
                source = slot_ref[near_ref[piece, row]]
                hit = (tile >= 0) & (source // 2 == me)
                turn = turn_ref[piece, row] & 3
                entry = source % 2 * 4 + ((piece + 2 + turn) & 3)
                cap = CORNER_CAP if kind else STRIP_CAP[where]
                rank = jnp.minimum(seen[kind], cap - 1)
                if offset in (-3, 3):
                    over = over + jnp.where(hit & (core == (0 if offset < 0 else 1)), 1, 0)
                over = over + jnp.where(hit & (seen[kind] >= cap), 1, 0)
                seen[kind] = seen[kind] + jnp.where(hit, 1, 0)
                width = 4 if kind else 2
                place_at = (T_CORNER_LIST if kind else T_STRIP_LIST) + where * width + rank
                table[jnp.where(hit, place_at, T_SPARE)] = entry
                over = over + contribute(hit, kind, entry, where * width + rank, turn)
    seen = [[jnp.int32(0)] * 7, [jnp.int32(0)] * 7]
    for slot in range(2):
        tile = tile_at[me * 2 + slot]
        row = jnp.maximum(tile, 0)
        valid = jnp.where(tile >= 0, 1, 0)
        table[T_PRESENT + slot] = valid
        for piece in range(8):
            kind = piece // 4
            source = slot_ref[near_ref[piece, row]]
            turn = turn_ref[piece, row] & 3
            offset = jnp.clip((source // 2 - me + 3 + SPAN) % SPAN, 0, 6)
            where = jnp.where(offset == 3, SELF, jnp.where(offset < 3, offset, offset - 1))
            rank = jnp.int32(0)
            for choice in range(7):
                match = jnp.where(offset == choice, valid, 0)
                rank = rank + match * seen[kind][choice]
                seen[kind][choice] = seen[kind][choice] + match
            rank = jnp.minimum(rank, 3 if kind else 1)
            keep = valid
            if kind:
                keep = valid * jnp.where(flag_ref[piece - 4, row] == 0, 1, 0)
            entry = source % 2 * 4 + ((piece + 2 + turn) & 3)
            base = T_PIECES + (slot * 8 + piece) * 6
            table[base] = valid
            table[base + 1] = where
            table[base + 2] = rank
            table[base + 3] = turn
            table[base + 4] = entry
            table[base + 5] = keep
            mine = slot * 4 + piece % 4
            own = (valid > 0) & (where == SELF)
            away = (valid > 0) & (where != SELF)
            place_at = (T_GIVE_CORNER if kind else T_GIVE_STRIP) + where * (4 if kind else 2) + rank
            table[jnp.where(away, place_at, T_SPARE)] = mine
            over = over + contribute(own, kind, entry, (24 if kind else 12) + mine, turn)
    table[T_OVER] = over


def piece_of(table, slot, piece):
    base = T_PIECES + (slot * 8 + piece) * 6
    return [table[base + field] for field in range(6)]


def blocks(value):
    return value.reshape((-1, 16, 128))


def cells(value):
    return value.reshape((-1, 128))


def product(left, right):
    return jnp.dot(left, right, preferred_element_type=F32)


EDGE_OF = ((0, slice(None)), (slice(None), 7), (7, slice(None)), (slice(None), 0))
CORNER_OF = ((0, 7), (7, 7), (7, 0), (0, 0))
BAND_OF = ((0, slice(1, 9)), (slice(1, 9), 9), (9, slice(1, 9)), (slice(1, 9), 0))
BLOCK_OF = ((0, 9), (9, 9), (9, 0), (0, 0))


def take_rims(tile_ref, strips, corners):
    for slot in range(2):
        for side in range(4):
            strips[slot * 4 + side] = blocks(tile_ref[(slot,) + EDGE_OF[side]])
            corners[slot * 4 + side] = tile_ref[(slot,) + CORNER_OF[side]]


def send_rims(table, strips, corners, send, strip_list=T_STRIP_LIST, corner_list=T_CORNER_LIST):
    for where in range(6):
        for rank in range(STRIP_CAP[where]):
            send[where, 4 + rank * 8 : 12 + rank * 8] = strips[table[strip_list + where * 2 + rank]]
        for rank in range(CORNER_CAP):
            send[where, rank] = corners[table[corner_list + where * 4 + rank]]


def corner_turns(table, turns, back):
    parts = []
    for slot in range(2):
        for side in range(4):
            fields = piece_of(table, slot, 4 + side)
            turn = (4 - fields[3]) & 3 if back else fields[3]
            rows = turns[turn_matrix(turn, 0)]
            at = (slot * 4 + side) * 16
            parts.append(rows[at : at + 16] * jnp.where(fields[5] > 0, 1.0, 0.0).astype(BF16))
    return jnp.concatenate(parts, axis=0)


def widen(table, tile_ref, strips, corners, arrived, turns, padded):
    for slot in range(2):
        padded[slot, 1:9, 1:9] = tile_ref[slot]
        for edge in range(4):
            valid, where, rank, turn, entry, keep = piece_of(table, slot, edge)
            own = strips[entry]
            other = arrived[jnp.minimum(where, 5), pl.ds(4 + rank * 8, 8)]
            strip = jnp.where(where == SELF, own, other)
            strip = jnp.where(valid > 0, strip, jnp.zeros_like(strip))
            turned = product(turns[turn_matrix(turn, flips(edge, turn))], cells(strip))
            padded[(slot,) + BAND_OF[edge]] = blocks(turned.astype(BF16))
    stack = []
    for slot in range(2):
        for side in range(4):
            valid, where, rank, turn, entry, keep = piece_of(table, slot, 4 + side)
            block = jnp.where(where == SELF, corners[entry], arrived[jnp.minimum(where, 5), rank])
            stack.append(jnp.where(valid > 0, block, jnp.zeros_like(block)))
    turned = product(corner_turns(table, turns, False), jnp.concatenate(stack, axis=0))
    turned = blocks(turned.astype(BF16))
    for slot in range(2):
        for side in range(4):
            padded[(slot,) + BLOCK_OF[side]] = turned[slot * 4 + side]


def give_back(table, wide, turns, send, strips, corners):
    for slot in range(2):
        for edge in range(4):
            valid, where, rank, turn, entry, keep = piece_of(table, slot, edge)
            band = cells(blocks(wide[(slot,) + BAND_OF[edge]])).astype(BF16)
            turned = product(turns[turn_matrix((4 - turn) & 3, flips(edge, turn))], band)
            strips[slot * 4 + edge] = blocks(turned.astype(BF16))
    stack = [wide[(slot,) + BLOCK_OF[side]].astype(BF16) for slot in range(2) for side in range(4)]
    turned = product(corner_turns(table, turns, True), jnp.concatenate(stack, axis=0))
    corners[...] = blocks(turned.astype(BF16))
    send_rims(table, strips, corners, send, T_GIVE_STRIP, T_GIVE_CORNER)


def owner_of(table, kind, entry):
    code = table[T_ADD + kind * 16 + entry]
    turn = table[T_ADD + kind * 16 + 8 + entry]
    return code, turn, (entry % 4 - 2 - turn) & 3


def copied_strip(code, arrived, strips):
    far = jnp.minimum(code, 11)
    near = jnp.clip(code - 12, 0, 7)
    part = jnp.where(code < 12, arrived[far // 2, pl.ds(4 + far % 2 * 8, 8)], strips[near])
    return jnp.where(code == NOT_THERE, jnp.zeros_like(part), part)


def copied_corner(code, arrived, corners):
    far = jnp.minimum(code, 23)
    near = jnp.clip(code - 24, 0, 7)
    part = jnp.where(code < 24, arrived[far // 4, far % 4], corners[near])
    return jnp.where(code == NOT_THERE, jnp.zeros_like(part), part)


def take_back(table, arrived, strips, corners, total):
    for slot in range(2):
        for side in range(4):
            at = (slot,) + EDGE_OF[side]
            code = owner_of(table, 0, slot * 4 + side)[0]
            total[at] = total[at] + copied_strip(code, arrived, strips).astype(F32)
    for slot in range(2):
        for side in range(4):
            at = (slot,) + CORNER_OF[side]
            code = owner_of(table, 1, slot * 4 + side)[0]
            total[at] = total[at] + copied_corner(code, arrived, corners).astype(F32)


STRIP_TAPS = (
    ((0, 0), (0, 1), (0, 2)),
    ((0, 2), (1, 2), (2, 2)),
    ((2, 0), (2, 1), (2, 2)),
    ((0, 0), (1, 0), (2, 0)),
)
CORNER_TAPS = ((0, 2), (2, 2), (2, 0), (0, 0))


def rim_terms(table, arrived, given_strips, given_corners, strips, corners, turns, masked):
    rims = []
    for entry in range(8):
        code, turn, edge = owner_of(table, 0, entry)
        grad = cells(copied_strip(code, arrived, given_strips)).T
        for choice in range(4):
            chosen = jnp.where(edge == choice, grad, jnp.zeros_like(grad))
            masked[choice * 128 : choice * 128 + 128, entry * 128 : entry * 128 + 128] = chosen
        band = product(turns[turn_matrix(turn, flips(edge, turn))], cells(strips[entry])).astype(BF16)
        blank = jnp.zeros((16, 128), BF16)
        longer = jnp.concatenate([blank, band, blank], axis=0)
        rims.append(jnp.concatenate([longer[step * 16 : step * 16 + 128] for step in range(3)], axis=1))
    edges = product(masked[...], jnp.concatenate(rims, axis=0))
    lane = lax.broadcasted_iota(jnp.int32, (128, 128), 1) // 16
    which = jnp.zeros((128, 128), jnp.int32)
    grads, parts = [], []
    for entry in range(8):
        code, turn, side = owner_of(table, 1, entry)
        grads.append(copied_corner(code, arrived, given_corners))
        which = jnp.where(lane == entry, side, which)
        parts.append(turns[turn_matrix(turn, 0)][entry * 16 : entry * 16 + 16])
    block = product(jnp.concatenate(parts, axis=0), cells(corners[...])).astype(BF16)
    grad = jnp.concatenate(grads, axis=0).astype(F32).T
    spread = [jnp.where(which == choice, grad, jnp.zeros_like(grad)) for choice in range(4)]
    ends = product(jnp.concatenate(spread, axis=0).astype(BF16), block)
    sums = [None] * 9
    for choice in range(4):
        rows = slice(choice * 128, choice * 128 + 128)
        found = [(tap, edges[rows, step * 128 : step * 128 + 128]) for step, tap in enumerate(STRIP_TAPS[choice])]
        found.append((CORNER_TAPS[choice], ends[rows]))
        for (up, across), value in found:
            old = sums[up * 3 + across]
            sums[up * 3 + across] = value if old is None else old + value
    return sums


def halves(value):
    return value.astype(F32).reshape(value.shape[0], value.shape[1] * 2, 8, 128)


def shifted_up(upper, lower):
    low = lax.broadcasted_iota(jnp.int32, upper.shape, upper.ndim - 2) < 4
    mixed = jnp.where(low, lower, upper)
    return jnp.concatenate([mixed[..., 4:, :], mixed[..., :4, :]], axis=mixed.ndim - 2)


def gelu_parts(value):
    root = math.sqrt(2.0 / math.pi)
    square = value * value
    bent = jnp.tanh(root * (value + 0.044715 * (value * square)))
    half = 0.5 * (1.0 + bent)
    slope = half + 0.5 * value * (1.0 - bent * bent) * (root * (1.0 + 3 * 0.044715 * square))
    return (value * half, slope)


UNITS = 72
HALF = 37
CHUNK = 3


def chunk_start(index):
    return (index * (HALF - CHUNK)) // 15


class Swap:
    def __init__(self, me, send, arrived, sems):
        core = me % 2
        far = 5 - 5 * core
        self.copies = []
        for where in (2, 3, 1, 4, far):
            near = isinstance(where, int)
            size = 4 + 8 * (STRIP_CAP[where] if near else STRIP_CAP[0])
            offset = OFFSETS[where] if near else 3 - 6 * core
            self.copies.append(
                pltpu.make_async_remote_copy(
                    src_ref=send.at[where, pl.ds(0, size)],
                    dst_ref=arrived.at[5 - where, pl.ds(0, size)],
                    send_sem=sems.at[0, where if near else 0],
                    recv_sem=sems.at[1, 5 - where if near else 0],
                    device_id={"space": lax.rem(me + offset + SPAN, SPAN)},
                    device_id_type=MESH_ID,
                )
            )

    def start(self):
        for copy in self.copies:
            copy.start()

    def wait(self):
        for copy in self.copies:
            copy.wait()


class Place:
    def __init__(self):
        me = lax.axis_index("space")
        self.me = me
        self.core, self.y, self.z, self.x_lo = me % 2, me // 2 % 4, me // 8 % 8, me // 64
        self.plane = (lax.axis_index("dp") * 2 + self.x_lo) * 4 + self.y
        self.mate = {"space": me + 1 - 2 * self.core}

    def at_plane(self, index):
        return {
            "dp": index // 8,
            "space": ((index // 4 % 2) * 8 + self.z) * 8 + index % 4 * 2 + self.core,
        }

    def at_line(self, index):
        return {"space": (self.x_lo * 8 + index) * 8 + self.y * 2 + self.core}


class Sum:
    def __init__(self, place, buffers, sems):
        self.place = place
        self.half_send, self.half_in, self.plane_send, self.plane_in, self.line_in = buffers[:5]
        self.wide_in, self.pair_send, self.pair_in, self.acc = buffers[5:]
        self.sems = sems
        self.copies = []

    def copy(self, source, target, index, where):
        one = pltpu.make_async_remote_copy(
            src_ref=source,
            dst_ref=target,
            send_sem=self.sems.at[0, index],
            recv_sem=self.sems.at[1, index],
            device_id=where,
            device_id_type=MESH_ID,
        )
        one.start()
        self.copies.append(one)

    def put(self, terms):
        for tap, term in enumerate(terms):
            value = blocks(term.astype(BF16))
            for part in range(2):
                half, at = divmod(tap * 8 + part * 4, 36)
                self.half_send[half, at : at + 4] = value[part * 4 : part * 4 + 4]

    def wait(self):
        for one in self.copies:
            one.wait()
        self.copies = []

    def one(self):
        place = self.place
        self.copy(self.half_send.at[1 - place.core], self.half_in, 0, place.mate)

    def two(self):
        place = self.place
        self.wait()
        self.acc[...] = self.half_send[place.core].astype(F32) + self.half_in[...].astype(F32)
        self.plane_send[...] = self.acc[...].astype(BF16)
        for step in range(1, 16):
            peer = lax.rem(place.plane + step, 16)
            source = self.plane_send.at[pl.ds(chunk_start(peer), CHUNK)]
            self.copy(source, self.plane_in.at[step - 1], step, place.at_plane(peer))

    def three(self):
        place = self.place
        self.wait()
        total = self.acc[pl.ds(chunk_start(place.plane), CHUNK)]
        for step in range(15):
            total = total + self.plane_in[step].astype(F32)
        self.line_in[place.z] = total.astype(BF16)
        for step in range(1, 8):
            peer = lax.rem(place.z + step, 8)
            self.copy(self.line_in.at[place.z], self.line_in.at[place.z], 15 + step, place.at_line(peer))

    def four(self):
        place = self.place
        self.wait()
        total = self.line_in[0].astype(F32)
        for index in range(1, 8):
            total = total + self.line_in[index].astype(F32)
        self.wide_in[place.plane] = total.astype(BF16)
        for step in range(1, 16):
            peer = lax.rem(place.plane + step, 16)
            here = self.wide_in.at[place.plane]
            self.copy(here, here, 22 + step, place.at_plane(peer))

    def five(self):
        self.wait()
        for index in range(16):
            at = chunk_start(index)
            self.pair_send[at : at + CHUNK] = self.wide_in[index]
        self.copy(self.pair_send, self.pair_in, 38, self.place.mate)

    def end(self, out, layer, over):
        self.wait()
        core = self.place.core
        mine, other = self.pair_send[...], self.pair_in[...]
        out[layer, :36] = jnp.where(core == 0, mine[:36], other[:36])
        out[layer, 36:] = jnp.where(core == 0, other[:36], mine[:36])
        if over is not None:
            over[0] = jnp.where(jnp.max(mine[36].astype(F32)) > 0.0, 1, 0)


def columns(value, first, count):
    rows, wide = value.shape[:2]
    paired = value.reshape(rows, wide // 2, 2, 16, 128)
    return [
        cells(paired[:, (first + step) // 2 : (first + step) // 2 + count, (first + step) % 2])
        for step in range(4)
    ]


def split_pairs(result, rows, count):
    wide = result.reshape(rows, count, 16, 256)
    return jnp.stack([wide[..., :128], wide[..., 128:]], axis=2).reshape(rows, count * 2, 16, 128)


def paired_conv(sources, first, count, weight):
    taps = [tap for value in sources for tap in columns(value, first, count)]
    result = product(jnp.concatenate(taps, axis=1), weight)
    return split_pairs(result, sources[0].shape[0], count)


def gradient_terms(turned, windows, extra=None):
    total = None
    for at, taps in windows:
        part = product(turned[:, at : at + taps[0].shape[0]], jnp.concatenate(taps, axis=1))
        total = part if total is None else total + part
    terms = [total[:, tap * 128 : tap * 128 + 128] for tap in range(9)]
    if extra is not None:
        terms = [term if more is None else term + more for term, more in zip(terms, extra)]
    return [term.T for term in terms]


def whole(
    table, state, cotangent, kernels, turns, fresh, summed, sums, over,
    state_blocks, grad_blocks, hidden_blocks, strips, corners, given_strips, given_corners,
    grad_strips, grad_corners,
    send_a, send_b, send_c, send_d, send_e, in_a, in_b, in_c, in_d, in_e,
    forward, flipped, grad_wide, wide, total, padded, widened, even, odd, slope, grad_even, grad_odd,
    turned_one, turned_two, masked, *rest,
):
    swap_sems, one_sems, two_sems = rest[18:]
    place = Place()
    me = place.me
    barrier = pltpu.get_barrier_semaphore()

    def greet(where):
        pl.semaphore_signal(barrier, inc=1, device_id=where, device_id_type=MESH_ID)

    for offset in OFFSETS:
        greet({"space": lax.rem(me + offset + SPAN, SPAN)})
    greet(place.mate)
    for step in range(1, 16):
        greet(place.at_plane(lax.rem(place.plane + step, 16)))
    for step in range(1, 8):
        greet(place.at_line(lax.rem(place.z + step, 8)))

    rims_one = Swap(me, send_a, in_a, swap_sems.at[0])
    back_two = Swap(me, send_b, in_b, swap_sems.at[1])
    rims_two = Swap(me, send_c, in_c, swap_sems.at[2])
    back_one = Swap(me, send_d, in_d, swap_sems.at[3])
    rims_grad = Swap(me, send_e, in_e, swap_sems.at[4])
    reduce_one = Sum(place, rest[:9], one_sems)
    reduce_two = Sum(place, rest[9:18], two_sems)

    for slot in range(2):
        for row in range(8):
            moved = product(turns[0], state[slot, row])
            state_blocks[slot, row] = blocks(moved.astype(BF16))
    take_rims(state_blocks, strips, corners)
    send_rims(table, strips, corners, send_a)
    pl.semaphore_wait(barrier, 29)
    rims_one.start()

    grad_wide[...] = jnp.zeros_like(grad_wide)
    for slot in range(2):
        present = jnp.where(table[T_PRESENT + slot] > 0, 1.0, 0.0)
        for row in range(8):
            moved = blocks((product(turns[0], cotangent[slot, row]) * present).astype(BF16))
            grad_blocks[slot, row] = moved
            grad_wide[slot, 2 + row, 2:10] = moved
    take_rims(grad_blocks, grad_strips, grad_corners)
    for slot in range(2):
        for side in range(4):
            keep = jnp.where(piece_of(table, slot, 4 + side)[5] > 0, 1.0, 0.0).astype(BF16)
            at = slot * 4 + side
            grad_corners[at] = grad_corners[at] * keep
    send_rims(table, grad_strips, grad_corners, send_e, T_GIVE_STRIP, T_GIVE_CORNER)
    rims_grad.start()

    forward[...] = jnp.zeros_like(forward)
    flipped[...] = jnp.zeros_like(flipped)
    for layer in range(2):
        for up in range(3):
            for across in range(3):
                weight = kernels[layer, up, across]
                turned = weight.T
                for side in range(2):
                    at = (up * 4 + side + across) * 128
                    forward[layer, at : at + 128, side * 128 : side * 128 + 128] = weight
                    at = (up * 4 + side + 2 - across) * 128
                    flipped[layer, at : at + 128, side * 128 : side * 128 + 128] = turned
    for slot in range(2):
        for row in (0, 5):
            sources = [grad_wide[slot, row + 2 - up : row + 7 - up] for up in range(3)]
            wide[slot, row : row + 5] = paired_conv(sources, 0, 5, flipped[1])
        total[slot] = wide[slot, 1:9, 1:9]
    give_back(table, wide, turns, send_b, given_strips, given_corners)
    back_two.start()

    for slot in range(2):
        for step in range(4):
            at = slot * 1024 + step * 256
            turned_two[:, at : at + 256] = cells(grad_blocks[slot, step * 2 : step * 2 + 2]).T
    widened[...] = jnp.zeros_like(widened)
    grad_even[...] = jnp.zeros_like(grad_even)
    grad_odd[...] = jnp.zeros_like(grad_odd)
    for slot in range(2):
        padded[slot, 1:9, 1:9] = state_blocks[slot]

    def arrange(rows_even, rows_odd, span):
        def half_rows(slot, row):
            return halves(padded[slot, row : row + 1, span])[0]

        at = slice(span.start * 2, span.stop * 2)
        for row in rows_even:
            both = [half_rows(slot, row) for slot in range(2)]
            even[row, at] = jnp.concatenate(both, axis=1).astype(BF16)
        for row in rows_odd:
            both = [shifted_up(half_rows(slot, row), half_rows(slot, row + 1)) for slot in range(2)]
            odd[row, at] = jnp.concatenate(both, axis=1).astype(BF16)

    arrange(range(1, 9), range(1, 8), slice(1, 9))
    rims_one.wait()
    widen(table, state_blocks, strips, corners, in_a, turns, padded)
    arrange(range(1, 9), range(1, 8), slice(0, 1))
    arrange(range(1, 9), range(1, 8), slice(9, 10))
    arrange((), (0, 8), slice(0, 10))
    for row in (0, 4):
        sources = [odd[row : row + 4], even[row + 1 : row + 5], odd[row + 1 : row + 5]]
        result = paired_conv(sources, 1, 8, forward[0])
        hidden, slopes = gelu_parts(result)
        slope[row : row + 4] = slopes
        for slot in range(2):
            part = hidden[:, :, slot * 8 : slot * 8 + 8].reshape(4, 8, 16, 128).astype(BF16)
            hidden_blocks[slot, row : row + 4] = part
            widened[slot, row + 1 : row + 5, 1:9] = part
    take_rims(hidden_blocks, strips, corners)
    send_rims(table, strips, corners, send_c)
    rims_two.start()

    rims_grad.wait()
    extra = rim_terms(table, in_e, grad_strips, grad_corners, strips, corners, turns, masked)
    windows = []
    for slot in range(2):
        for row in (0, 4):
            taps = [
                cells(widened[slot, row + up : row + up + 4, across : across + 8])
                for up in range(3)
                for across in range(3)
            ]
            windows.append((slot * 1024 + row * 128, taps))
    reduce_two.put(gradient_terms(turned_two, windows, extra))
    broken = jnp.zeros((1, 16, 128), F32) + table[T_OVER].astype(F32)
    for half in range(2):
        reduce_one.half_send[half, 36:37] = jnp.zeros((1, 16, 128), BF16)
        reduce_two.half_send[half, 36:37] = broken.astype(BF16)
    reduce_two.one()

    back_two.wait()
    take_back(table, in_b, given_strips, given_corners, total)
    for row in range(8):
        both = [total[slot, row].astype(BF16).astype(F32).reshape(16, 8, 128) for slot in range(2)]
        grad = (jnp.concatenate(both, axis=1) * slope[row]).astype(BF16)
        grad_even[row + 1, 2:18] = grad
        turned_one[:, row * 256 : row * 256 + 256] = cells(grad).T
    reduce_two.two()
    windows = []
    for row in range(0, 8, 2):
        taps = []
        for source, at in ((odd, row), (even, row + 1), (odd, row + 1)):
            for across in range(3):
                taps.append(cells(source[at : at + 2, 1 + across : 17 + across]))
        windows.append((row * 256, taps))
    reduce_one.put(gradient_terms(turned_one, windows))
    reduce_one.one()

    for row in range(9):
        low = grad_even[row, 2:18].astype(F32)
        high = grad_even[row + 1, 2:18].astype(F32)
        both = [
            shifted_up(low[:, slot * 8 : slot * 8 + 8], high[:, slot * 8 : slot * 8 + 8])
            for slot in range(2)
        ]
        grad_odd[row + 1, 2:18] = jnp.concatenate(both, axis=1).astype(BF16)
    reduce_one.two()

    def returned(row):
        sources = [grad_odd[row + 1 : row + 6], grad_even[row : row + 5], grad_odd[row : row + 5]]
        result = paired_conv(sources, 0, 9, flipped[0])
        blank = jnp.zeros((5, 1, 8, 128), F32)
        for slot in range(2):
            part = jnp.concatenate([blank, result[:, :, slot * 8 : slot * 8 + 8], blank], axis=1)
            wide[slot, row : row + 5] = part.reshape(5, 10, 16, 128)

    def finish(slot):
        present = jnp.where(table[T_PRESENT + slot] > 0, 1.0, 0.0)
        for row in (0, 4):
            sources = [widened[slot, row + up : row + up + 4] for up in range(3)]
            result = paired_conv(sources, 0, 4, forward[1])
            value = state_blocks[slot, row : row + 4].astype(F32) + result
            fresh[slot, row : row + 4] = (value * present).astype(BF16)

    returned(0)
    returned(5)
    give_back(table, wide, turns, send_d, given_strips, given_corners)
    back_one.start()
    for slot in range(2):
        total[slot] = wide[slot, 1:9, 1:9]
    reduce_two.three()
    reduce_one.three()
    rims_two.wait()
    widen(table, hidden_blocks, strips, corners, in_c, turns, widened)
    finish(0)
    finish(1)
    reduce_two.four()
    reduce_one.four()
    back_one.wait()
    take_back(table, in_d, given_strips, given_corners, total)
    for slot in range(2):
        present = jnp.where(table[T_PRESENT + slot] > 0, 1.0, 0.0)
        value = grad_blocks[slot].astype(F32) + total[slot]
        summed[slot] = (value * present).astype(BF16)
    reduce_two.five()
    reduce_one.five()
    reduce_two.end(sums, 1, over)
    reduce_one.end(sums, 0, None)


def settle(scale, fresh, summed, sums, back, next_state, cell_grad, kernel_grads):
    for row in range(fresh.shape[0]):
        next_state[row] = product(back[...], cells(fresh[row])).astype(BF16)
        cell_grad[row] = product(back[...], cells(summed[row])).astype(BF16)
    kernel_grads[...] = sums[...].astype(F32) * scale


def vmem(shape, kind):
    return pltpu.VMEM(shape, kind)


def specs(kinds):
    return [pl.BlockSpec(memory_space=pltpu.SMEM if kind == "s" else pltpu.VMEM) for kind in kinds]


def shape(dims, kind):
    return jax.ShapeDtypeStruct(dims, kind)


TILES = (2, 8, 8, 16, 128)
STRIPS = (8, 8, 16, 128)
CORNERS = (8, 16, 128)
SENT = (6, PART, 16, 128)
NATURAL = (2, 8, 128, 128)


def sum_buffers():
    return [
        vmem((2, HALF, 16, 128), BF16), vmem((HALF, 16, 128), BF16), vmem((HALF, 16, 128), BF16),
        vmem((15, CHUNK, 16, 128), BF16), vmem((8, CHUNK, 16, 128), BF16), vmem((16, CHUNK, 16, 128), BF16),
        vmem((HALF, 16, 128), BF16), vmem((HALF, 16, 128), BF16), vmem((HALF, 16, 128), F32),
    ]


def finished(scale, fresh, summed, sums, back):
    def rows(count, *tail):
        return pl.BlockSpec((count,) + tail, lambda step: (step,) + (0,) * len(tail))

    return pl.pallas_call(
        functools.partial(settle, scale),
        grid=(4,),
        out_shape=[
            shape((16, 128, 128), BF16), shape((16, 128, 128), BF16), shape((2 * UNITS, 16, 128), F32)
        ],
        in_specs=[
            rows(4, 8, 16, 128), rows(4, 8, 16, 128), rows(36, 16, 128),
            pl.BlockSpec((128, 128), lambda step: (0, 0)),
        ],
        out_specs=[rows(4, 128, 128), rows(4, 128, 128), rows(36, 16, 128)],
    )(
        fresh.reshape(16, 8, 16, 128), summed.reshape(16, 8, 16, 128),
        sums.reshape(2 * UNITS, 16, 128), back,
    )


def routed(cell_state, cotangent, kernels, slot_of_tile, neighbours, rotations, corner_flags):
    table = pl.pallas_call(
        plan_kernel,
        out_shape=shape((T_SIZE,), jnp.int32),
        in_specs=specs("ssss"),
        out_specs=specs("s")[0],
        scratch_shapes=[pltpu.SMEM((2 * SPAN,), jnp.int32)],
    )(slot_of_tile, neighbours.T, rotations.T, corner_flags.T)
    scale = 1.0 / math.sqrt(
        cell_state.shape[0] * lax.axis_size("dp") * slot_of_tile.shape[0] * cell_state.shape[2] ** 2
    )
    turns = permutations()
    fresh, summed, sums, over = pl.pallas_call(
        whole,
        out_shape=[
            shape(TILES, BF16), shape(TILES, BF16), shape((2, UNITS, 16, 128), BF16), shape((1,), jnp.int32)
        ],
        in_specs=specs("svvvv"),
        out_specs=specs("vvvs"),
        scratch_shapes=[
            vmem(TILES, BF16), vmem(TILES, BF16), vmem(TILES, BF16),
            vmem(STRIPS, BF16), vmem(CORNERS, BF16), vmem(STRIPS, BF16), vmem(CORNERS, BF16),
            vmem(STRIPS, BF16), vmem(CORNERS, BF16),
        ]
        + [vmem(SENT, BF16)] * 10
        + [
            vmem((2, 1536, 256), BF16), vmem((2, 1536, 256), BF16),
            vmem((2, 12, 12, 16, 128), BF16), vmem((2, 10, 10, 16, 128), F32), vmem(TILES, F32),
            vmem((2, 10, 10, 16, 128), BF16), vmem((2, 10, 10, 16, 128), BF16),
            vmem((10, 20, 16, 128), BF16), vmem((9, 20, 16, 128), BF16),
            vmem((8, 16, 16, 128), F32), vmem((10, 20, 16, 128), BF16), vmem((11, 20, 16, 128), BF16),
            vmem((128, 2048), BF16), vmem((128, 2048), BF16), vmem((512, 1024), BF16),
        ]
        + sum_buffers()
        + sum_buffers()
        + [
            pltpu.SemaphoreType.DMA((5, 2, 6)),
            pltpu.SemaphoreType.DMA((2, 39)),
            pltpu.SemaphoreType.DMA((2, 39)),
        ],
        compiler_params=pltpu.CompilerParams(
            vmem_limit_bytes=VMEM_BYTES, collective_id=1, has_side_effects=True
        ),
    )(
        table, cell_state.reshape(NATURAL), cotangent.reshape(NATURAL), kernels,
        jnp.asarray(turns, BF16),
    )
    back = jnp.asarray(turns[1], BF16)
    arrays = (cell_state, cotangent, kernels, slot_of_tile, neighbours, rotations, corner_flags)

    def fast(*_):
        outs = finished(scale, fresh, summed, sums, back)
        return tuple(out.reshape(like) for out, like in zip(outs, (cell_state.shape, cell_state.shape, kernels.shape)))

    return lax.cond(over[0] == 0, fast, shards, *arrays)


def solution(mesh):
    in_specs = (
        P("dp", "space", None, None, None),
        P("dp", "space", None, None, None),
        P(),
        P(),
        P(),
        P(),
        P(),
    )
    out_specs = (P("dp", "space", None, None, None), P("dp", "space", None, None, None), P())
    return jax.shard_map(routed, mesh=mesh, in_specs=in_specs, out_specs=out_specs, check_vma=False)
```

```python
import functools
import math

import jax
import jax.numpy as jnp
import numpy as np
from jax import lax
from jax.experimental import pallas as pl
from jax.experimental.pallas import tpu as pltpu
from jax.sharding import PartitionSpec as P

RES_BLOCKS = 1
DILATION_ONE = 2
DILATION_TWO = 4
REACH_DEV = 3


CONV_AXES = ("NHWC", "HWIO", "NHWC")


def as_sent(shard):

    def short(part):
        return part.astype(jnp.bfloat16) if part.dtype == jnp.float32 else part

    return jax.tree.map(short, shard)


def shifted(value, axis, steps):
    count = lax.axis_size(axis)
    pairs = [(source, (source + steps) % count) for source in range(count)]
    return lax.ppermute(value, axis, pairs)


def boundary(tile_data, rim_depth):
    extent = tile_data.shape[3]
    far = extent - rim_depth
    sides = [
        tile_data[:, :, :rim_depth],
        tile_data[:, :, :, far:],
        tile_data[:, :, far:],
        tile_data[:, :, :, :rim_depth],
    ]
    blocks = [
        tile_data[:, :, :rim_depth, far:],
        tile_data[:, :, far:, far:],
        tile_data[:, :, far:, :rim_depth],
        tile_data[:, :, :rim_depth, :rim_depth],
    ]
    strips = jnp.stack(
        [jnp.rot90(sides[quarter], quarter, axes=(2, 3)) for quarter in range(4)], axis=2
    )
    corners = jnp.stack(
        [jnp.rot90(blocks[quarter], quarter, axes=(2, 3))[:, :, :, ::-1] for quarter in range(4)],
        axis=2,
    )
    return (strips, corners)


def assemble(tile_data, strips, corners):
    edge_parts = [
        jnp.rot90(strips[:, :, quarter, ::-1, ::-1], -quarter, axes=(2, 3)) for quarter in range(4)
    ]
    corner_parts = [
        jnp.rot90(corners[:, :, quarter, ::-1], -quarter, axes=(2, 3)) for quarter in range(4)
    ]
    top_row = jnp.concatenate([corner_parts[3], edge_parts[0], corner_parts[0]], axis=3)
    middle = jnp.concatenate([edge_parts[3], tile_data, edge_parts[1]], axis=3)
    bottom = jnp.concatenate([corner_parts[2], edge_parts[2], corner_parts[1]], axis=3)
    return jnp.concatenate([top_row, middle, bottom], axis=2)


def rim_pieces(tile_data, rim_depth):
    strips, corners = boundary(tile_data, rim_depth)
    joined = jnp.concatenate([strips, corners], axis=4)
    return joined.reshape((joined.shape[0], joined.shape[1] * 4) + joined.shape[3:])


def conv_apply(padded, kernel, spread):
    merged = padded.reshape((-1,) + padded.shape[2:])
    result = lax.conv_general_dilated(
        merged,
        kernel,
        (1, 1),
        "VALID",
        rhs_dilation=(spread, spread),
        dimension_numbers=CONV_AXES,
        preferred_element_type=jnp.float32,
    )
    return result.reshape(padded.shape[:2] + result.shape[1:])


def conv_back(grad_out, kernel, spread):
    merged = grad_out.reshape((-1,) + grad_out.shape[2:])
    flipped = jnp.swapaxes(kernel[::-1, ::-1], 2, 3)
    margin = 2 * spread
    result = lax.conv_general_dilated(
        merged,
        flipped,
        (1, 1),
        ((margin, margin), (margin, margin)),
        rhs_dilation=(spread, spread),
        dimension_numbers=CONV_AXES,
        preferred_element_type=jnp.float32,
    )
    return result.reshape(grad_out.shape[:2] + result.shape[1:])


def kernel_grad(padded, grad_out, spread):
    extent = grad_out.shape[2]
    tap_terms = []
    for row_tap in range(3):
        for col_tap in range(3):
            window = padded[
                :,
                :,
                row_tap * spread : row_tap * spread + extent,
                col_tap * spread : col_tap * spread + extent,
            ]
            tap_terms.append(
                lax.dot_general(
                    window,
                    grad_out,
                    (((0, 1, 2, 3), (0, 1, 2, 3)), ((), ())),
                    preferred_element_type=jnp.float32,
                )
            )
    stacked = jnp.stack(tap_terms)
    return stacked.reshape((3, 3) + stacked.shape[1:])


def halo_plan(slot_of_tile, neighbours, rotations, corner_flags, slot_count):
    span_count = lax.axis_size("space")
    myself = lax.axis_index("space")
    tile_count = slot_of_tile.shape[0]
    owned = myself * slot_count + jnp.arange(slot_count, dtype=jnp.int32)
    matches = slot_of_tile[None, :] == owned[:, None]
    present = jnp.any(matches, axis=1)
    tile_here = jnp.sum(
        jnp.where(matches, jnp.arange(tile_count, dtype=jnp.int32)[None, :], 0), axis=1
    )
    nearby = jnp.take(neighbours, tile_here, axis=0)
    turn_code = jnp.take(rotations, tile_here, axis=0)
    facing = (jnp.arange(8, dtype=jnp.int32)[None, :] % 4 + 2 + turn_code) % 4
    source = jnp.take(slot_of_tile, nearby)
    holder = source // slot_count
    within = source % slot_count
    offset = jnp.clip(
        (myself - holder + span_count + REACH_DEV) % span_count - REACH_DEV, -REACH_DEV, REACH_DEV
    )
    select = ((offset + REACH_DEV) * slot_count + within) * 4 + facing
    keep_corner = jnp.take(corner_flags, tile_here, axis=0) == 0
    return (select[:, :4].reshape(-1), select[:, 4:].reshape(-1), keep_corner.reshape(-1), present)


def fetch_near(bundle):
    arrived = {0: bundle}
    for offset in list(range(-REACH_DEV, 0)) + list(range(1, REACH_DEV + 1)):
        arrived[offset] = shifted(as_sent(bundle), "space", offset).astype(bundle.dtype)
    return [arrived[offset] for offset in range(-REACH_DEV, REACH_DEV + 1)]


def return_near(parts):
    total = parts[0]
    for offset in list(range(-REACH_DEV, 0)) + list(range(1, REACH_DEV + 1)):
        total = total + shifted(parts[offset].astype(jnp.bfloat16), "space", -offset).astype(
            jnp.float32
        )
    return total


def halo_forward(tile_data, rim_depth, plan):
    pick_edge, pick_corner, keep_corner = plan[:3]
    samples_here, slot_count, extent = (tile_data.shape[0], tile_data.shape[1], tile_data.shape[2])
    channels = tile_data.shape[4]
    gathered = jnp.concatenate(fetch_near(rim_pieces(tile_data, rim_depth)), axis=1)
    edge_part = jnp.take(gathered, pick_edge, axis=1)[:, :, :, :extent]
    corner_part = jnp.take(gathered, pick_corner, axis=1)[:, :, :, extent:]
    corner_part = jnp.where(
        keep_corner[None, :, None, None, None], corner_part, jnp.zeros((), corner_part.dtype)
    )
    strips = edge_part.reshape(samples_here, slot_count, 4, rim_depth, extent, channels)
    corners = corner_part.reshape(samples_here, slot_count, 4, rim_depth, rim_depth, channels)
    return assemble(tile_data, strips, corners)


def halo_backward(grad_wide, rim_depth, plan):
    pick_edge, pick_corner, keep_corner = plan[:3]
    samples_here, slot_count = (grad_wide.shape[0], grad_wide.shape[1])
    extent = grad_wide.shape[2] - 2 * rim_depth
    channels = grad_wide.shape[4]
    tile_zero = jnp.zeros((samples_here, slot_count, extent, extent, channels), jnp.float32)
    strip_zero = jnp.zeros((samples_here, slot_count, 4, rim_depth, extent, channels), jnp.float32)
    corner_zero = jnp.zeros(
        (samples_here, slot_count, 4, rim_depth, rim_depth, channels), jnp.float32
    )
    _, assemble_back = jax.vjp(assemble, tile_zero, strip_zero, corner_zero)
    grad_tiles, grad_strips, grad_corners = assemble_back(grad_wide)
    pieces = slot_count * 4
    grad_corners = grad_corners.reshape(samples_here, pieces, rim_depth, rim_depth, channels)
    grad_corners = jnp.where(keep_corner[None, :, None, None, None], grad_corners, 0.0)
    spread_out = jnp.zeros(
        (samples_here, (2 * REACH_DEV + 1) * pieces, rim_depth, extent + rim_depth, channels),
        jnp.float32,
    )
    spread_out = spread_out.at[:, pick_edge, :, :extent].add(
        grad_strips.reshape(samples_here, pieces, rim_depth, extent, channels)
    )
    spread_out = spread_out.at[:, pick_corner, :, extent:].add(grad_corners)
    parts = {
        offset: spread_out[:, (offset + REACH_DEV) * pieces : (offset + REACH_DEV + 1) * pieces]
        for offset in range(-REACH_DEV, REACH_DEV + 1)
    }
    returned = return_near(parts)
    _, rim_back = jax.vjp(lambda tile_part: rim_pieces(tile_part, rim_depth), tile_zero)
    return grad_tiles + rim_back(returned)[0]


def sum_over(value, axis):
    count = lax.axis_size(axis)
    step = 1
    while step < count:
        pairs = [(source, source ^ step) for source in range(count)]
        value = value + lax.ppermute(value, axis, pairs)
        step *= 2
    return value


def shards(cell_state, cotangent, kernels, slot_of_tile, neighbours, rotations, corner_flags):
    plan = halo_plan(slot_of_tile, neighbours, rotations, corner_flags, cell_state.shape[1])
    keep_slot = plan[3][None, :, None, None, None]
    current = cell_state
    block_at = 0
    widened = halo_forward(current, DILATION_ONE, plan)
    before = conv_apply(widened, kernels[2 * block_at], DILATION_ONE)
    hidden = jax.nn.gelu(before).astype(jnp.bfloat16)
    widened_two = halo_forward(hidden, DILATION_TWO, plan)
    branch = conv_apply(widened_two, kernels[2 * block_at + 1], DILATION_TWO)
    stored = [(widened, before, widened_two)]
    current = (current.astype(jnp.float32) + branch).astype(jnp.bfloat16)
    next_state = jnp.where(keep_slot, current, jnp.zeros((), jnp.bfloat16))
    gradient = jnp.where(keep_slot, cotangent, jnp.zeros((), jnp.bfloat16))
    kernel_terms = [None] * (2 * RES_BLOCKS)
    extent = cell_state.shape[2]
    norm_scale = 1.0 / math.sqrt(
        cell_state.shape[0] * lax.axis_size("dp") * slot_of_tile.shape[0] * extent * extent
    )
    for block_at in reversed(range(RES_BLOCKS)):
        widened, before, widened_two = stored[block_at]
        outer_term = kernel_grad(widened_two, gradient, DILATION_TWO)
        kernel_terms[2 * block_at + 1] = outer_term
        grad_hidden = halo_backward(
            conv_back(gradient, kernels[2 * block_at + 1], DILATION_TWO), DILATION_TWO, plan
        ).astype(jnp.bfloat16)
        _, gelu_back = jax.vjp(jax.nn.gelu, before)
        grad_before = gelu_back(grad_hidden.astype(jnp.float32))[0].astype(jnp.bfloat16)
        inner_term = kernel_grad(widened, grad_before, DILATION_ONE)
        kernel_terms[2 * block_at] = inner_term
        returned = halo_backward(
            conv_back(grad_before, kernels[2 * block_at], DILATION_ONE), DILATION_ONE, plan
        )
        gradient = (gradient.astype(jnp.float32) + returned).astype(jnp.bfloat16)
    stacked = jnp.stack(kernel_terms)
    stacked = sum_over(sum_over(stacked, "space"), "dp")
    return (next_state, gradient, stacked * norm_scale)


MESH_ID = pl.DeviceIdType.MESH
SPAN = 128
STRIP_SLOTS = (1, 2, 2, 2, 2, 1)
CORNER_CAP = 3
PART = CORNER_CAP + 16
THIN = 9
OFFSETS = (-3, -2, -1, 1, 2, 3)
ORDER = (2, 3, 1, 4, 0, 5)
SELF = 6
NOT_THERE = 32
T_STRIP_LIST, T_CORNER_LIST, T_GIVE_STRIP, T_GIVE_CORNER = 0, 12, 36, 48
T_ADD, T_PIECES, T_PRESENT = 72, 104, 200
T_OVER, T_SPARE, T_SIZE = 202, 203, 208
VMEM_BYTES = 56 * 1024 * 1024
F32 = jnp.float32
BF16 = jnp.bfloat16


def cell_order():
    rows, cols = np.meshgrid(np.arange(4), np.arange(4), indexing="ij")
    return ((cols // 2) * 8 + (rows // 2) * 4 + (rows % 2) * 2 + cols % 2).astype(np.int64)


def permutations():
    order = cell_order()
    to_blocks = np.zeros((128, 128), np.float32)
    for row in range(4):
        for col in range(32):
            to_blocks[(col // 4) * 16 + order[row, col % 4], row * 32 + col] = 1
    mats = [to_blocks, to_blocks.T]
    for turn in range(4):
        turned = np.rot90(order, turn)
        small = np.zeros((16, 16), np.float32)
        small[order.reshape(-1), turned.reshape(-1)] = 1
        for flip in range(2):
            line = np.eye(8)[::-1] if flip else np.eye(8)
            mats.append(np.kron(line, small))
    return np.stack(mats)


def turn_matrix(turn, flip):
    return 2 + 2 * turn + flip


def flips(edge, turn):
    side = (edge + 2 + turn) & 1
    once = jnp.where((turn == 1) & (side == 0), 1, 0)
    thrice = jnp.where((turn == 3) & (side == 1), 1, 0)
    return jnp.where(turn == 2, 1, once + thrice)


def packings():
    order = cell_order()
    mats = permutations()
    inner = (order[:2], order[:, 2:], order[2:], order[:, :2])
    ends = (order[:2, 2:], order[2:, 2:], order[2:, :2], order[:2, :2])
    pack = np.zeros((4, 64, 128), np.float32)
    pack_corners = np.zeros((128, 128), np.float32)
    for side in range(4):
        for block in range(8):
            for at, cell in enumerate(sorted(inner[side].reshape(-1))):
                pack[side, block * 8 + at, block * 16 + cell] = 1
        for at, cell in enumerate(sorted(ends[side].reshape(-1))):
            for slot in range(2):
                for copy in range(4):
                    base = (slot * 4 + side) * 16
                    pack_corners[base + copy * 4 + at, base + cell] = 1
    unpack = np.zeros((16, 128, 64), np.float32)
    unpack_corners = np.zeros((16, 16, 128), np.float32)
    for turn in range(4):
        for edge in range(4):
            side = (edge + 2 + turn) % 4
            flip = int(turn == 2 or (turn == 1 and side % 2 == 0) or (turn == 3 and side % 2 == 1))
            unpack[turn * 4 + edge] = mats[2 + 2 * turn + flip] @ pack[side].T
            four = pack_corners[side * 16 : side * 16 + 4, side * 16 : side * 16 + 16]
            small = mats[2 + 2 * turn][:16, :16] @ four.T
            unpack_corners[turn * 4 + edge] = np.tile(small, (1, 32))
    return pack, pack_corners, unpack, unpack_corners


def plan_kernel(slot_ref, near_ref, turn_ref, flag_ref, table, tile_at):
    me = lax.axis_index("space")
    for entry in range(T_SIZE):
        table[entry] = 0
    for entry in range(8):
        table[T_ADD + entry] = NOT_THERE
        table[T_ADD + 16 + entry] = NOT_THERE
    for rel in range(14):
        tile_at[(me + rel // 2 - 3 + SPAN) % SPAN * 2 + rel % 2] = -1

    def place(step, carry):
        for inner in range(16):
            tile = step * 16 + inner
            tile_at[slot_ref[tile]] = tile
        return carry

    lax.fori_loop(0, slot_ref.shape[0] // 16, place, 0)
    over = jnp.int32(0)
    core = me % 2

    def contribute(hit, kind, entry, code, turn):
        place_at = jnp.where(hit, T_ADD + kind * 16 + entry, T_SPARE)
        taken = jnp.where(hit & (table[place_at] != NOT_THERE), 1, 0)
        table[place_at] = code
        table[place_at + jnp.where(hit, 8, 0)] = jnp.where(hit, turn, code)
        return taken

    for where, offset in enumerate(OFFSETS):
        seen = [jnp.int32(0), jnp.int32(0)]
        for slot in range(2):
            tile = tile_at[(me + offset + SPAN) % SPAN * 2 + slot]
            row = jnp.maximum(tile, 0)
            for piece in range(8):
                kind = piece // 4
                source = slot_ref[near_ref[piece, row]]
                hit = (tile >= 0) & (source // 2 == me)
                turn = turn_ref[piece, row] & 3
                entry = source % 2 * 4 + ((piece + 2 + turn) & 3)
                cap = CORNER_CAP if kind else (1, 2, 1 + core, 2 - core, 2, 1)[where]
                rank = jnp.minimum(seen[kind], cap - 1)
                if offset in (-3, 3):
                    over = over + jnp.where(hit & (core == (0 if offset < 0 else 1)), 1, 0)
                over = over + jnp.where(hit & (seen[kind] >= cap), 1, 0)
                seen[kind] = seen[kind] + jnp.where(hit, 1, 0)
                width = 4 if kind else 2
                place_at = (T_CORNER_LIST if kind else T_STRIP_LIST) + where * width + rank
                table[jnp.where(hit, place_at, T_SPARE)] = entry
                over = over + contribute(hit, kind, entry, where * width + rank, turn)
    seen = [[jnp.int32(0)] * 7, [jnp.int32(0)] * 7]
    for slot in range(2):
        tile = tile_at[me * 2 + slot]
        row = jnp.maximum(tile, 0)
        valid = jnp.where(tile >= 0, 1, 0)
        table[T_PRESENT + slot] = valid
        for piece in range(8):
            kind = piece // 4
            source = slot_ref[near_ref[piece, row]]
            turn = turn_ref[piece, row] & 3
            offset = jnp.clip((source // 2 - me + 3 + SPAN) % SPAN, 0, 6)
            where = jnp.where(offset == 3, SELF, jnp.where(offset < 3, offset, offset - 1))
            rank = jnp.int32(0)
            for choice in range(7):
                match = jnp.where(offset == choice, valid, 0)
                rank = rank + match * seen[kind][choice]
                seen[kind][choice] = seen[kind][choice] + match
            rank = jnp.minimum(rank, CORNER_CAP - 1 if kind else 1)
            keep = valid
            if kind:
                keep = valid * jnp.where(flag_ref[piece - 4, row] == 0, 1, 0)
            entry = source % 2 * 4 + ((piece + 2 + turn) & 3)
            base = T_PIECES + (slot * 8 + piece) * 6
            table[base] = valid
            table[base + 1] = where
            table[base + 2] = rank
            table[base + 3] = turn
            table[base + 4] = entry
            table[base + 5] = keep
            mine = slot * 4 + piece % 4
            own = (valid > 0) & (where == SELF)
            away = (valid > 0) & (where != SELF)
            place_at = (T_GIVE_CORNER if kind else T_GIVE_STRIP) + where * (4 if kind else 2) + rank
            table[jnp.where(away, place_at, T_SPARE)] = mine
            over = over + contribute(own, kind, entry, (24 if kind else 12) + mine, turn)
    table[T_OVER] = over


def piece_of(table, slot, piece):
    base = T_PIECES + (slot * 8 + piece) * 6
    return [table[base + field] for field in range(6)]


def blocks(value):
    return value.reshape((-1, 16, 128))


def cells(value):
    return value.reshape((-1, 128))


def product(left, right):
    return jnp.dot(left, right, preferred_element_type=F32)


EDGE_OF = ((0, slice(None)), (slice(None), 7), (7, slice(None)), (slice(None), 0))
CORNER_OF = ((0, 7), (7, 7), (7, 0), (0, 0))
BAND_OF = ((0, slice(1, 9)), (slice(1, 9), 9), (9, slice(1, 9)), (slice(1, 9), 0))
BLOCK_OF = ((0, 9), (9, 9), (9, 0), (0, 0))


def take_rims(tile_ref, strips, corners):
    for slot in range(2):
        for side in range(4):
            strips[slot * 4 + side] = blocks(tile_ref[(slot,) + EDGE_OF[side]])
            corners[slot * 4 + side] = tile_ref[(slot,) + CORNER_OF[side]]


def send_rims(table, strips, corners, send, strip_list=T_STRIP_LIST, corner_list=T_CORNER_LIST):
    for where in range(6):
        for rank in range(STRIP_SLOTS[where]):
            at = CORNER_CAP + rank * 8
            send[where, at : at + 8] = strips[table[strip_list + where * 2 + rank]]
        for rank in range(CORNER_CAP):
            send[where, rank] = corners[table[corner_list + where * 4 + rank]]


def send_thin(table, strips, corners, send):
    group = lax.broadcasted_iota(jnp.int32, (16, 128), 0) // 4
    for where in range(6):
        for rank in range(STRIP_SLOTS[where]):
            send[where, 1 + rank * 4 : 5 + rank * 4] = strips[table[T_STRIP_LIST + where * 2 + rank]]
        unit = corners[table[T_CORNER_LIST + where * 4]]
        for rank in range(1, CORNER_CAP):
            unit = jnp.where(group == rank, corners[table[T_CORNER_LIST + where * 4 + rank]], unit)
        send[where, 0] = unit.astype(BF16)


def thin_rims(strips, corners, pack, pack_corners, thin_strips, thin_corners):
    for entry in range(8):
        packed = product(pack[entry % 4], cells(strips[entry]))
        thin_strips[entry] = blocks(packed.astype(BF16))
    thin_corners[...] = blocks(product(pack_corners[...], cells(corners[...])))


def corner_turns(table, turns, back):
    parts = []
    for slot in range(2):
        for side in range(4):
            fields = piece_of(table, slot, 4 + side)
            turn = (4 - fields[3]) & 3 if back else fields[3]
            rows = turns[turn_matrix(turn, 0)]
            at = (slot * 4 + side) * 16
            parts.append(rows[at : at + 16] * jnp.where(fields[5] > 0, 1.0, 0.0).astype(BF16))
    return jnp.concatenate(parts, axis=0)


def widen(table, tile_ref, strips, corners, arrived, turns, padded):
    for slot in range(2):
        padded[slot, 1:9, 1:9] = tile_ref[slot]
        for edge in range(4):
            valid, where, rank, turn, entry, keep = piece_of(table, slot, edge)
            own = strips[entry]
            other = arrived[jnp.minimum(where, 5), pl.ds(CORNER_CAP + rank * 8, 8)]
            strip = jnp.where(where == SELF, own, other)
            strip = jnp.where(valid > 0, strip, jnp.zeros_like(strip))
            turned = product(turns[turn_matrix(turn, flips(edge, turn))], cells(strip))
            padded[(slot,) + BAND_OF[edge]] = blocks(turned.astype(BF16))
    stack = []
    for slot in range(2):
        for side in range(4):
            valid, where, rank, turn, entry, keep = piece_of(table, slot, 4 + side)
            block = jnp.where(where == SELF, corners[entry], arrived[jnp.minimum(where, 5), rank])
            stack.append(jnp.where(valid > 0, block, jnp.zeros_like(block)))
    turned = product(corner_turns(table, turns, False), jnp.concatenate(stack, axis=0))
    turned = blocks(turned.astype(BF16))
    for slot in range(2):
        for side in range(4):
            padded[(slot,) + BLOCK_OF[side]] = turned[slot * 4 + side]


def give_back(table, wide, turns, send, strips, corners):
    for slot in range(2):
        for edge in range(4):
            valid, where, rank, turn, entry, keep = piece_of(table, slot, edge)
            band = cells(blocks(wide[(slot,) + BAND_OF[edge]])).astype(BF16)
            turned = product(turns[turn_matrix((4 - turn) & 3, flips(edge, turn))], band)
            strips[slot * 4 + edge] = blocks(turned.astype(BF16))
    stack = [wide[(slot,) + BLOCK_OF[side]].astype(BF16) for slot in range(2) for side in range(4)]
    turned = product(corner_turns(table, turns, True), jnp.concatenate(stack, axis=0))
    corners[...] = blocks(turned.astype(BF16))
    send_rims(table, strips, corners, send, T_GIVE_STRIP, T_GIVE_CORNER)


def widen_thin(table, thin_strips, thin_corners, arrived, unpack, unpack_corners, padded):
    for slot in range(2):
        for edge in range(4):
            valid, where, rank, turn, entry, keep = piece_of(table, slot, edge)
            other = arrived[jnp.minimum(where, 5), pl.ds(1 + rank * 4, 4)]
            strip = jnp.where(where == SELF, thin_strips[entry], other)
            strip = jnp.where(valid > 0, strip, jnp.zeros_like(strip))
            turned = product(unpack[turn * 4 + edge], cells(strip))
            padded[(slot,) + BAND_OF[edge]] = blocks(turned.astype(BF16))
    lane = lax.broadcasted_iota(jnp.int32, (16, 128), 1)
    stack, parts = [], []
    for slot in range(2):
        for side in range(4):
            valid, where, rank, turn, entry, keep = piece_of(table, slot, 4 + side)
            block = jnp.where(where == SELF, thin_corners[entry], arrived[jnp.minimum(where, 5), 0].astype(F32))
            stack.append(jnp.where(valid > 0, block, jnp.zeros_like(block)).astype(BF16))
            first = (slot * 4 + side) * 16 + jnp.where(where == SELF, 0, rank) * 4
            chosen = (lane >= first) & (lane < first + 4) & (keep > 0)
            rows = unpack_corners[turn * 4 + side].astype(F32)
            parts.append(jnp.where(chosen, rows, jnp.zeros_like(rows)).astype(BF16))
    turned = product(jnp.concatenate(parts, axis=0), jnp.concatenate(stack, axis=0))
    turned = blocks(turned.astype(BF16))
    for slot in range(2):
        for side in range(4):
            padded[(slot,) + BLOCK_OF[side]] = turned[slot * 4 + side]


def owner_of(table, kind, entry):
    code = table[T_ADD + kind * 16 + entry]
    turn = table[T_ADD + kind * 16 + 8 + entry]
    return code, turn, (entry % 4 - 2 - turn) & 3


def copied_strip(code, arrived, strips):
    far = jnp.minimum(code, 11)
    near = jnp.clip(code - 12, 0, 7)
    part = jnp.where(code < 12, arrived[far // 2, pl.ds(CORNER_CAP + far % 2 * 8, 8)], strips[near])
    return jnp.where(code == NOT_THERE, jnp.zeros_like(part), part)


def copied_corner(code, arrived, corners):
    far = jnp.minimum(code, 23)
    near = jnp.clip(code - 24, 0, 7)
    part = jnp.where(code < 24, arrived[far // 4, far % 4], corners[near])
    return jnp.where(code == NOT_THERE, jnp.zeros_like(part), part)


def take_back(table, arrived, strips, corners, total):
    for slot in range(2):
        for side in range(4):
            at = (slot,) + EDGE_OF[side]
            code = owner_of(table, 0, slot * 4 + side)[0]
            total[at] = total[at] + copied_strip(code, arrived, strips).astype(F32)
    for slot in range(2):
        for side in range(4):
            at = (slot,) + CORNER_OF[side]
            code = owner_of(table, 1, slot * 4 + side)[0]
            total[at] = total[at] + copied_corner(code, arrived, corners).astype(F32)


STRIP_TAPS = (
    ((0, 0), (0, 1), (0, 2)),
    ((0, 2), (1, 2), (2, 2)),
    ((2, 0), (2, 1), (2, 2)),
    ((0, 0), (1, 0), (2, 0)),
)
CORNER_TAPS = ((0, 2), (2, 2), (2, 0), (0, 0))


def rim_terms(table, arrived, given_strips, given_corners, strips, corners, turns, masked):
    rims = []
    for entry in range(8):
        code, turn, edge = owner_of(table, 0, entry)
        grad = cells(copied_strip(code, arrived, given_strips)).T
        for choice in range(4):
            chosen = jnp.where(edge == choice, grad, jnp.zeros_like(grad))
            masked[choice * 128 : choice * 128 + 128, entry * 128 : entry * 128 + 128] = chosen
        band = product(turns[turn_matrix(turn, flips(edge, turn))], cells(strips[entry])).astype(BF16)
        blank = jnp.zeros((16, 128), BF16)
        longer = jnp.concatenate([blank, band, blank], axis=0)
        rims.append(jnp.concatenate([longer[step * 16 : step * 16 + 128] for step in range(3)], axis=1))
    edges = product(masked[...], jnp.concatenate(rims, axis=0))
    lane = lax.broadcasted_iota(jnp.int32, (128, 128), 1) // 16
    which = jnp.zeros((128, 128), jnp.int32)
    grads, parts = [], []
    for entry in range(8):
        code, turn, side = owner_of(table, 1, entry)
        grads.append(copied_corner(code, arrived, given_corners))
        which = jnp.where(lane == entry, side, which)
        parts.append(turns[turn_matrix(turn, 0)][entry * 16 : entry * 16 + 16])
    block = product(jnp.concatenate(parts, axis=0), cells(corners[...])).astype(BF16)
    grad = jnp.concatenate(grads, axis=0).astype(F32).T
    spread = [jnp.where(which == choice, grad, jnp.zeros_like(grad)) for choice in range(4)]
    ends = product(jnp.concatenate(spread, axis=0).astype(BF16), block)
    sums = [None] * 9
    for choice in range(4):
        rows = slice(choice * 128, choice * 128 + 128)
        found = [(tap, edges[rows, step * 128 : step * 128 + 128]) for step, tap in enumerate(STRIP_TAPS[choice])]
        found.append((CORNER_TAPS[choice], ends[rows]))
        for (up, across), value in found:
            old = sums[up * 3 + across]
            sums[up * 3 + across] = value if old is None else old + value
    return sums


def halves(value):
    return value.astype(F32).reshape(value.shape[0], value.shape[1] * 2, 8, 128)


def shifted_up(upper, lower):
    low = lax.broadcasted_iota(jnp.int32, upper.shape, upper.ndim - 2) < 4
    mixed = jnp.where(low, lower, upper)
    return jnp.concatenate([mixed[..., 4:, :], mixed[..., :4, :]], axis=mixed.ndim - 2)


def gelu_parts(value):
    root = math.sqrt(2.0 / math.pi)
    square = value * value
    bent = jnp.tanh(root * (value + 0.044715 * (value * square)))
    half = 0.5 * (1.0 + bent)
    slope = half + 0.5 * value * (1.0 - bent * bent) * (root * (1.0 + 3 * 0.044715 * square))
    return (value * half, slope)


UNITS = 72
HALF = 37
CHUNK = 3


def chunk_start(index):
    return (index * (HALF - CHUNK)) // 15


class Swap:
    def __init__(self, me, send, arrived, sems, corner_units=CORNER_CAP, strip_units=8):
        core = me % 2
        far, mate, other = 5 - 5 * core, 3 - core, 2 + core
        self.copies = []
        for where, offset, strips, send_at, recv_at in (
            (other, 2 * core - 1, 1, 2, 2),
            (1, -2, 2, 1, 4),
            (4, 2, 2, 4, 1),
            (far, 3 - 6 * core, 1, 0, 0),
            (mate, 1 - 2 * core, 2, 3, 3),
        ):
            size = corner_units + strip_units * strips
            self.copies.append(
                pltpu.make_async_remote_copy(
                    src_ref=send.at[where, pl.ds(0, size)],
                    dst_ref=arrived.at[5 - where, pl.ds(0, size)],
                    send_sem=sems.at[0, send_at],
                    recv_sem=sems.at[1, recv_at],
                    device_id={"space": lax.rem(me + offset + SPAN, SPAN)},
                    device_id_type=MESH_ID,
                )
            )

    def start(self):
        for copy in self.copies:
            copy.start()

    def wait(self):
        for copy in self.copies:
            copy.wait()


class Place:
    def __init__(self):
        me = lax.axis_index("space")
        self.me = me
        self.core, self.y, self.z, self.x_lo = me % 2, me // 2 % 4, me // 8 % 8, me // 64
        self.plane = (lax.axis_index("dp") * 2 + self.x_lo) * 4 + self.y
        self.mate = {"space": me + 1 - 2 * self.core}

    def at_plane(self, index):
        return {
            "dp": index // 8,
            "space": ((index // 4 % 2) * 8 + self.z) * 8 + index % 4 * 2 + self.core,
        }

    def at_line(self, index):
        return {"space": (self.x_lo * 8 + index) * 8 + self.y * 2 + self.core}


class Sum:
    def __init__(self, place, buffers, sems):
        self.place = place
        self.half_send, self.half_in, self.plane_send, self.plane_in, self.line_in = buffers[:5]
        self.wide_in, self.pair_send, self.pair_in, self.acc = buffers[5:]
        self.sems = sems
        self.copies = []

    def copy(self, source, target, index, where):
        one = pltpu.make_async_remote_copy(
            src_ref=source,
            dst_ref=target,
            send_sem=self.sems.at[0, index],
            recv_sem=self.sems.at[1, index],
            device_id=where,
            device_id_type=MESH_ID,
        )
        one.start()
        self.copies.append(one)

    def put(self, terms):
        for tap, term in enumerate(terms):
            value = blocks(term.astype(BF16))
            for part in range(2):
                half, at = divmod(tap * 8 + part * 4, 36)
                self.half_send[half, at : at + 4] = value[part * 4 : part * 4 + 4]

    def wait(self):
        for one in self.copies:
            one.wait()
        self.copies = []

    def one(self):
        place = self.place
        self.copy(self.half_send.at[1 - place.core], self.half_in, 0, place.mate)

    def two(self):
        place = self.place
        self.wait()
        self.acc[...] = self.half_send[place.core].astype(F32) + self.half_in[...].astype(F32)
        self.plane_send[...] = self.acc[...].astype(BF16)
        for step in range(1, 16):
            peer = lax.rem(place.plane + step, 16)
            source = self.plane_send.at[pl.ds(chunk_start(peer), CHUNK)]
            self.copy(source, self.plane_in.at[step - 1], step, place.at_plane(peer))

    def three(self):
        place = self.place
        self.wait()
        total = self.acc[pl.ds(chunk_start(place.plane), CHUNK)]
        for step in range(15):
            total = total + self.plane_in[step].astype(F32)
        self.line_in[place.z] = total.astype(BF16)
        for step in range(1, 8):
            peer = lax.rem(place.z + step, 8)
            self.copy(self.line_in.at[place.z], self.line_in.at[place.z], 15 + step, place.at_line(peer))

    def four(self):
        place = self.place
        self.wait()
        total = self.line_in[0].astype(F32)
        for index in range(1, 8):
            total = total + self.line_in[index].astype(F32)
        self.wide_in[place.plane] = total.astype(BF16)
        for step in range(1, 16):
            peer = lax.rem(place.plane + step, 16)
            here = self.wide_in.at[place.plane]
            self.copy(here, here, 22 + step, place.at_plane(peer))

    def five(self):
        self.wait()
        for index in range(16):
            at = chunk_start(index)
            self.pair_send[at : at + CHUNK] = self.wide_in[index]
        self.copy(self.pair_send, self.pair_in, 38, self.place.mate)

    def end(self, out, layer, over):
        self.wait()
        core = self.place.core
        mine, other = self.pair_send[...], self.pair_in[...]
        out[layer, :36] = jnp.where(core == 0, mine[:36], other[:36])
        out[layer, 36:] = jnp.where(core == 0, other[:36], mine[:36])
        if over is not None:
            over[0] = jnp.where(jnp.max(mine[36].astype(F32)) > 0.0, 1, 0)


def columns(value, first, count):
    rows, wide = value.shape[:2]
    paired = value.reshape(rows, wide // 2, 2, 16, 128)
    return [
        cells(paired[:, (first + step) // 2 : (first + step) // 2 + count, (first + step) % 2])
        for step in range(4)
    ]


def split_pairs(result, rows, count):
    wide = result.reshape(rows, count, 16, 256)
    return jnp.stack([wide[..., :128], wide[..., 128:]], axis=2).reshape(rows, count * 2, 16, 128)


def paired_conv(sources, first, count, weight):
    taps = [tap for value in sources for tap in columns(value, first, count)]
    result = product(jnp.concatenate(taps, axis=1), weight)
    return split_pairs(result, sources[0].shape[0], count)


def gradient_terms(turned, windows, extra=None):
    total = None
    for at, taps in windows:
        part = product(turned[:, at : at + taps[0].shape[0]], jnp.concatenate(taps, axis=1))
        total = part if total is None else total + part
    terms = [total[:, tap * 128 : tap * 128 + 128] for tap in range(9)]
    if extra is not None:
        terms = [term if more is None else term + more for term, more in zip(terms, extra)]
    return [term.T for term in terms]


def whole(
    table, state_far, cotangent_far, kernels_far, turns_far, pack, pack_corners, unpack, unpack_corners,
    fresh, summed, sums, over,
    state, cotangent, kernels, turns, load_sems, thin_strips, thin_corners, state_blocks, grad_blocks, hidden_blocks, strips, corners, given_strips, given_corners,
    grad_strips, grad_corners,
    send_a, send_b, send_c, send_d, send_e, in_a, in_b, in_c, in_d, in_e,
    forward, flipped, grad_wide, wide, total, padded, widened, even, odd, slope, grad_even, grad_odd,
    turned_one, turned_two, masked, *rest,
):
    swap_sems, one_sems, two_sems = rest[18:]
    loads = []
    pairs = ((turns_far, turns), (state_far, state), (cotangent_far, cotangent), (kernels_far, kernels))
    for index, (source, target) in enumerate(pairs):
        loads.append(pltpu.make_async_copy(source, target, load_sems.at[index]))
        loads[index].start()
    place = Place()
    me = place.me
    barrier = pltpu.get_barrier_semaphore()

    def greet(where):
        pl.semaphore_signal(barrier, inc=1, device_id=where, device_id_type=MESH_ID)

    for offset in OFFSETS:
        greet({"space": lax.rem(me + offset + SPAN, SPAN)})
    greet(place.mate)
    for step in range(1, 16):
        greet(place.at_plane(lax.rem(place.plane + step, 16)))
    for step in range(1, 8):
        greet(place.at_line(lax.rem(place.z + step, 8)))

    rims_one = Swap(me, send_a, in_a, swap_sems.at[0], 1, 4)
    back_two = Swap(me, send_b, in_b, swap_sems.at[1])
    rims_two = Swap(me, send_c, in_c, swap_sems.at[2])
    back_one = Swap(me, send_d, in_d, swap_sems.at[3])
    rims_grad = Swap(me, send_e, in_e, swap_sems.at[4])
    reduce_one = Sum(place, rest[:9], one_sems)
    reduce_two = Sum(place, rest[9:18], two_sems)

    loads[0].wait()
    loads[1].wait()
    for slot in range(2):
        for row in range(8):
            moved = product(turns[0], state[slot, row])
            state_blocks[slot, row] = blocks(moved.astype(BF16))
    take_rims(state_blocks, strips, corners)
    thin_rims(strips, corners, pack, pack_corners, thin_strips, thin_corners)
    send_thin(table, thin_strips, thin_corners, send_a)
    pl.semaphore_wait(barrier, 29)
    rims_one.start()

    grad_wide[...] = jnp.zeros_like(grad_wide)
    loads[2].wait()
    for slot in range(2):
        present = jnp.where(table[T_PRESENT + slot] > 0, 1.0, 0.0)
        for row in range(8):
            moved = blocks((product(turns[0], cotangent[slot, row]) * present).astype(BF16))
            grad_blocks[slot, row] = moved
            grad_wide[slot, 2 + row, 2:10] = moved
    take_rims(grad_blocks, grad_strips, grad_corners)
    for slot in range(2):
        for side in range(4):
            keep = jnp.where(piece_of(table, slot, 4 + side)[5] > 0, 1.0, 0.0).astype(BF16)
            at = slot * 4 + side
            grad_corners[at] = grad_corners[at] * keep
    send_rims(table, grad_strips, grad_corners, send_e, T_GIVE_STRIP, T_GIVE_CORNER)
    rims_grad.start()

    loads[3].wait()
    forward[...] = jnp.zeros_like(forward)
    flipped[...] = jnp.zeros_like(flipped)
    for layer in range(2):
        for up in range(3):
            for across in range(3):
                weight = kernels[layer, up, across]
                turned = weight.T
                for side in range(2):
                    at = (up * 4 + side + across) * 128
                    forward[layer, at : at + 128, side * 128 : side * 128 + 128] = weight
                    at = (up * 4 + side + 2 - across) * 128
                    flipped[layer, at : at + 128, side * 128 : side * 128 + 128] = turned
    for slot in range(2):
        for row in (0, 5):
            sources = [grad_wide[slot, row + 2 - up : row + 7 - up] for up in range(3)]
            wide[slot, row : row + 5] = paired_conv(sources, 0, 5, flipped[1])
        total[slot] = wide[slot, 1:9, 1:9]
    give_back(table, wide, turns, send_b, given_strips, given_corners)
    back_two.start()

    for slot in range(2):
        for step in range(4):
            at = slot * 1024 + step * 256
            turned_two[:, at : at + 256] = cells(grad_blocks[slot, step * 2 : step * 2 + 2]).T
    widened[...] = jnp.zeros_like(widened)
    grad_even[...] = jnp.zeros_like(grad_even)
    grad_odd[...] = jnp.zeros_like(grad_odd)
    for slot in range(2):
        padded[slot, 1:9, 1:9] = state_blocks[slot]

    def arrange(rows_even, rows_odd, span):
        def half_rows(slot, row):
            return halves(padded[slot, row : row + 1, span])[0]

        at = slice(span.start * 2, span.stop * 2)
        for row in rows_even:
            both = [half_rows(slot, row) for slot in range(2)]
            even[row, at] = jnp.concatenate(both, axis=1).astype(BF16)
        for row in rows_odd:
            both = [shifted_up(half_rows(slot, row), half_rows(slot, row + 1)) for slot in range(2)]
            odd[row, at] = jnp.concatenate(both, axis=1).astype(BF16)

    arrange(range(1, 9), range(1, 8), slice(1, 9))
    rims_one.wait()
    widen_thin(table, thin_strips, thin_corners, in_a, unpack, unpack_corners, padded)
    arrange(range(1, 9), range(1, 8), slice(0, 1))
    arrange(range(1, 9), range(1, 8), slice(9, 10))
    arrange((), (0, 8), slice(0, 10))
    for row in (0, 4):
        sources = [odd[row : row + 4], even[row + 1 : row + 5], odd[row + 1 : row + 5]]
        result = paired_conv(sources, 1, 8, forward[0])
        hidden, slopes = gelu_parts(result)
        slope[row : row + 4] = slopes
        for slot in range(2):
            part = hidden[:, :, slot * 8 : slot * 8 + 8].reshape(4, 8, 16, 128).astype(BF16)
            hidden_blocks[slot, row : row + 4] = part
            widened[slot, row + 1 : row + 5, 1:9] = part
    take_rims(hidden_blocks, strips, corners)
    send_rims(table, strips, corners, send_c)
    rims_two.start()

    rims_grad.wait()
    extra = rim_terms(table, in_e, grad_strips, grad_corners, strips, corners, turns, masked)
    windows = []
    for slot in range(2):
        for row in (0, 4):
            taps = [
                cells(widened[slot, row + up : row + up + 4, across : across + 8])
                for up in range(3)
                for across in range(3)
            ]
            windows.append((slot * 1024 + row * 128, taps))
    reduce_two.put(gradient_terms(turned_two, windows, extra))
    broken = jnp.zeros((1, 16, 128), F32) + table[T_OVER].astype(F32)
    for half in range(2):
        reduce_one.half_send[half, 36:37] = jnp.zeros((1, 16, 128), BF16)
        reduce_two.half_send[half, 36:37] = broken.astype(BF16)
    reduce_two.one()

    back_two.wait()
    take_back(table, in_b, given_strips, given_corners, total)
    for row in range(8):
        both = [total[slot, row].astype(BF16).astype(F32).reshape(16, 8, 128) for slot in range(2)]
        grad = (jnp.concatenate(both, axis=1) * slope[row]).astype(BF16)
        grad_even[row + 1, 2:18] = grad
        turned_one[:, row * 256 : row * 256 + 256] = cells(grad).T
    reduce_two.two()
    windows = []
    for row in range(0, 8, 2):
        taps = []
        for source, at in ((odd, row), (even, row + 1), (odd, row + 1)):
            for across in range(3):
                taps.append(cells(source[at : at + 2, 1 + across : 17 + across]))
        windows.append((row * 256, taps))
    reduce_one.put(gradient_terms(turned_one, windows))
    reduce_one.one()

    for row in range(9):
        low = grad_even[row, 2:18].astype(F32)
        high = grad_even[row + 1, 2:18].astype(F32)
        both = [
            shifted_up(low[:, slot * 8 : slot * 8 + 8], high[:, slot * 8 : slot * 8 + 8])
            for slot in range(2)
        ]
        grad_odd[row + 1, 2:18] = jnp.concatenate(both, axis=1).astype(BF16)
    reduce_one.two()

    def returned(row):
        sources = [grad_odd[row + 1 : row + 6], grad_even[row : row + 5], grad_odd[row : row + 5]]
        result = paired_conv(sources, 0, 9, flipped[0])
        blank = jnp.zeros((5, 1, 8, 128), F32)
        for slot in range(2):
            part = jnp.concatenate([blank, result[:, :, slot * 8 : slot * 8 + 8], blank], axis=1)
            wide[slot, row : row + 5] = part.reshape(5, 10, 16, 128)

    def finish(slot):
        present = jnp.where(table[T_PRESENT + slot] > 0, 1.0, 0.0)
        for row in (0, 4):
            sources = [widened[slot, row + up : row + up + 4] for up in range(3)]
            result = paired_conv(sources, 0, 4, forward[1])
            value = state_blocks[slot, row : row + 4].astype(F32) + result
            fresh[slot, row : row + 4] = (value * present).astype(BF16)

    returned(0)
    returned(5)
    give_back(table, wide, turns, send_d, given_strips, given_corners)
    back_one.start()
    for slot in range(2):
        total[slot] = wide[slot, 1:9, 1:9]
    reduce_two.three()
    reduce_one.three()
    rims_two.wait()
    widen(table, hidden_blocks, strips, corners, in_c, turns, widened)
    finish(0)
    finish(1)
    reduce_two.four()
    reduce_one.four()
    back_one.wait()
    take_back(table, in_d, given_strips, given_corners, total)
    for slot in range(2):
        present = jnp.where(table[T_PRESENT + slot] > 0, 1.0, 0.0)
        value = grad_blocks[slot].astype(F32) + total[slot]
        summed[slot] = (value * present).astype(BF16)
    reduce_two.five()
    reduce_one.five()
    reduce_two.end(sums, 1, over)
    reduce_one.end(sums, 0, None)


def settle(scale, fresh, summed, sums, back, next_state, cell_grad, kernel_grads):
    for row in range(fresh.shape[0]):
        next_state[row] = product(back[...], cells(fresh[row])).astype(BF16)
        cell_grad[row] = product(back[...], cells(summed[row])).astype(BF16)
    kernel_grads[...] = sums[...].astype(F32) * scale


def vmem(shape, kind):
    return pltpu.VMEM(shape, kind)


def specs(kinds):
    spaces = {"s": pltpu.SMEM, "v": pltpu.VMEM, "a": pl.ANY}
    return [pl.BlockSpec(memory_space=spaces[kind]) for kind in kinds]


def shape(dims, kind):
    return jax.ShapeDtypeStruct(dims, kind)


TILES = (2, 8, 8, 16, 128)
STRIPS = (8, 8, 16, 128)
CORNERS = (8, 16, 128)
SENT = (6, PART, 16, 128)
THIN_SENT = (6, THIN, 16, 128)
NATURAL = (2, 8, 128, 128)


def sum_buffers():
    return [
        vmem((2, HALF, 16, 128), BF16), vmem((HALF, 16, 128), BF16), vmem((HALF, 16, 128), BF16),
        vmem((15, CHUNK, 16, 128), BF16), vmem((8, CHUNK, 16, 128), BF16), vmem((16, CHUNK, 16, 128), BF16),
        vmem((HALF, 16, 128), BF16), vmem((HALF, 16, 128), BF16), vmem((HALF, 16, 128), F32),
    ]


def finished(scale, fresh, summed, sums, back):
    def rows(count, *tail):
        return pl.BlockSpec((count,) + tail, lambda step: (step,) + (0,) * len(tail))

    return pl.pallas_call(
        functools.partial(settle, scale),
        grid=(2,),
        out_shape=[
            shape((16, 128, 128), BF16), shape((16, 128, 128), BF16), shape((2 * UNITS, 16, 128), F32)
        ],
        in_specs=[
            rows(8, 8, 16, 128), rows(8, 8, 16, 128), rows(UNITS, 16, 128),
            pl.BlockSpec((128, 128), lambda step: (0, 0)),
        ],
        out_specs=[rows(8, 128, 128), rows(8, 128, 128), rows(UNITS, 16, 128)],
        compiler_params=pltpu.CompilerParams(vmem_limit_bytes=10 * 1024 * 1024),
    )(
        fresh.reshape(16, 8, 16, 128), summed.reshape(16, 8, 16, 128),
        sums.reshape(2 * UNITS, 16, 128), back,
    )


def routed(cell_state, cotangent, kernels, slot_of_tile, neighbours, rotations, corner_flags):
    table = pl.pallas_call(
        plan_kernel,
        out_shape=shape((T_SIZE,), jnp.int32),
        in_specs=specs("ssss"),
        out_specs=specs("s")[0],
        scratch_shapes=[pltpu.SMEM((2 * SPAN,), jnp.int32)],
    )(slot_of_tile, neighbours.T, rotations.T, corner_flags.T)
    scale = 1.0 / math.sqrt(
        cell_state.shape[0] * lax.axis_size("dp") * slot_of_tile.shape[0] * cell_state.shape[2] ** 2
    )
    turns = permutations()
    fresh, summed, sums, over = pl.pallas_call(
        whole,
        out_shape=[
            shape(TILES, BF16), shape(TILES, BF16), shape((2, UNITS, 16, 128), BF16), shape((1,), jnp.int32)
        ],
        in_specs=specs("saaaavvvv"),
        out_specs=specs("vvvs"),
        scratch_shapes=[
            vmem(NATURAL, BF16), vmem(NATURAL, BF16), vmem(kernels.shape, BF16), vmem(turns.shape, BF16),
            pltpu.SemaphoreType.DMA((4,)), vmem((8, 4, 16, 128), BF16), vmem(CORNERS, F32),
            vmem(TILES, BF16), vmem(TILES, BF16), vmem(TILES, BF16),
            vmem(STRIPS, BF16), vmem(CORNERS, BF16), vmem(STRIPS, BF16), vmem(CORNERS, BF16),
            vmem(STRIPS, BF16), vmem(CORNERS, BF16),
        ]
        + [vmem(THIN_SENT, BF16)]
        + [vmem(SENT, BF16)] * 4
        + [vmem(THIN_SENT, BF16)]
        + [vmem(SENT, BF16)] * 4
        + [
            vmem((2, 1536, 256), BF16), vmem((2, 1536, 256), BF16),
            vmem((2, 12, 12, 16, 128), BF16), vmem((2, 10, 10, 16, 128), F32), vmem(TILES, F32),
            vmem((2, 10, 10, 16, 128), BF16), vmem((2, 10, 10, 16, 128), BF16),
            vmem((10, 20, 16, 128), BF16), vmem((9, 20, 16, 128), BF16),
            vmem((8, 16, 16, 128), F32), vmem((10, 20, 16, 128), BF16), vmem((11, 20, 16, 128), BF16),
            vmem((128, 2048), BF16), vmem((128, 2048), BF16), vmem((512, 1024), BF16),
        ]
        + sum_buffers()
        + sum_buffers()
        + [
            pltpu.SemaphoreType.DMA((5, 2, 6)),
            pltpu.SemaphoreType.DMA((2, 39)),
            pltpu.SemaphoreType.DMA((2, 39)),
        ],
        compiler_params=pltpu.CompilerParams(
            vmem_limit_bytes=VMEM_BYTES, collective_id=1, has_side_effects=True
        ),
    )(
        table, cell_state.reshape(NATURAL), cotangent.reshape(NATURAL), kernels,
        jnp.asarray(turns, BF16), *(jnp.asarray(part, BF16) for part in packings()),
    )
    back = jnp.asarray(turns[1], BF16)
    arrays = (cell_state, cotangent, kernels, slot_of_tile, neighbours, rotations, corner_flags)

    def fast(*_):
        outs = finished(scale, fresh, summed, sums, back)
        return tuple(out.reshape(like) for out, like in zip(outs, (cell_state.shape, cell_state.shape, kernels.shape)))

    return lax.cond(over[0] == 0, fast, shards, *arrays)


def solution(mesh):
    in_specs = (
        P("dp", "space", None, None, None),
        P("dp", "space", None, None, None),
        P(),
        P(),
        P(),
        P(),
        P(),
    )
    out_specs = (P("dp", "space", None, None, None), P("dp", "space", None, None, None), P())
    return jax.shard_map(routed, mesh=mesh, in_specs=in_specs, out_specs=out_specs, check_vma=False)
```

```python
import functools
import math

import jax
import jax.numpy as jnp
import numpy as np
from jax import lax
from jax.experimental import pallas as pl
from jax.experimental.pallas import tpu as pltpu
from jax.sharding import PartitionSpec as P

RES_BLOCKS = 1
DILATION_ONE = 2
DILATION_TWO = 4
REACH_DEV = 3


CONV_AXES = ("NHWC", "HWIO", "NHWC")


def as_sent(shard):

    def short(part):
        return part.astype(jnp.bfloat16) if part.dtype == jnp.float32 else part

    return jax.tree.map(short, shard)


def shifted(value, axis, steps):
    count = lax.axis_size(axis)
    pairs = [(source, (source + steps) % count) for source in range(count)]
    return lax.ppermute(value, axis, pairs)


def boundary(tile_data, rim_depth):
    extent = tile_data.shape[3]
    far = extent - rim_depth
    sides = [
        tile_data[:, :, :rim_depth],
        tile_data[:, :, :, far:],
        tile_data[:, :, far:],
        tile_data[:, :, :, :rim_depth],
    ]
    blocks = [
        tile_data[:, :, :rim_depth, far:],
        tile_data[:, :, far:, far:],
        tile_data[:, :, far:, :rim_depth],
        tile_data[:, :, :rim_depth, :rim_depth],
    ]
    strips = jnp.stack(
        [jnp.rot90(sides[quarter], quarter, axes=(2, 3)) for quarter in range(4)], axis=2
    )
    corners = jnp.stack(
        [jnp.rot90(blocks[quarter], quarter, axes=(2, 3))[:, :, :, ::-1] for quarter in range(4)],
        axis=2,
    )
    return (strips, corners)


def assemble(tile_data, strips, corners):
    edge_parts = [
        jnp.rot90(strips[:, :, quarter, ::-1, ::-1], -quarter, axes=(2, 3)) for quarter in range(4)
    ]
    corner_parts = [
        jnp.rot90(corners[:, :, quarter, ::-1], -quarter, axes=(2, 3)) for quarter in range(4)
    ]
    top_row = jnp.concatenate([corner_parts[3], edge_parts[0], corner_parts[0]], axis=3)
    middle = jnp.concatenate([edge_parts[3], tile_data, edge_parts[1]], axis=3)
    bottom = jnp.concatenate([corner_parts[2], edge_parts[2], corner_parts[1]], axis=3)
    return jnp.concatenate([top_row, middle, bottom], axis=2)


def rim_pieces(tile_data, rim_depth):
    strips, corners = boundary(tile_data, rim_depth)
    joined = jnp.concatenate([strips, corners], axis=4)
    return joined.reshape((joined.shape[0], joined.shape[1] * 4) + joined.shape[3:])


def conv_apply(padded, kernel, spread):
    merged = padded.reshape((-1,) + padded.shape[2:])
    result = lax.conv_general_dilated(
        merged,
        kernel,
        (1, 1),
        "VALID",
        rhs_dilation=(spread, spread),
        dimension_numbers=CONV_AXES,
        preferred_element_type=jnp.float32,
    )
    return result.reshape(padded.shape[:2] + result.shape[1:])


def conv_back(grad_out, kernel, spread):
    merged = grad_out.reshape((-1,) + grad_out.shape[2:])
    flipped = jnp.swapaxes(kernel[::-1, ::-1], 2, 3)
    margin = 2 * spread
    result = lax.conv_general_dilated(
        merged,
        flipped,
        (1, 1),
        ((margin, margin), (margin, margin)),
        rhs_dilation=(spread, spread),
        dimension_numbers=CONV_AXES,
        preferred_element_type=jnp.float32,
    )
    return result.reshape(grad_out.shape[:2] + result.shape[1:])


def kernel_grad(padded, grad_out, spread):
    extent = grad_out.shape[2]
    tap_terms = []
    for row_tap in range(3):
        for col_tap in range(3):
            window = padded[
                :,
                :,
                row_tap * spread : row_tap * spread + extent,
                col_tap * spread : col_tap * spread + extent,
            ]
            tap_terms.append(
                lax.dot_general(
                    window,
                    grad_out,
                    (((0, 1, 2, 3), (0, 1, 2, 3)), ((), ())),
                    preferred_element_type=jnp.float32,
                )
            )
    stacked = jnp.stack(tap_terms)
    return stacked.reshape((3, 3) + stacked.shape[1:])


def halo_plan(slot_of_tile, neighbours, rotations, corner_flags, slot_count):
    span_count = lax.axis_size("space")
    myself = lax.axis_index("space")
    tile_count = slot_of_tile.shape[0]
    owned = myself * slot_count + jnp.arange(slot_count, dtype=jnp.int32)
    matches = slot_of_tile[None, :] == owned[:, None]
    present = jnp.any(matches, axis=1)
    tile_here = jnp.sum(
        jnp.where(matches, jnp.arange(tile_count, dtype=jnp.int32)[None, :], 0), axis=1
    )
    nearby = jnp.take(neighbours, tile_here, axis=0)
    turn_code = jnp.take(rotations, tile_here, axis=0)
    facing = (jnp.arange(8, dtype=jnp.int32)[None, :] % 4 + 2 + turn_code) % 4
    source = jnp.take(slot_of_tile, nearby)
    holder = source // slot_count
    within = source % slot_count
    offset = jnp.clip(
        (myself - holder + span_count + REACH_DEV) % span_count - REACH_DEV, -REACH_DEV, REACH_DEV
    )
    select = ((offset + REACH_DEV) * slot_count + within) * 4 + facing
    keep_corner = jnp.take(corner_flags, tile_here, axis=0) == 0
    return (select[:, :4].reshape(-1), select[:, 4:].reshape(-1), keep_corner.reshape(-1), present)


def fetch_near(bundle):
    arrived = {0: bundle}
    for offset in list(range(-REACH_DEV, 0)) + list(range(1, REACH_DEV + 1)):
        arrived[offset] = shifted(as_sent(bundle), "space", offset).astype(bundle.dtype)
    return [arrived[offset] for offset in range(-REACH_DEV, REACH_DEV + 1)]


def return_near(parts):
    total = parts[0]
    for offset in list(range(-REACH_DEV, 0)) + list(range(1, REACH_DEV + 1)):
        total = total + shifted(parts[offset].astype(jnp.bfloat16), "space", -offset).astype(
            jnp.float32
        )
    return total


def halo_forward(tile_data, rim_depth, plan):
    pick_edge, pick_corner, keep_corner = plan[:3]
    samples_here, slot_count, extent = (tile_data.shape[0], tile_data.shape[1], tile_data.shape[2])
    channels = tile_data.shape[4]
    gathered = jnp.concatenate(fetch_near(rim_pieces(tile_data, rim_depth)), axis=1)
    edge_part = jnp.take(gathered, pick_edge, axis=1)[:, :, :, :extent]
    corner_part = jnp.take(gathered, pick_corner, axis=1)[:, :, :, extent:]
    corner_part = jnp.where(
        keep_corner[None, :, None, None, None], corner_part, jnp.zeros((), corner_part.dtype)
    )
    strips = edge_part.reshape(samples_here, slot_count, 4, rim_depth, extent, channels)
    corners = corner_part.reshape(samples_here, slot_count, 4, rim_depth, rim_depth, channels)
    return assemble(tile_data, strips, corners)


def halo_backward(grad_wide, rim_depth, plan):
    pick_edge, pick_corner, keep_corner = plan[:3]
    samples_here, slot_count = (grad_wide.shape[0], grad_wide.shape[1])
    extent = grad_wide.shape[2] - 2 * rim_depth
    channels = grad_wide.shape[4]
    tile_zero = jnp.zeros((samples_here, slot_count, extent, extent, channels), jnp.float32)
    strip_zero = jnp.zeros((samples_here, slot_count, 4, rim_depth, extent, channels), jnp.float32)
    corner_zero = jnp.zeros(
        (samples_here, slot_count, 4, rim_depth, rim_depth, channels), jnp.float32
    )
    _, assemble_back = jax.vjp(assemble, tile_zero, strip_zero, corner_zero)
    grad_tiles, grad_strips, grad_corners = assemble_back(grad_wide)
    pieces = slot_count * 4
    grad_corners = grad_corners.reshape(samples_here, pieces, rim_depth, rim_depth, channels)
    grad_corners = jnp.where(keep_corner[None, :, None, None, None], grad_corners, 0.0)
    spread_out = jnp.zeros(
        (samples_here, (2 * REACH_DEV + 1) * pieces, rim_depth, extent + rim_depth, channels),
        jnp.float32,
    )
    spread_out = spread_out.at[:, pick_edge, :, :extent].add(
        grad_strips.reshape(samples_here, pieces, rim_depth, extent, channels)
    )
    spread_out = spread_out.at[:, pick_corner, :, extent:].add(grad_corners)
    parts = {
        offset: spread_out[:, (offset + REACH_DEV) * pieces : (offset + REACH_DEV + 1) * pieces]
        for offset in range(-REACH_DEV, REACH_DEV + 1)
    }
    returned = return_near(parts)
    _, rim_back = jax.vjp(lambda tile_part: rim_pieces(tile_part, rim_depth), tile_zero)
    return grad_tiles + rim_back(returned)[0]


def sum_over(value, axis):
    count = lax.axis_size(axis)
    step = 1
    while step < count:
        pairs = [(source, source ^ step) for source in range(count)]
        value = value + lax.ppermute(value, axis, pairs)
        step *= 2
    return value


def shards(cell_state, cotangent, kernels, slot_of_tile, neighbours, rotations, corner_flags):
    plan = halo_plan(slot_of_tile, neighbours, rotations, corner_flags, cell_state.shape[1])
    keep_slot = plan[3][None, :, None, None, None]
    current = cell_state
    block_at = 0
    widened = halo_forward(current, DILATION_ONE, plan)
    before = conv_apply(widened, kernels[2 * block_at], DILATION_ONE)
    hidden = jax.nn.gelu(before).astype(jnp.bfloat16)
    widened_two = halo_forward(hidden, DILATION_TWO, plan)
    branch = conv_apply(widened_two, kernels[2 * block_at + 1], DILATION_TWO)
    stored = [(widened, before, widened_two)]
    current = (current.astype(jnp.float32) + branch).astype(jnp.bfloat16)
    next_state = jnp.where(keep_slot, current, jnp.zeros((), jnp.bfloat16))
    gradient = jnp.where(keep_slot, cotangent, jnp.zeros((), jnp.bfloat16))
    kernel_terms = [None] * (2 * RES_BLOCKS)
    extent = cell_state.shape[2]
    norm_scale = 1.0 / math.sqrt(
        cell_state.shape[0] * lax.axis_size("dp") * slot_of_tile.shape[0] * extent * extent
    )
    for block_at in reversed(range(RES_BLOCKS)):
        widened, before, widened_two = stored[block_at]
        outer_term = kernel_grad(widened_two, gradient, DILATION_TWO)
        kernel_terms[2 * block_at + 1] = outer_term
        grad_hidden = halo_backward(
            conv_back(gradient, kernels[2 * block_at + 1], DILATION_TWO), DILATION_TWO, plan
        ).astype(jnp.bfloat16)
        _, gelu_back = jax.vjp(jax.nn.gelu, before)
        grad_before = gelu_back(grad_hidden.astype(jnp.float32))[0].astype(jnp.bfloat16)
        inner_term = kernel_grad(widened, grad_before, DILATION_ONE)
        kernel_terms[2 * block_at] = inner_term
        returned = halo_backward(
            conv_back(grad_before, kernels[2 * block_at], DILATION_ONE), DILATION_ONE, plan
        )
        gradient = (gradient.astype(jnp.float32) + returned).astype(jnp.bfloat16)
    stacked = jnp.stack(kernel_terms)
    stacked = sum_over(sum_over(stacked, "space"), "dp")
    return (next_state, gradient, stacked * norm_scale)


MESH_ID = pl.DeviceIdType.MESH
SPAN = 128
STRIP_SLOTS = (1, 2, 2, 2, 2, 1)
CORNER_CAP = 3
PART = CORNER_CAP + 16
THIN = 9
OFFSETS = (-3, -2, -1, 1, 2, 3)
ORDER = (2, 3, 1, 4, 0, 5)
SELF = 6
NOT_THERE = 32
T_STRIP_LIST, T_CORNER_LIST, T_GIVE_STRIP, T_GIVE_CORNER = 0, 12, 36, 48
T_ADD, T_PIECES, T_PRESENT = 72, 104, 200
T_OVER, T_SPARE, T_SIZE = 202, 203, 208
VMEM_BYTES = 56 * 1024 * 1024
F32 = jnp.float32
BF16 = jnp.bfloat16


def cell_order():
    rows, cols = np.meshgrid(np.arange(4), np.arange(4), indexing="ij")
    return ((cols // 2) * 8 + (rows // 2) * 4 + (rows % 2) * 2 + cols % 2).astype(np.int64)


def permutations():
    order = cell_order()
    to_blocks = np.zeros((128, 128), np.float32)
    for row in range(4):
        for col in range(32):
            to_blocks[(col // 4) * 16 + order[row, col % 4], row * 32 + col] = 1
    mats = [to_blocks, to_blocks.T]
    for turn in range(4):
        turned = np.rot90(order, turn)
        small = np.zeros((16, 16), np.float32)
        small[order.reshape(-1), turned.reshape(-1)] = 1
        for flip in range(2):
            line = np.eye(8)[::-1] if flip else np.eye(8)
            mats.append(np.kron(line, small))
    return np.stack(mats)


def turn_matrix(turn, flip):
    return 2 + 2 * turn + flip


def flips(edge, turn):
    side = (edge + 2 + turn) & 1
    once = jnp.where((turn == 1) & (side == 0), 1, 0)
    thrice = jnp.where((turn == 3) & (side == 1), 1, 0)
    return jnp.where(turn == 2, 1, once + thrice)


def packings():
    order = cell_order()
    mats = permutations()
    inner = (order[:2], order[:, 2:], order[2:], order[:, :2])
    ends = (order[:2, 2:], order[2:, 2:], order[2:, :2], order[:2, :2])
    pack = np.zeros((4, 64, 128), np.float32)
    pack_corners = np.zeros((128, 128), np.float32)
    for side in range(4):
        for block in range(8):
            for at, cell in enumerate(sorted(inner[side].reshape(-1))):
                pack[side, block * 8 + at, block * 16 + cell] = 1
        for at, cell in enumerate(sorted(ends[side].reshape(-1))):
            for slot in range(2):
                for copy in range(4):
                    base = (slot * 4 + side) * 16
                    pack_corners[base + copy * 4 + at, base + cell] = 1
    unpack = np.zeros((16, 128, 128), np.float32)
    unpack_corners = np.zeros((16, 16, 128), np.float32)
    for turn in range(4):
        for edge in range(4):
            side = (edge + 2 + turn) % 4
            flip = int(turn == 2 or (turn == 1 and side % 2 == 0) or (turn == 3 and side % 2 == 1))
            unpack[turn * 4 + edge, :, :64] = mats[2 + 2 * turn + flip] @ pack[side].T
            four = pack_corners[side * 16 : side * 16 + 4, side * 16 : side * 16 + 16]
            small = mats[2 + 2 * turn][:16, :16] @ four.T
            unpack_corners[turn * 4 + edge] = np.tile(small, (1, 32))
    return pack, pack_corners, unpack, unpack_corners


def make_plan(me, order_ref, slot_ref, near_ref, turn_ref, flag_ref, table):
    core = me % 2
    order = order_ref[...]
    spot = lax.broadcasted_iota(jnp.int32, order.shape, 1) + 1
    over = jnp.int32(0)
    found = [[], []]

    def tile_in(offset, slot):
        number = jnp.max(jnp.where(order == (me + offset + SPAN) % SPAN * 2 + slot, spot, 0))
        return number > 0, jnp.maximum(number - 1, 0)

    for where, offset in enumerate(OFFSETS):
        lists = [[jnp.int32(0)] * 2, [jnp.int32(0)] * CORNER_CAP]
        seen = [jnp.int32(0), jnp.int32(0)]
        for slot in range(2):
            there, row = tile_in(offset, slot)
            for piece in range(8):
                kind = piece // 4
                source = slot_ref[near_ref[piece, row]]
                hit = there & (source // 2 == me)
                turn = turn_ref[piece, row] & 3
                packed = (source % 2 * 4 + ((piece + 2 + turn) & 3)) * 4 + turn + 1
                cap = CORNER_CAP if kind else (1, 2, 1 + core, 2 - core, 2, 1)[where]
                late = seen[kind] >= cap
                if offset in (-3, 3):
                    late = late | (core == (0 if offset < 0 else 1))
                over = over + jnp.where(hit & late, 1, 0)
                for rank, old in enumerate(lists[kind]):
                    lists[kind][rank] = jnp.where(hit & (seen[kind] == rank), packed, old)
                seen[kind] = seen[kind] + jnp.where(hit, 1, 0)
        for kind, base in enumerate((T_STRIP_LIST, T_CORNER_LIST)):
            for rank, packed in enumerate(lists[kind]):
                code = where * (4 if kind else 2) + rank
                table[base + code] = jnp.maximum(packed - 1, 0) // 4
                found[kind].append((packed, code))
    seen = [[jnp.int32(0)] * 7, [jnp.int32(0)] * 7]
    given = [[], []]
    for slot in range(2):
        there, row = tile_in(0, slot)
        valid = jnp.where(there, 1, 0)
        table[T_PRESENT + slot] = valid
        for piece in range(8):
            kind = piece // 4
            source = slot_ref[near_ref[piece, row]]
            turn = turn_ref[piece, row] & 3
            offset = jnp.clip((source // 2 - me + 3 + SPAN) % SPAN, 0, 6)
            where = jnp.where(offset == 3, SELF, jnp.where(offset < 3, offset, offset - 1))
            rank = jnp.int32(0)
            for choice in range(7):
                match = jnp.where(offset == choice, valid, 0)
                rank = rank + match * seen[kind][choice]
                seen[kind][choice] = seen[kind][choice] + match
            rank = jnp.minimum(rank, CORNER_CAP - 1 if kind else 1)
            keep = valid
            if kind:
                keep = valid * jnp.where(flag_ref[piece - 4, row] == 0, 1, 0)
            entry = source % 2 * 4 + ((piece + 2 + turn) & 3)
            base = T_PIECES + (slot * 8 + piece) * 6
            for field, value in enumerate((valid, where, rank, turn, entry, keep)):
                table[base + field] = value
            mine = slot * 4 + piece % 4
            own = there & (where == SELF)
            found[kind].append((jnp.where(own, entry * 4 + turn + 1, 0), (24 if kind else 12) + mine))
            code = where * (4 if kind else 2) + rank
            given[kind].append((jnp.where(there & (where != SELF), code, -1), mine))
    for kind, base in enumerate((T_GIVE_STRIP, T_GIVE_CORNER)):
        for where in range(6):
            for rank in range(CORNER_CAP if kind else 2):
                code = where * (4 if kind else 2) + rank
                chosen = jnp.int32(0)
                for place, mine in given[kind]:
                    chosen = jnp.where(place == code, mine, chosen)
                table[base + code] = chosen
        for entry in range(8):
            chosen, count = jnp.int32(NOT_THERE * 4), jnp.int32(0)
            for packed, code in found[kind]:
                turn = packed - 1 - entry * 4
                hit = (turn >= 0) & (turn < 4)
                chosen = jnp.where(hit, code * 4 + turn, chosen)
                count = count + jnp.where(hit, 1, 0)
            table[T_ADD + kind * 16 + entry] = chosen // 4
            table[T_ADD + kind * 16 + 8 + entry] = chosen & 3
            over = over + jnp.maximum(count - 1, 0)
    table[T_OVER] = over


def piece_of(table, slot, piece):
    base = T_PIECES + (slot * 8 + piece) * 6
    return [table[base + field] for field in range(6)]


def blocks(value):
    return value.reshape((-1, 16, 128))


def cells(value):
    return value.reshape((-1, 128))


def product(left, right):
    return jnp.dot(left, right, preferred_element_type=F32)


EDGE_OF = ((0, slice(None)), (slice(None), 7), (7, slice(None)), (slice(None), 0))
CORNER_OF = ((0, 7), (7, 7), (7, 0), (0, 0))
BAND_OF = ((0, slice(1, 9)), (slice(1, 9), 9), (9, slice(1, 9)), (slice(1, 9), 0))
BLOCK_OF = ((0, 9), (9, 9), (9, 0), (0, 0))


def take_rims(tile_ref, strips, corners):
    for slot in range(2):
        for side in range(4):
            strips[slot * 4 + side] = blocks(tile_ref[(slot,) + EDGE_OF[side]])
            corners[slot * 4 + side] = tile_ref[(slot,) + CORNER_OF[side]]


def send_rims(table, strips, corners, send, strip_list=T_STRIP_LIST, corner_list=T_CORNER_LIST):
    for where in range(6):
        for rank in range(STRIP_SLOTS[where]):
            at = CORNER_CAP + rank * 8
            send[where, at : at + 8] = strips[table[strip_list + where * 2 + rank]]
        for rank in range(CORNER_CAP):
            send[where, rank] = corners[table[corner_list + where * 4 + rank]]


def send_thin(table, strips, corners, send):
    group = lax.broadcasted_iota(jnp.int32, (16, 128), 0) // 4
    for where in range(6):
        for rank in range(STRIP_SLOTS[where]):
            send[where, 1 + rank * 4 : 5 + rank * 4] = strips[table[T_STRIP_LIST + where * 2 + rank]]
        unit = corners[table[T_CORNER_LIST + where * 4]]
        for rank in range(1, CORNER_CAP):
            unit = jnp.where(group == rank, corners[table[T_CORNER_LIST + where * 4 + rank]], unit)
        send[where, 0] = unit.astype(BF16)


def thin_rims(strips, corners, pack, pack_corners, thin_strips, thin_corners):
    for entry in range(8):
        packed = product(pack[entry % 4], cells(strips[entry]))
        thin_strips[entry] = blocks(packed.astype(BF16))
    thin_corners[...] = blocks(product(pack_corners[...], cells(corners[...])))


def corner_turns(table, turns, back):
    parts = []
    for slot in range(2):
        for side in range(4):
            fields = piece_of(table, slot, 4 + side)
            turn = (4 - fields[3]) & 3 if back else fields[3]
            rows = turns[turn_matrix(turn, 0)]
            at = (slot * 4 + side) * 16
            parts.append(rows[at : at + 16] * jnp.where(fields[5] > 0, 1.0, 0.0).astype(BF16))
    return jnp.concatenate(parts, axis=0)


def widen(table, tile_ref, strips, corners, arrived, turns, padded):
    for slot in range(2):
        padded[slot, 1:9, 1:9] = tile_ref[slot]
        for edge in range(4):
            valid, where, rank, turn, entry, keep = piece_of(table, slot, edge)
            own = strips[entry]
            other = arrived[jnp.minimum(where, 5), pl.ds(CORNER_CAP + rank * 8, 8)]
            strip = jnp.where(where == SELF, own, other)
            strip = jnp.where(valid > 0, strip, jnp.zeros_like(strip))
            turned = product(turns[turn_matrix(turn, flips(edge, turn))], cells(strip))
            padded[(slot,) + BAND_OF[edge]] = blocks(turned.astype(BF16))
    stack = []
    for slot in range(2):
        for side in range(4):
            valid, where, rank, turn, entry, keep = piece_of(table, slot, 4 + side)
            block = jnp.where(where == SELF, corners[entry], arrived[jnp.minimum(where, 5), rank])
            stack.append(jnp.where(valid > 0, block, jnp.zeros_like(block)))
    turned = product(corner_turns(table, turns, False), jnp.concatenate(stack, axis=0))
    turned = blocks(turned.astype(BF16))
    for slot in range(2):
        for side in range(4):
            padded[(slot,) + BLOCK_OF[side]] = turned[slot * 4 + side]


def give_back(table, wide, turns, send, strips, corners):
    for slot in range(2):
        for edge in range(4):
            valid, where, rank, turn, entry, keep = piece_of(table, slot, edge)
            band = cells(blocks(wide[(slot,) + BAND_OF[edge]])).astype(BF16)
            turned = product(turns[turn_matrix((4 - turn) & 3, flips(edge, turn))], band)
            strips[slot * 4 + edge] = blocks(turned.astype(BF16))
    stack = [wide[(slot,) + BLOCK_OF[side]].astype(BF16) for slot in range(2) for side in range(4)]
    turned = product(corner_turns(table, turns, True), jnp.concatenate(stack, axis=0))
    corners[...] = blocks(turned.astype(BF16))
    send_rims(table, strips, corners, send, T_GIVE_STRIP, T_GIVE_CORNER)


def widen_thin(table, thin_strips, thin_corners, arrived, unpack, unpack_corners, padded):
    for slot in range(2):
        for edge in range(4):
            valid, where, rank, turn, entry, keep = piece_of(table, slot, edge)
            other = arrived[jnp.minimum(where, 5), pl.ds(1 + rank * 4, 4)]
            strip = jnp.where(where == SELF, thin_strips[entry], other)
            strip = jnp.where(valid > 0, strip, jnp.zeros_like(strip))
            turned = product(unpack[turn * 4 + edge][:, :64], cells(strip))
            padded[(slot,) + BAND_OF[edge]] = blocks(turned.astype(BF16))
    lane = lax.broadcasted_iota(jnp.int32, (16, 128), 1)
    stack, parts = [], []
    for slot in range(2):
        for side in range(4):
            valid, where, rank, turn, entry, keep = piece_of(table, slot, 4 + side)
            block = jnp.where(where == SELF, thin_corners[entry], arrived[jnp.minimum(where, 5), 0].astype(F32))
            stack.append(jnp.where(valid > 0, block, jnp.zeros_like(block)).astype(BF16))
            first = (slot * 4 + side) * 16 + jnp.where(where == SELF, 0, rank) * 4
            chosen = (lane >= first) & (lane < first + 4) & (keep > 0)
            rows = unpack_corners[turn * 4 + side].astype(F32)
            parts.append(jnp.where(chosen, rows, jnp.zeros_like(rows)).astype(BF16))
    turned = product(jnp.concatenate(parts, axis=0), jnp.concatenate(stack, axis=0))
    turned = blocks(turned.astype(BF16))
    for slot in range(2):
        for side in range(4):
            padded[(slot,) + BLOCK_OF[side]] = turned[slot * 4 + side]


def owner_of(table, kind, entry):
    code = table[T_ADD + kind * 16 + entry]
    turn = table[T_ADD + kind * 16 + 8 + entry]
    return code, turn, (entry % 4 - 2 - turn) & 3


def copied_strip(code, arrived, strips):
    far = jnp.minimum(code, 11)
    near = jnp.clip(code - 12, 0, 7)
    part = jnp.where(code < 12, arrived[far // 2, pl.ds(CORNER_CAP + far % 2 * 8, 8)], strips[near])
    return jnp.where(code == NOT_THERE, jnp.zeros_like(part), part)


def copied_corner(code, arrived, corners):
    far = jnp.minimum(code, 23)
    near = jnp.clip(code - 24, 0, 7)
    part = jnp.where(code < 24, arrived[far // 4, far % 4], corners[near])
    return jnp.where(code == NOT_THERE, jnp.zeros_like(part), part)


def take_back(table, arrived, strips, corners, total):
    for slot in range(2):
        for side in range(4):
            at = (slot,) + EDGE_OF[side]
            code = owner_of(table, 0, slot * 4 + side)[0]
            total[at] = total[at] + copied_strip(code, arrived, strips).astype(F32)
    for slot in range(2):
        for side in range(4):
            at = (slot,) + CORNER_OF[side]
            code = owner_of(table, 1, slot * 4 + side)[0]
            total[at] = total[at] + copied_corner(code, arrived, corners).astype(F32)


STRIP_TAPS = (
    ((0, 0), (0, 1), (0, 2)),
    ((0, 2), (1, 2), (2, 2)),
    ((2, 0), (2, 1), (2, 2)),
    ((0, 0), (1, 0), (2, 0)),
)
CORNER_TAPS = ((0, 2), (2, 2), (2, 0), (0, 0))


def rim_terms(table, arrived, given_strips, given_corners, strips, corners, turns, masked):
    rims = []
    for entry in range(8):
        code, turn, edge = owner_of(table, 0, entry)
        grad = cells(copied_strip(code, arrived, given_strips)).T
        for choice in range(4):
            chosen = jnp.where(edge == choice, grad, jnp.zeros_like(grad))
            masked[choice * 128 : choice * 128 + 128, entry * 128 : entry * 128 + 128] = chosen
        band = product(turns[turn_matrix(turn, flips(edge, turn))], cells(strips[entry])).astype(BF16)
        blank = jnp.zeros((16, 128), BF16)
        longer = jnp.concatenate([blank, band, blank], axis=0)
        rims.append(jnp.concatenate([longer[step * 16 : step * 16 + 128] for step in range(3)], axis=1))
    edges = product(masked[...], jnp.concatenate(rims, axis=0))
    lane = lax.broadcasted_iota(jnp.int32, (128, 128), 1) // 16
    which = jnp.zeros((128, 128), jnp.int32)
    grads, parts = [], []
    for entry in range(8):
        code, turn, side = owner_of(table, 1, entry)
        grads.append(copied_corner(code, arrived, given_corners))
        which = jnp.where(lane == entry, side, which)
        parts.append(turns[turn_matrix(turn, 0)][entry * 16 : entry * 16 + 16])
    block = product(jnp.concatenate(parts, axis=0), cells(corners[...])).astype(BF16)
    grad = jnp.concatenate(grads, axis=0).astype(F32).T
    spread = [jnp.where(which == choice, grad, jnp.zeros_like(grad)) for choice in range(4)]
    ends = product(jnp.concatenate(spread, axis=0).astype(BF16), block)
    sums = [None] * 9
    for choice in range(4):
        rows = slice(choice * 128, choice * 128 + 128)
        found = [(tap, edges[rows, step * 128 : step * 128 + 128]) for step, tap in enumerate(STRIP_TAPS[choice])]
        found.append((CORNER_TAPS[choice], ends[rows]))
        for (up, across), value in found:
            old = sums[up * 3 + across]
            sums[up * 3 + across] = value if old is None else old + value
    return sums


def halves(value):
    return value.astype(F32).reshape(value.shape[0], value.shape[1] * 2, 8, 128)


def shifted_up(upper, lower):
    low = lax.broadcasted_iota(jnp.int32, upper.shape, upper.ndim - 2) < 4
    mixed = jnp.where(low, lower, upper)
    return jnp.concatenate([mixed[..., 4:, :], mixed[..., :4, :]], axis=mixed.ndim - 2)


def gelu_parts(value):
    root = math.sqrt(2.0 / math.pi)
    square = value * value
    bent = jnp.tanh(root * (value + 0.044715 * (value * square)))
    half = 0.5 * (1.0 + bent)
    slope = half + 0.5 * value * (1.0 - bent * bent) * (root * (1.0 + 3 * 0.044715 * square))
    return (value * half, slope)


UNITS = 72
HALF = 37
CHUNK = 3


def chunk_start(index):
    return (index * (HALF - CHUNK)) // 15


class Swap:
    def __init__(self, me, send, arrived, sems, corner_units=CORNER_CAP, strip_units=8):
        core = me % 2
        far, mate, other = 5 - 5 * core, 3 - core, 2 + core
        self.copies = []
        for where, offset, strips, send_at, recv_at in (
            (other, 2 * core - 1, 1, 2, 2),
            (1, -2, 2, 1, 4),
            (4, 2, 2, 4, 1),
            (far, 3 - 6 * core, 1, 0, 0),
            (mate, 1 - 2 * core, 2, 3, 3),
        ):
            size = corner_units + strip_units * strips
            self.copies.append(
                pltpu.make_async_remote_copy(
                    src_ref=send.at[where, pl.ds(0, size)],
                    dst_ref=arrived.at[5 - where, pl.ds(0, size)],
                    send_sem=sems.at[0, send_at],
                    recv_sem=sems.at[1, recv_at],
                    device_id={"space": lax.rem(me + offset + SPAN, SPAN)},
                    device_id_type=MESH_ID,
                )
            )

    def start(self):
        for copy in self.copies:
            copy.start()

    def wait(self):
        for copy in self.copies:
            copy.wait()


class Place:
    def __init__(self):
        me = lax.axis_index("space")
        self.me = me
        self.core, self.y, self.z, self.x_lo = me % 2, me // 2 % 4, me // 8 % 8, me // 64
        self.plane = (lax.axis_index("dp") * 2 + self.x_lo) * 4 + self.y
        self.mate = {"space": me + 1 - 2 * self.core}

    def at_plane(self, index):
        return {
            "dp": index // 8,
            "space": ((index // 4 % 2) * 8 + self.z) * 8 + index % 4 * 2 + self.core,
        }

    def at_line(self, index):
        return {"space": (self.x_lo * 8 + index) * 8 + self.y * 2 + self.core}


class Sum:
    def __init__(self, place, buffers, sems):
        self.place = place
        self.half_send, self.half_in, self.plane_send, self.plane_in, self.line_in = buffers[:5]
        self.wide_in, self.pair_send, self.pair_in, self.acc = buffers[5:]
        self.sems = sems
        self.copies = []

    def copy(self, source, target, index, where):
        one = pltpu.make_async_remote_copy(
            src_ref=source,
            dst_ref=target,
            send_sem=self.sems.at[0, index],
            recv_sem=self.sems.at[1, index],
            device_id=where,
            device_id_type=MESH_ID,
        )
        one.start()
        self.copies.append(one)

    def put(self, terms):
        for tap, term in enumerate(terms):
            value = blocks(term.astype(BF16))
            for part in range(2):
                half, at = divmod(tap * 8 + part * 4, 36)
                self.half_send[half, at : at + 4] = value[part * 4 : part * 4 + 4]

    def wait(self):
        for one in self.copies:
            one.wait()
        self.copies = []

    def one(self):
        place = self.place
        self.copy(self.half_send.at[1 - place.core], self.half_in, 0, place.mate)

    def two(self):
        place = self.place
        self.wait()
        self.acc[...] = self.half_send[place.core].astype(F32) + self.half_in[...].astype(F32)
        self.plane_send[...] = self.acc[...].astype(BF16)
        for step in range(1, 16):
            peer = lax.rem(place.plane + step, 16)
            source = self.plane_send.at[pl.ds(chunk_start(peer), CHUNK)]
            self.copy(source, self.plane_in.at[step - 1], step, place.at_plane(peer))

    def three(self):
        place = self.place
        self.wait()
        total = self.acc[pl.ds(chunk_start(place.plane), CHUNK)]
        for step in range(15):
            total = total + self.plane_in[step].astype(F32)
        self.line_in[place.z] = total.astype(BF16)
        for step in range(1, 8):
            peer = lax.rem(place.z + step, 8)
            self.copy(self.line_in.at[place.z], self.line_in.at[place.z], 15 + step, place.at_line(peer))

    def four(self):
        place = self.place
        self.wait()
        total = self.line_in[0].astype(F32)
        for index in range(1, 8):
            total = total + self.line_in[index].astype(F32)
        self.wide_in[place.plane] = total.astype(BF16)
        for step in range(1, 16):
            peer = lax.rem(place.plane + step, 16)
            here = self.wide_in.at[place.plane]
            self.copy(here, here, 22 + step, place.at_plane(peer))

    def five(self):
        self.wait()
        for index in range(16):
            at = chunk_start(index)
            self.pair_send[at : at + CHUNK] = self.wide_in[index]
        self.copy(self.pair_send, self.pair_in, 38, self.place.mate)

    def end(self, out, layer, over):
        self.wait()
        core = self.place.core
        mine, other = self.pair_send[...], self.pair_in[...]
        out[layer, :36] = jnp.where(core == 0, mine[:36], other[:36])
        out[layer, 36:] = jnp.where(core == 0, other[:36], mine[:36])
        if over is not None:
            over[0] = jnp.where(jnp.max(mine[36].astype(F32)) > 0.0, 1, 0)


def columns(value, first, count):
    rows, wide = value.shape[:2]
    paired = value.reshape(rows, wide // 2, 2, 16, 128)
    return [
        cells(paired[:, (first + step) // 2 : (first + step) // 2 + count, (first + step) % 2])
        for step in range(4)
    ]


def split_pairs(result, rows, count):
    wide = result.reshape(rows, count, 16, 256)
    return jnp.stack([wide[..., :128], wide[..., 128:]], axis=2).reshape(rows, count * 2, 16, 128)


def paired_conv(sources, first, count, weight):
    taps = [tap for value in sources for tap in columns(value, first, count)]
    result = product(jnp.concatenate(taps, axis=1), weight)
    return split_pairs(result, sources[0].shape[0], count)


def gradient_terms(turned, windows, extra=None):
    total = None
    for at, taps in windows:
        part = product(turned[:, at : at + taps[0].shape[0]], jnp.concatenate(taps, axis=1))
        total = part if total is None else total + part
    terms = [total[:, tap * 128 : tap * 128 + 128] for tap in range(9)]
    if extra is not None:
        terms = [term if more is None else term + more for term, more in zip(terms, extra)]
    return [term.T for term in terms]


def whole(
    slot_ref, near_ref, turn_ref, flag_ref, order_ref,
    state_far, cotangent_far, kernels_far, turns_far, unpack_far, pack, pack_corners, unpack_corners,
    fresh, summed, sums, over,
    table, state, cotangent, kernels, turns, unpack, load_sems, thin_strips, thin_corners, state_blocks, grad_blocks, hidden_blocks, strips, corners, given_strips, given_corners,
    grad_strips, grad_corners,
    send_a, send_b, send_c, send_d, send_e, in_a, in_b, in_c, in_d, in_e,
    forward, flipped, grad_wide, wide, total, padded, widened, even, odd, slope, grad_even, grad_odd,
    turned_one, turned_two, masked, *rest,
):
    swap_sems, one_sems, two_sems = rest[18:]
    loads = []
    pairs = (
        (turns_far, turns), (state_far, state), (cotangent_far, cotangent), (kernels_far, kernels),
        (unpack_far, unpack),
    )
    for index, (source, target) in enumerate(pairs):
        loads.append(pltpu.make_async_copy(source, target, load_sems.at[index]))
        loads[index].start()
    place = Place()
    me = place.me
    barrier = pltpu.get_barrier_semaphore()

    def greet(where):
        pl.semaphore_signal(barrier, inc=1, device_id=where, device_id_type=MESH_ID)

    for offset in OFFSETS:
        greet({"space": lax.rem(me + offset + SPAN, SPAN)})
    greet(place.mate)
    for step in range(1, 16):
        greet(place.at_plane(lax.rem(place.plane + step, 16)))
    for step in range(1, 8):
        greet(place.at_line(lax.rem(place.z + step, 8)))

    rims_one = Swap(me, send_a, in_a, swap_sems.at[0], 1, 4)
    back_two = Swap(me, send_b, in_b, swap_sems.at[1])
    rims_two = Swap(me, send_c, in_c, swap_sems.at[2])
    back_one = Swap(me, send_d, in_d, swap_sems.at[3])
    rims_grad = Swap(me, send_e, in_e, swap_sems.at[4])
    reduce_one = Sum(place, rest[:9], one_sems)
    reduce_two = Sum(place, rest[9:18], two_sems)

    make_plan(me, order_ref, slot_ref, near_ref, turn_ref, flag_ref, table)
    loads[0].wait()
    loads[1].wait()
    for slot in range(2):
        for row in range(8):
            moved = product(turns[0], state[slot, row])
            state_blocks[slot, row] = blocks(moved.astype(BF16))
    take_rims(state_blocks, strips, corners)
    thin_rims(strips, corners, pack, pack_corners, thin_strips, thin_corners)
    send_thin(table, thin_strips, thin_corners, send_a)
    pl.semaphore_wait(barrier, 29)
    rims_one.start()

    grad_wide[...] = jnp.zeros_like(grad_wide)
    loads[2].wait()
    for slot in range(2):
        present = jnp.where(table[T_PRESENT + slot] > 0, 1.0, 0.0)
        for row in range(8):
            moved = blocks((product(turns[0], cotangent[slot, row]) * present).astype(BF16))
            grad_blocks[slot, row] = moved
            grad_wide[slot, 2 + row, 2:10] = moved
    take_rims(grad_blocks, grad_strips, grad_corners)
    for slot in range(2):
        for side in range(4):
            keep = jnp.where(piece_of(table, slot, 4 + side)[5] > 0, 1.0, 0.0).astype(BF16)
            at = slot * 4 + side
            grad_corners[at] = grad_corners[at] * keep
    send_rims(table, grad_strips, grad_corners, send_e, T_GIVE_STRIP, T_GIVE_CORNER)
    rims_grad.start()

    loads[3].wait()
    forward[...] = jnp.zeros_like(forward)
    flipped[...] = jnp.zeros_like(flipped)
    for layer in range(2):
        for up in range(3):
            for across in range(3):
                weight = kernels[layer, up, across]
                turned = weight.T
                for side in range(2):
                    at = (up * 4 + side + across) * 128
                    forward[layer, at : at + 128, side * 128 : side * 128 + 128] = weight
                    at = (up * 4 + side + 2 - across) * 128
                    flipped[layer, at : at + 128, side * 128 : side * 128 + 128] = turned
    for slot in range(2):
        for row in (0, 5):
            sources = [grad_wide[slot, row + 2 - up : row + 7 - up] for up in range(3)]
            wide[slot, row : row + 5] = paired_conv(sources, 0, 5, flipped[1])
        total[slot] = wide[slot, 1:9, 1:9]
    give_back(table, wide, turns, send_b, given_strips, given_corners)
    back_two.start()

    for slot in range(2):
        for step in range(4):
            at = slot * 1024 + step * 256
            turned_two[:, at : at + 256] = cells(grad_blocks[slot, step * 2 : step * 2 + 2]).T
    widened[...] = jnp.zeros_like(widened)
    grad_even[...] = jnp.zeros_like(grad_even)
    grad_odd[...] = jnp.zeros_like(grad_odd)
    for slot in range(2):
        padded[slot, 1:9, 1:9] = state_blocks[slot]

    def arrange(rows_even, rows_odd, span):
        def half_rows(slot, row):
            return halves(padded[slot, row : row + 1, span])[0]

        at = slice(span.start * 2, span.stop * 2)
        for row in rows_even:
            both = [half_rows(slot, row) for slot in range(2)]
            even[row, at] = jnp.concatenate(both, axis=1).astype(BF16)
        for row in rows_odd:
            both = [shifted_up(half_rows(slot, row), half_rows(slot, row + 1)) for slot in range(2)]
            odd[row, at] = jnp.concatenate(both, axis=1).astype(BF16)

    arrange(range(1, 9), range(1, 8), slice(1, 9))
    loads[4].wait()
    rims_one.wait()
    widen_thin(table, thin_strips, thin_corners, in_a, unpack, unpack_corners, padded)
    arrange(range(1, 9), range(1, 8), slice(0, 1))
    arrange(range(1, 9), range(1, 8), slice(9, 10))
    arrange((), (0, 8), slice(0, 10))
    for row in (0, 4):
        sources = [odd[row : row + 4], even[row + 1 : row + 5], odd[row + 1 : row + 5]]
        result = paired_conv(sources, 1, 8, forward[0])
        hidden, slopes = gelu_parts(result)
        slope[row : row + 4] = slopes
        for slot in range(2):
            part = hidden[:, :, slot * 8 : slot * 8 + 8].reshape(4, 8, 16, 128).astype(BF16)
            hidden_blocks[slot, row : row + 4] = part
            widened[slot, row + 1 : row + 5, 1:9] = part
    take_rims(hidden_blocks, strips, corners)
    send_rims(table, strips, corners, send_c)
    rims_two.start()

    rims_grad.wait()
    extra = rim_terms(table, in_e, grad_strips, grad_corners, strips, corners, turns, masked)
    windows = []
    for slot in range(2):
        for row in (0, 4):
            taps = [
                cells(widened[slot, row + up : row + up + 4, across : across + 8])
                for up in range(3)
                for across in range(3)
            ]
            windows.append((slot * 1024 + row * 128, taps))
    reduce_two.put(gradient_terms(turned_two, windows, extra))
    broken = jnp.zeros((1, 16, 128), F32) + table[T_OVER].astype(F32)
    for half in range(2):
        reduce_one.half_send[half, 36:37] = jnp.zeros((1, 16, 128), BF16)
        reduce_two.half_send[half, 36:37] = broken.astype(BF16)
    reduce_two.one()

    back_two.wait()
    take_back(table, in_b, given_strips, given_corners, total)
    for row in range(8):
        both = [total[slot, row].astype(BF16).astype(F32).reshape(16, 8, 128) for slot in range(2)]
        grad = (jnp.concatenate(both, axis=1) * slope[row]).astype(BF16)
        grad_even[row + 1, 2:18] = grad
        turned_one[:, row * 256 : row * 256 + 256] = cells(grad).T
    reduce_two.two()
    windows = []
    for row in range(0, 8, 2):
        taps = []
        for source, at in ((odd, row), (even, row + 1), (odd, row + 1)):
            for across in range(3):
                taps.append(cells(source[at : at + 2, 1 + across : 17 + across]))
        windows.append((row * 256, taps))
    reduce_one.put(gradient_terms(turned_one, windows))
    reduce_one.one()

    for row in range(9):
        low = grad_even[row, 2:18].astype(F32)
        high = grad_even[row + 1, 2:18].astype(F32)
        both = [
            shifted_up(low[:, slot * 8 : slot * 8 + 8], high[:, slot * 8 : slot * 8 + 8])
            for slot in range(2)
        ]
        grad_odd[row + 1, 2:18] = jnp.concatenate(both, axis=1).astype(BF16)
    reduce_one.two()

    def returned(row):
        sources = [grad_odd[row + 1 : row + 6], grad_even[row : row + 5], grad_odd[row : row + 5]]
        result = paired_conv(sources, 0, 9, flipped[0])
        blank = jnp.zeros((5, 1, 8, 128), F32)
        for slot in range(2):
            part = jnp.concatenate([blank, result[:, :, slot * 8 : slot * 8 + 8], blank], axis=1)
            wide[slot, row : row + 5] = part.reshape(5, 10, 16, 128)

    def finish(slot):
        present = jnp.where(table[T_PRESENT + slot] > 0, 1.0, 0.0)
        for row in (0, 4):
            sources = [widened[slot, row + up : row + up + 4] for up in range(3)]
            result = paired_conv(sources, 0, 4, forward[1])
            value = state_blocks[slot, row : row + 4].astype(F32) + result
            fresh[slot, row : row + 4] = (value * present).astype(BF16)

    returned(0)
    returned(5)
    give_back(table, wide, turns, send_d, given_strips, given_corners)
    back_one.start()
    for slot in range(2):
        total[slot] = wide[slot, 1:9, 1:9]
    reduce_two.three()
    reduce_one.three()
    rims_two.wait()
    widen(table, hidden_blocks, strips, corners, in_c, turns, widened)
    finish(0)
    finish(1)
    reduce_two.four()
    reduce_one.four()
    back_one.wait()
    take_back(table, in_d, given_strips, given_corners, total)
    for slot in range(2):
        present = jnp.where(table[T_PRESENT + slot] > 0, 1.0, 0.0)
        value = grad_blocks[slot].astype(F32) + total[slot]
        summed[slot] = (value * present).astype(BF16)
    reduce_two.five()
    reduce_one.five()
    reduce_two.end(sums, 1, over)
    reduce_one.end(sums, 0, None)


def settle(scale, fresh, summed, sums, back, next_state, cell_grad, kernel_grads):
    for row in range(fresh.shape[0]):
        next_state[row] = product(back[...], cells(fresh[row])).astype(BF16)
        cell_grad[row] = product(back[...], cells(summed[row])).astype(BF16)
    kernel_grads[...] = sums[...].astype(F32) * scale


def vmem(shape, kind):
    return pltpu.VMEM(shape, kind)


def specs(kinds):
    spaces = {"s": pltpu.SMEM, "v": pltpu.VMEM, "a": pl.ANY}
    return [pl.BlockSpec(memory_space=spaces[kind]) for kind in kinds]


def shape(dims, kind):
    return jax.ShapeDtypeStruct(dims, kind)


TILES = (2, 8, 8, 16, 128)
STRIPS = (8, 8, 16, 128)
CORNERS = (8, 16, 128)
SENT = (6, PART, 16, 128)
THIN_SENT = (6, THIN, 16, 128)
NATURAL = (2, 8, 128, 128)


def sum_buffers():
    return [
        vmem((2, HALF, 16, 128), BF16), vmem((HALF, 16, 128), BF16), vmem((HALF, 16, 128), BF16),
        vmem((15, CHUNK, 16, 128), BF16), vmem((8, CHUNK, 16, 128), BF16), vmem((16, CHUNK, 16, 128), BF16),
        vmem((HALF, 16, 128), BF16), vmem((HALF, 16, 128), BF16), vmem((HALF, 16, 128), F32),
    ]


def finished(scale, fresh, summed, sums, back):
    def rows(count, *tail):
        return pl.BlockSpec((count,) + tail, lambda step: (step,) + (0,) * len(tail))

    return pl.pallas_call(
        functools.partial(settle, scale),
        grid=(2,),
        out_shape=[
            shape((16, 128, 128), BF16), shape((16, 128, 128), BF16), shape((2 * UNITS, 16, 128), F32)
        ],
        in_specs=[
            rows(8, 8, 16, 128), rows(8, 8, 16, 128), rows(UNITS, 16, 128),
            pl.BlockSpec((128, 128), lambda step: (0, 0)),
        ],
        out_specs=[rows(8, 128, 128), rows(8, 128, 128), rows(UNITS, 16, 128)],
        compiler_params=pltpu.CompilerParams(vmem_limit_bytes=10 * 1024 * 1024),
    )(
        fresh.reshape(16, 8, 16, 128), summed.reshape(16, 8, 16, 128),
        sums.reshape(2 * UNITS, 16, 128), back,
    )


def routed(cell_state, cotangent, kernels, slot_of_tile, neighbours, rotations, corner_flags):
    scale = 1.0 / math.sqrt(
        cell_state.shape[0] * lax.axis_size("dp") * slot_of_tile.shape[0] * cell_state.shape[2] ** 2
    )
    turns = permutations()
    pack, pack_corners, unpack, unpack_corners = packings()
    fresh, summed, sums, over = pl.pallas_call(
        whole,
        out_shape=[
            shape(TILES, BF16), shape(TILES, BF16), shape((2, UNITS, 16, 128), BF16), shape((1,), jnp.int32)
        ],
        in_specs=specs("ssssvaaaaavvv"),
        out_specs=specs("vvvs"),
        scratch_shapes=[
            pltpu.SMEM((T_SIZE,), jnp.int32),
            vmem(NATURAL, BF16), vmem(NATURAL, BF16), vmem(kernels.shape, BF16), vmem(turns.shape, BF16),
            vmem((16, 128, 128), BF16), pltpu.SemaphoreType.DMA((5,)), vmem((8, 4, 16, 128), BF16), vmem(CORNERS, F32),
            vmem(TILES, BF16), vmem(TILES, BF16), vmem(TILES, BF16),
            vmem(STRIPS, BF16), vmem(CORNERS, BF16), vmem(STRIPS, BF16), vmem(CORNERS, BF16),
            vmem(STRIPS, BF16), vmem(CORNERS, BF16),
        ]
        + [vmem(THIN_SENT, BF16)]
        + [vmem(SENT, BF16)] * 4
        + [vmem(THIN_SENT, BF16)]
        + [vmem(SENT, BF16)] * 4
        + [
            vmem((2, 1536, 256), BF16), vmem((2, 1536, 256), BF16),
            vmem((2, 12, 12, 16, 128), BF16), vmem((2, 10, 10, 16, 128), F32), vmem(TILES, F32),
            vmem((2, 10, 10, 16, 128), BF16), vmem((2, 10, 10, 16, 128), BF16),
            vmem((10, 20, 16, 128), BF16), vmem((9, 20, 16, 128), BF16),
            vmem((8, 16, 16, 128), F32), vmem((10, 20, 16, 128), BF16), vmem((11, 20, 16, 128), BF16),
            vmem((128, 2048), BF16), vmem((128, 2048), BF16), vmem((512, 1024), BF16),
        ]
        + sum_buffers()
        + sum_buffers()
        + [
            pltpu.SemaphoreType.DMA((5, 2, 6)),
            pltpu.SemaphoreType.DMA((2, 39)),
            pltpu.SemaphoreType.DMA((2, 39)),
        ],
        compiler_params=pltpu.CompilerParams(
            vmem_limit_bytes=VMEM_BYTES, collective_id=1, has_side_effects=True
        ),
    )(
        slot_of_tile, neighbours.T, rotations.T, corner_flags.T, slot_of_tile.reshape(1, -1),
        cell_state.reshape(NATURAL), cotangent.reshape(NATURAL), kernels, jnp.asarray(turns, BF16),
        *(jnp.asarray(part, BF16) for part in (unpack, pack, pack_corners, unpack_corners)),
    )
    back = jnp.asarray(turns[1], BF16)
    arrays = (cell_state, cotangent, kernels, slot_of_tile, neighbours, rotations, corner_flags)

    def fast(*_):
        outs = finished(scale, fresh, summed, sums, back)
        return tuple(out.reshape(like) for out, like in zip(outs, (cell_state.shape, cell_state.shape, kernels.shape)))

    return lax.cond(over[0] == 0, fast, shards, *arrays)


def solution(mesh):
    in_specs = (
        P("dp", "space", None, None, None),
        P("dp", "space", None, None, None),
        P(),
        P(),
        P(),
        P(),
        P(),
    )
    out_specs = (P("dp", "space", None, None, None), P("dp", "space", None, None, None), P())
    return jax.shard_map(routed, mesh=mesh, in_specs=in_specs, out_specs=out_specs, check_vma=False)
```

```python
import functools
import math

import jax
import jax.numpy as jnp
import numpy as np
from jax import lax
from jax.experimental import pallas as pl
from jax.experimental.pallas import tpu as pltpu
from jax.sharding import PartitionSpec as P

RES_BLOCKS = 1
DILATION_ONE = 2
DILATION_TWO = 4
REACH_DEV = 3


CONV_AXES = ("NHWC", "HWIO", "NHWC")


def as_sent(shard):

    def short(part):
        return part.astype(jnp.bfloat16) if part.dtype == jnp.float32 else part

    return jax.tree.map(short, shard)


def shifted(value, axis, steps):
    count = lax.axis_size(axis)
    pairs = [(source, (source + steps) % count) for source in range(count)]
    return lax.ppermute(value, axis, pairs)


def boundary(tile_data, rim_depth):
    extent = tile_data.shape[3]
    far = extent - rim_depth
    sides = [
        tile_data[:, :, :rim_depth],
        tile_data[:, :, :, far:],
        tile_data[:, :, far:],
        tile_data[:, :, :, :rim_depth],
    ]
    blocks = [
        tile_data[:, :, :rim_depth, far:],
        tile_data[:, :, far:, far:],
        tile_data[:, :, far:, :rim_depth],
        tile_data[:, :, :rim_depth, :rim_depth],
    ]
    strips = jnp.stack(
        [jnp.rot90(sides[quarter], quarter, axes=(2, 3)) for quarter in range(4)], axis=2
    )
    corners = jnp.stack(
        [jnp.rot90(blocks[quarter], quarter, axes=(2, 3))[:, :, :, ::-1] for quarter in range(4)],
        axis=2,
    )
    return (strips, corners)


def assemble(tile_data, strips, corners):
    edge_parts = [
        jnp.rot90(strips[:, :, quarter, ::-1, ::-1], -quarter, axes=(2, 3)) for quarter in range(4)
    ]
    corner_parts = [
        jnp.rot90(corners[:, :, quarter, ::-1], -quarter, axes=(2, 3)) for quarter in range(4)
    ]
    top_row = jnp.concatenate([corner_parts[3], edge_parts[0], corner_parts[0]], axis=3)
    middle = jnp.concatenate([edge_parts[3], tile_data, edge_parts[1]], axis=3)
    bottom = jnp.concatenate([corner_parts[2], edge_parts[2], corner_parts[1]], axis=3)
    return jnp.concatenate([top_row, middle, bottom], axis=2)


def rim_pieces(tile_data, rim_depth):
    strips, corners = boundary(tile_data, rim_depth)
    joined = jnp.concatenate([strips, corners], axis=4)
    return joined.reshape((joined.shape[0], joined.shape[1] * 4) + joined.shape[3:])


def conv_apply(padded, kernel, spread):
    merged = padded.reshape((-1,) + padded.shape[2:])
    result = lax.conv_general_dilated(
        merged,
        kernel,
        (1, 1),
        "VALID",
        rhs_dilation=(spread, spread),
        dimension_numbers=CONV_AXES,
        preferred_element_type=jnp.float32,
    )
    return result.reshape(padded.shape[:2] + result.shape[1:])


def conv_back(grad_out, kernel, spread):
    merged = grad_out.reshape((-1,) + grad_out.shape[2:])
    flipped = jnp.swapaxes(kernel[::-1, ::-1], 2, 3)
    margin = 2 * spread
    result = lax.conv_general_dilated(
        merged,
        flipped,
        (1, 1),
        ((margin, margin), (margin, margin)),
        rhs_dilation=(spread, spread),
        dimension_numbers=CONV_AXES,
        preferred_element_type=jnp.float32,
    )
    return result.reshape(grad_out.shape[:2] + result.shape[1:])


def kernel_grad(padded, grad_out, spread):
    extent = grad_out.shape[2]
    tap_terms = []
    for row_tap in range(3):
        for col_tap in range(3):
            window = padded[
                :,
                :,
                row_tap * spread : row_tap * spread + extent,
                col_tap * spread : col_tap * spread + extent,
            ]
            tap_terms.append(
                lax.dot_general(
                    window,
                    grad_out,
                    (((0, 1, 2, 3), (0, 1, 2, 3)), ((), ())),
                    preferred_element_type=jnp.float32,
                )
            )
    stacked = jnp.stack(tap_terms)
    return stacked.reshape((3, 3) + stacked.shape[1:])


def halo_plan(slot_of_tile, neighbours, rotations, corner_flags, slot_count):
    span_count = lax.axis_size("space")
    myself = lax.axis_index("space")
    tile_count = slot_of_tile.shape[0]
    owned = myself * slot_count + jnp.arange(slot_count, dtype=jnp.int32)
    matches = slot_of_tile[None, :] == owned[:, None]
    present = jnp.any(matches, axis=1)
    tile_here = jnp.sum(
        jnp.where(matches, jnp.arange(tile_count, dtype=jnp.int32)[None, :], 0), axis=1
    )
    nearby = jnp.take(neighbours, tile_here, axis=0)
    turn_code = jnp.take(rotations, tile_here, axis=0)
    facing = (jnp.arange(8, dtype=jnp.int32)[None, :] % 4 + 2 + turn_code) % 4
    source = jnp.take(slot_of_tile, nearby)
    holder = source // slot_count
    within = source % slot_count
    offset = jnp.clip(
        (myself - holder + span_count + REACH_DEV) % span_count - REACH_DEV, -REACH_DEV, REACH_DEV
    )
    select = ((offset + REACH_DEV) * slot_count + within) * 4 + facing
    keep_corner = jnp.take(corner_flags, tile_here, axis=0) == 0
    return (select[:, :4].reshape(-1), select[:, 4:].reshape(-1), keep_corner.reshape(-1), present)


def fetch_near(bundle):
    arrived = {0: bundle}
    for offset in list(range(-REACH_DEV, 0)) + list(range(1, REACH_DEV + 1)):
        arrived[offset] = shifted(as_sent(bundle), "space", offset).astype(bundle.dtype)
    return [arrived[offset] for offset in range(-REACH_DEV, REACH_DEV + 1)]


def return_near(parts):
    total = parts[0]
    for offset in list(range(-REACH_DEV, 0)) + list(range(1, REACH_DEV + 1)):
        total = total + shifted(parts[offset].astype(jnp.bfloat16), "space", -offset).astype(
            jnp.float32
        )
    return total


def halo_forward(tile_data, rim_depth, plan):
    pick_edge, pick_corner, keep_corner = plan[:3]
    samples_here, slot_count, extent = (tile_data.shape[0], tile_data.shape[1], tile_data.shape[2])
    channels = tile_data.shape[4]
    gathered = jnp.concatenate(fetch_near(rim_pieces(tile_data, rim_depth)), axis=1)
    edge_part = jnp.take(gathered, pick_edge, axis=1)[:, :, :, :extent]
    corner_part = jnp.take(gathered, pick_corner, axis=1)[:, :, :, extent:]
    corner_part = jnp.where(
        keep_corner[None, :, None, None, None], corner_part, jnp.zeros((), corner_part.dtype)
    )
    strips = edge_part.reshape(samples_here, slot_count, 4, rim_depth, extent, channels)
    corners = corner_part.reshape(samples_here, slot_count, 4, rim_depth, rim_depth, channels)
    return assemble(tile_data, strips, corners)


def halo_backward(grad_wide, rim_depth, plan):
    pick_edge, pick_corner, keep_corner = plan[:3]
    samples_here, slot_count = (grad_wide.shape[0], grad_wide.shape[1])
    extent = grad_wide.shape[2] - 2 * rim_depth
    channels = grad_wide.shape[4]
    tile_zero = jnp.zeros((samples_here, slot_count, extent, extent, channels), jnp.float32)
    strip_zero = jnp.zeros((samples_here, slot_count, 4, rim_depth, extent, channels), jnp.float32)
    corner_zero = jnp.zeros(
        (samples_here, slot_count, 4, rim_depth, rim_depth, channels), jnp.float32
    )
    _, assemble_back = jax.vjp(assemble, tile_zero, strip_zero, corner_zero)
    grad_tiles, grad_strips, grad_corners = assemble_back(grad_wide)
    pieces = slot_count * 4
    grad_corners = grad_corners.reshape(samples_here, pieces, rim_depth, rim_depth, channels)
    grad_corners = jnp.where(keep_corner[None, :, None, None, None], grad_corners, 0.0)
    spread_out = jnp.zeros(
        (samples_here, (2 * REACH_DEV + 1) * pieces, rim_depth, extent + rim_depth, channels),
        jnp.float32,
    )
    spread_out = spread_out.at[:, pick_edge, :, :extent].add(
        grad_strips.reshape(samples_here, pieces, rim_depth, extent, channels)
    )
    spread_out = spread_out.at[:, pick_corner, :, extent:].add(grad_corners)
    parts = {
        offset: spread_out[:, (offset + REACH_DEV) * pieces : (offset + REACH_DEV + 1) * pieces]
        for offset in range(-REACH_DEV, REACH_DEV + 1)
    }
    returned = return_near(parts)
    _, rim_back = jax.vjp(lambda tile_part: rim_pieces(tile_part, rim_depth), tile_zero)
    return grad_tiles + rim_back(returned)[0]


def sum_over(value, axis):
    count = lax.axis_size(axis)
    step = 1
    while step < count:
        pairs = [(source, source ^ step) for source in range(count)]
        value = value + lax.ppermute(value, axis, pairs)
        step *= 2
    return value


def shards(cell_state, cotangent, kernels, slot_of_tile, neighbours, rotations, corner_flags):
    plan = halo_plan(slot_of_tile, neighbours, rotations, corner_flags, cell_state.shape[1])
    keep_slot = plan[3][None, :, None, None, None]
    current = cell_state
    block_at = 0
    widened = halo_forward(current, DILATION_ONE, plan)
    before = conv_apply(widened, kernels[2 * block_at], DILATION_ONE)
    hidden = jax.nn.gelu(before).astype(jnp.bfloat16)
    widened_two = halo_forward(hidden, DILATION_TWO, plan)
    branch = conv_apply(widened_two, kernels[2 * block_at + 1], DILATION_TWO)
    stored = [(widened, before, widened_two)]
    current = (current.astype(jnp.float32) + branch).astype(jnp.bfloat16)
    next_state = jnp.where(keep_slot, current, jnp.zeros((), jnp.bfloat16))
    gradient = jnp.where(keep_slot, cotangent, jnp.zeros((), jnp.bfloat16))
    kernel_terms = [None] * (2 * RES_BLOCKS)
    extent = cell_state.shape[2]
    norm_scale = 1.0 / math.sqrt(
        cell_state.shape[0] * lax.axis_size("dp") * slot_of_tile.shape[0] * extent * extent
    )
    for block_at in reversed(range(RES_BLOCKS)):
        widened, before, widened_two = stored[block_at]
        outer_term = kernel_grad(widened_two, gradient, DILATION_TWO)
        kernel_terms[2 * block_at + 1] = outer_term
        grad_hidden = halo_backward(
            conv_back(gradient, kernels[2 * block_at + 1], DILATION_TWO), DILATION_TWO, plan
        ).astype(jnp.bfloat16)
        _, gelu_back = jax.vjp(jax.nn.gelu, before)
        grad_before = gelu_back(grad_hidden.astype(jnp.float32))[0].astype(jnp.bfloat16)
        inner_term = kernel_grad(widened, grad_before, DILATION_ONE)
        kernel_terms[2 * block_at] = inner_term
        returned = halo_backward(
            conv_back(grad_before, kernels[2 * block_at], DILATION_ONE), DILATION_ONE, plan
        )
        gradient = (gradient.astype(jnp.float32) + returned).astype(jnp.bfloat16)
    stacked = jnp.stack(kernel_terms)
    stacked = sum_over(sum_over(stacked, "space"), "dp")
    return (next_state, gradient, stacked * norm_scale)


MESH_ID = pl.DeviceIdType.MESH
SPAN = 128
STRIP_SLOTS = (1, 2, 2, 2, 2, 1)
CORNER_CAP = 3
PART = CORNER_CAP + 16
THIN = 9
OFFSETS = (-3, -2, -1, 1, 2, 3)
ORDER = (2, 3, 1, 4, 0, 5)
SELF = 6
NOT_THERE = 32
T_STRIP_LIST, T_CORNER_LIST, T_GIVE_STRIP, T_GIVE_CORNER = 0, 12, 36, 48
T_ADD, T_PIECES, T_PRESENT = 72, 104, 200
T_OVER, T_SPARE, T_SIZE = 202, 203, 208
VMEM_BYTES = 56 * 1024 * 1024
F32 = jnp.float32
BF16 = jnp.bfloat16


def cell_order():
    rows, cols = np.meshgrid(np.arange(4), np.arange(4), indexing="ij")
    return ((cols // 2) * 8 + (rows // 2) * 4 + (rows % 2) * 2 + cols % 2).astype(np.int64)


def permutations():
    order = cell_order()
    to_blocks = np.zeros((128, 128), np.float32)
    for row in range(4):
        for col in range(32):
            to_blocks[(col // 4) * 16 + order[row, col % 4], row * 32 + col] = 1
    mats = [to_blocks, to_blocks.T]
    for turn in range(4):
        turned = np.rot90(order, turn)
        small = np.zeros((16, 16), np.float32)
        small[order.reshape(-1), turned.reshape(-1)] = 1
        for flip in range(2):
            line = np.eye(8)[::-1] if flip else np.eye(8)
            mats.append(np.kron(line, small))
    return np.stack(mats)


def turn_matrix(turn, flip):
    return 2 + 2 * turn + flip


def flips(edge, turn):
    side = (edge + 2 + turn) & 1
    once = jnp.where((turn == 1) & (side == 0), 1, 0)
    thrice = jnp.where((turn == 3) & (side == 1), 1, 0)
    return jnp.where(turn == 2, 1, once + thrice)


def packings():
    order = cell_order()
    mats = permutations()
    inner = (order[:2], order[:, 2:], order[2:], order[:, :2])
    ends = (order[:2, 2:], order[2:, 2:], order[2:, :2], order[:2, :2])
    pack = np.zeros((4, 64, 128), np.float32)
    pack_corners = np.zeros((128, 128), np.float32)
    for side in range(4):
        for block in range(8):
            for at, cell in enumerate(sorted(inner[side].reshape(-1))):
                pack[side, block * 8 + at, block * 16 + cell] = 1
        for at, cell in enumerate(sorted(ends[side].reshape(-1))):
            for slot in range(2):
                for copy in range(4):
                    base = (slot * 4 + side) * 16
                    pack_corners[base + copy * 4 + at, base + cell] = 1
    unpack = np.zeros((16, 128, 128), np.float32)
    unpack_corners = np.zeros((16, 16, 128), np.float32)
    for turn in range(4):
        for edge in range(4):
            side = (edge + 2 + turn) % 4
            flip = int(turn == 2 or (turn == 1 and side % 2 == 0) or (turn == 3 and side % 2 == 1))
            unpack[turn * 4 + edge, :, :64] = mats[2 + 2 * turn + flip] @ pack[side].T
            four = pack_corners[side * 16 : side * 16 + 4, side * 16 : side * 16 + 16]
            small = mats[2 + 2 * turn][:16, :16] @ four.T
            unpack_corners[turn * 4 + edge] = np.tile(small, (1, 32))
    return pack, pack_corners, unpack, unpack_corners


def plan_sends(me, order_ref, slot_ref, near_ref, turn_ref, table):
    core = me % 2
    order = order_ref[...]
    spot = lax.broadcasted_iota(jnp.int32, order.shape, 1) + 1
    over = jnp.int32(0)
    found = [[], []]

    def tile_in(offset, slot):
        number = jnp.max(jnp.where(order == (me + offset + SPAN) % SPAN * 2 + slot, spot, 0))
        return number > 0, jnp.maximum(number - 1, 0)

    for where, offset in enumerate(OFFSETS):
        lists = [[jnp.int32(0)] * 2, [jnp.int32(0)] * CORNER_CAP]
        seen = [jnp.int32(0), jnp.int32(0)]
        for slot in range(2):
            there, row = tile_in(offset, slot)
            for piece in range(8):
                kind = piece // 4
                source = slot_ref[near_ref[piece, row]]
                hit = there & (source // 2 == me)
                turn = turn_ref[piece, row] & 3
                packed = (source % 2 * 4 + ((piece + 2 + turn) & 3)) * 4 + turn + 1
                cap = CORNER_CAP if kind else (1, 2, 1 + core, 2 - core, 2, 1)[where]
                late = seen[kind] >= cap
                if offset in (-3, 3):
                    late = late | (core == (0 if offset < 0 else 1))
                over = over + jnp.where(hit & late, 1, 0)
                for rank, old in enumerate(lists[kind]):
                    lists[kind][rank] = jnp.where(hit & (seen[kind] == rank), packed, old)
                seen[kind] = seen[kind] + jnp.where(hit, 1, 0)
        for kind, base in enumerate((T_STRIP_LIST, T_CORNER_LIST)):
            for rank, packed in enumerate(lists[kind]):
                code = where * (4 if kind else 2) + rank
                table[base + code] = jnp.maximum(packed - 1, 0) // 4
                found[kind].append((packed, code))
    return tile_in, found, over


def plan_pieces(me, tile_in, found, slot_ref, near_ref, turn_ref, flag_ref, table):
    seen = [[jnp.int32(0)] * 7, [jnp.int32(0)] * 7]
    given = [[], []]
    for slot in range(2):
        there, row = tile_in(0, slot)
        valid = jnp.where(there, 1, 0)
        table[T_PRESENT + slot] = valid
        for piece in range(8):
            kind = piece // 4
            source = slot_ref[near_ref[piece, row]]
            turn = turn_ref[piece, row] & 3
            offset = jnp.clip((source // 2 - me + 3 + SPAN) % SPAN, 0, 6)
            where = jnp.where(offset == 3, SELF, jnp.where(offset < 3, offset, offset - 1))
            rank = jnp.int32(0)
            for choice in range(7):
                match = jnp.where(offset == choice, valid, 0)
                rank = rank + match * seen[kind][choice]
                seen[kind][choice] = seen[kind][choice] + match
            rank = jnp.minimum(rank, CORNER_CAP - 1 if kind else 1)
            keep = valid
            if kind:
                keep = valid * jnp.where(flag_ref[piece - 4, row] == 0, 1, 0)
            entry = source % 2 * 4 + ((piece + 2 + turn) & 3)
            base = T_PIECES + (slot * 8 + piece) * 6
            for field, value in enumerate((valid, where, rank, turn, entry, keep)):
                table[base + field] = value
            mine = slot * 4 + piece % 4
            own = there & (where == SELF)
            found[kind].append((jnp.where(own, entry * 4 + turn + 1, 0), (24 if kind else 12) + mine))
            code = where * (4 if kind else 2) + rank
            given[kind].append((jnp.where(there & (where != SELF), code, -1), mine))
    for kind, base in enumerate((T_GIVE_STRIP, T_GIVE_CORNER)):
        for where in range(6):
            for rank in range(CORNER_CAP if kind else 2):
                code = where * (4 if kind else 2) + rank
                chosen = jnp.int32(0)
                for place, mine in given[kind]:
                    chosen = jnp.where(place == code, mine, chosen)
                table[base + code] = chosen


def plan_sums(found, over, table):
    for kind in range(2):
        for entry in range(8):
            chosen, count = jnp.int32(NOT_THERE * 4), jnp.int32(0)
            for packed, code in found[kind]:
                turn = packed - 1 - entry * 4
                hit = (turn >= 0) & (turn < 4)
                chosen = jnp.where(hit, code * 4 + turn, chosen)
                count = count + jnp.where(hit, 1, 0)
            table[T_ADD + kind * 16 + entry] = chosen // 4
            table[T_ADD + kind * 16 + 8 + entry] = chosen & 3
            over = over + jnp.maximum(count - 1, 0)
    table[T_OVER] = over


def piece_of(table, slot, piece):
    base = T_PIECES + (slot * 8 + piece) * 6
    return [table[base + field] for field in range(6)]


def blocks(value):
    return value.reshape((-1, 16, 128))


def cells(value):
    return value.reshape((-1, 128))


def product(left, right):
    return jnp.dot(left, right, preferred_element_type=F32)


EDGE_OF = ((0, slice(None)), (slice(None), 7), (7, slice(None)), (slice(None), 0))
CORNER_OF = ((0, 7), (7, 7), (7, 0), (0, 0))
BAND_OF = ((0, slice(1, 9)), (slice(1, 9), 9), (9, slice(1, 9)), (slice(1, 9), 0))
BLOCK_OF = ((0, 9), (9, 9), (9, 0), (0, 0))


def take_rims(tile_ref, strips, corners):
    for slot in range(2):
        for side in range(4):
            strips[slot * 4 + side] = blocks(tile_ref[(slot,) + EDGE_OF[side]])
            corners[slot * 4 + side] = tile_ref[(slot,) + CORNER_OF[side]]


def send_rims(table, strips, corners, send, strip_list=T_STRIP_LIST, corner_list=T_CORNER_LIST):
    for where in range(6):
        for rank in range(STRIP_SLOTS[where]):
            at = CORNER_CAP + rank * 8
            send[where, at : at + 8] = strips[table[strip_list + where * 2 + rank]]
        for rank in range(CORNER_CAP):
            send[where, rank] = corners[table[corner_list + where * 4 + rank]]


def send_thin(table, strips, corners, send):
    group = lax.broadcasted_iota(jnp.int32, (16, 128), 0) // 4
    for where in range(6):
        for rank in range(STRIP_SLOTS[where]):
            send[where, 1 + rank * 4 : 5 + rank * 4] = strips[table[T_STRIP_LIST + where * 2 + rank]]
        unit = corners[table[T_CORNER_LIST + where * 4]]
        for rank in range(1, CORNER_CAP):
            unit = jnp.where(group == rank, corners[table[T_CORNER_LIST + where * 4 + rank]], unit)
        send[where, 0] = unit.astype(BF16)


def thin_rims(strips, corners, pack, pack_corners, thin_strips, thin_corners):
    for entry in range(8):
        packed = product(pack[entry % 4], cells(strips[entry]))
        thin_strips[entry] = blocks(packed.astype(BF16))
    thin_corners[...] = blocks(product(pack_corners[...], cells(corners[...])))


def corner_turns(table, turns, back):
    parts = []
    for slot in range(2):
        for side in range(4):
            fields = piece_of(table, slot, 4 + side)
            turn = (4 - fields[3]) & 3 if back else fields[3]
            rows = turns[turn_matrix(turn, 0)]
            at = (slot * 4 + side) * 16
            parts.append(rows[at : at + 16] * jnp.where(fields[5] > 0, 1.0, 0.0).astype(BF16))
    return jnp.concatenate(parts, axis=0)


def widen(table, tile_ref, strips, corners, arrived, turns, padded):
    for slot in range(2):
        padded[slot, 1:9, 1:9] = tile_ref[slot]
        for edge in range(4):
            valid, where, rank, turn, entry, keep = piece_of(table, slot, edge)
            own = strips[entry]
            other = arrived[jnp.minimum(where, 5), pl.ds(CORNER_CAP + rank * 8, 8)]
            strip = jnp.where(where == SELF, own, other)
            strip = jnp.where(valid > 0, strip, jnp.zeros_like(strip))
            turned = product(turns[turn_matrix(turn, flips(edge, turn))], cells(strip))
            padded[(slot,) + BAND_OF[edge]] = blocks(turned.astype(BF16))
    stack = []
    for slot in range(2):
        for side in range(4):
            valid, where, rank, turn, entry, keep = piece_of(table, slot, 4 + side)
            block = jnp.where(where == SELF, corners[entry], arrived[jnp.minimum(where, 5), rank])
            stack.append(jnp.where(valid > 0, block, jnp.zeros_like(block)))
    turned = product(corner_turns(table, turns, False), jnp.concatenate(stack, axis=0))
    turned = blocks(turned.astype(BF16))
    for slot in range(2):
        for side in range(4):
            padded[(slot,) + BLOCK_OF[side]] = turned[slot * 4 + side]


def give_back(table, wide, turns, send, strips, corners):
    for slot in range(2):
        for edge in range(4):
            valid, where, rank, turn, entry, keep = piece_of(table, slot, edge)
            band = cells(blocks(wide[(slot,) + BAND_OF[edge]])).astype(BF16)
            turned = product(turns[turn_matrix((4 - turn) & 3, flips(edge, turn))], band)
            strips[slot * 4 + edge] = blocks(turned.astype(BF16))
    stack = [wide[(slot,) + BLOCK_OF[side]].astype(BF16) for slot in range(2) for side in range(4)]
    turned = product(corner_turns(table, turns, True), jnp.concatenate(stack, axis=0))
    corners[...] = blocks(turned.astype(BF16))
    send_rims(table, strips, corners, send, T_GIVE_STRIP, T_GIVE_CORNER)


def widen_thin(table, thin_strips, thin_corners, arrived, unpack, unpack_corners, padded):
    for slot in range(2):
        for edge in range(4):
            valid, where, rank, turn, entry, keep = piece_of(table, slot, edge)
            other = arrived[jnp.minimum(where, 5), pl.ds(1 + rank * 4, 4)]
            strip = jnp.where(where == SELF, thin_strips[entry], other)
            strip = jnp.where(valid > 0, strip, jnp.zeros_like(strip))
            turned = product(unpack[turn * 4 + edge][:, :64], cells(strip))
            padded[(slot,) + BAND_OF[edge]] = blocks(turned.astype(BF16))
    lane = lax.broadcasted_iota(jnp.int32, (16, 128), 1)
    stack, parts = [], []
    for slot in range(2):
        for side in range(4):
            valid, where, rank, turn, entry, keep = piece_of(table, slot, 4 + side)
            block = jnp.where(where == SELF, thin_corners[entry], arrived[jnp.minimum(where, 5), 0].astype(F32))
            stack.append(jnp.where(valid > 0, block, jnp.zeros_like(block)).astype(BF16))
            first = (slot * 4 + side) * 16 + jnp.where(where == SELF, 0, rank) * 4
            chosen = (lane >= first) & (lane < first + 4) & (keep > 0)
            rows = unpack_corners[turn * 4 + side].astype(F32)
            parts.append(jnp.where(chosen, rows, jnp.zeros_like(rows)).astype(BF16))
    turned = product(jnp.concatenate(parts, axis=0), jnp.concatenate(stack, axis=0))
    turned = blocks(turned.astype(BF16))
    for slot in range(2):
        for side in range(4):
            padded[(slot,) + BLOCK_OF[side]] = turned[slot * 4 + side]


def owner_of(table, kind, entry):
    code = table[T_ADD + kind * 16 + entry]
    turn = table[T_ADD + kind * 16 + 8 + entry]
    return code, turn, (entry % 4 - 2 - turn) & 3


def copied_strip(code, arrived, strips):
    far = jnp.minimum(code, 11)
    near = jnp.clip(code - 12, 0, 7)
    part = jnp.where(code < 12, arrived[far // 2, pl.ds(CORNER_CAP + far % 2 * 8, 8)], strips[near])
    return jnp.where(code == NOT_THERE, jnp.zeros_like(part), part)


def copied_corner(code, arrived, corners):
    far = jnp.minimum(code, 23)
    near = jnp.clip(code - 24, 0, 7)
    part = jnp.where(code < 24, arrived[far // 4, far % 4], corners[near])
    return jnp.where(code == NOT_THERE, jnp.zeros_like(part), part)


def take_back(table, arrived, strips, corners, total):
    for slot in range(2):
        for side in range(4):
            at = (slot,) + EDGE_OF[side]
            code = owner_of(table, 0, slot * 4 + side)[0]
            total[at] = total[at] + copied_strip(code, arrived, strips).astype(F32)
    for slot in range(2):
        for side in range(4):
            at = (slot,) + CORNER_OF[side]
            code = owner_of(table, 1, slot * 4 + side)[0]
            total[at] = total[at] + copied_corner(code, arrived, corners).astype(F32)


STRIP_TAPS = (
    ((0, 0), (0, 1), (0, 2)),
    ((0, 2), (1, 2), (2, 2)),
    ((2, 0), (2, 1), (2, 2)),
    ((0, 0), (1, 0), (2, 0)),
)
CORNER_TAPS = ((0, 2), (2, 2), (2, 0), (0, 0))


def rim_terms(
    table, arrived, grad_strips, grad_corners, strips, corners, turns, edge_weights, corner_weights, masked, total
):
    rims = []
    blank = jnp.zeros((16, 128), BF16)

    def shifts(value, order):
        longer = jnp.concatenate([blank, value, blank], axis=0)
        return jnp.concatenate([longer[step * 16 : step * 16 + 128] for step in order], axis=1)

    for entry in range(8):
        code, turn, edge = owner_of(table, 0, entry)
        strip = cells(copied_strip(code, arrived, grad_strips))
        grad = strip.T
        for choice in range(4):
            chosen = jnp.where(edge == choice, grad, jnp.zeros_like(grad))
            masked[choice * 128 : choice * 128 + 128, entry * 128 : entry * 128 + 128] = chosen
        flip = flips(edge, turn)
        band = product(turns[turn_matrix(turn, flip)], cells(strips[entry])).astype(BF16)
        rims.append(shifts(band, (0, 1, 2)))
        ring = product(shifts(strip, (2, 1, 0)), edge_weights[edge]).astype(BF16)
        at = (entry // 4,) + EDGE_OF[entry % 4]
        total[at] = total[at] + blocks(product(turns[turn_matrix((4 - turn) & 3, flip)], ring))
    edges = product(masked[...], jnp.concatenate(rims, axis=0))
    lane = lax.broadcasted_iota(jnp.int32, (128, 128), 1) // 16
    which = jnp.zeros((128, 128), jnp.int32)
    grads, parts, backs, sides = [], [], [], []
    for entry in range(8):
        code, turn, side = owner_of(table, 1, entry)
        grads.append(copied_corner(code, arrived, grad_corners))
        sides.append(side)
        backs.append(turns[turn_matrix((4 - turn) & 3, 0)][entry * 16 : entry * 16 + 16])
        which = jnp.where(lane == entry, side, which)
        parts.append(turns[turn_matrix(turn, 0)][entry * 16 : entry * 16 + 16])
    block = product(jnp.concatenate(parts, axis=0), cells(corners[...])).astype(BF16)
    stack = jnp.concatenate(grads, axis=0)
    rings = product(stack, corner_weights[...])
    chosen = []
    for entry in range(8):
        rows = rings[entry * 16 : entry * 16 + 16]
        value = rows[:, :128]
        for choice in range(1, 4):
            value = jnp.where(sides[entry] == choice, rows[:, choice * 128 : choice * 128 + 128], value)
        chosen.append(value.astype(BF16))
    rings = blocks(product(jnp.concatenate(backs, axis=0), jnp.concatenate(chosen, axis=0)))
    for entry in range(8):
        at = (entry // 4,) + CORNER_OF[entry % 4]
        total[at] = total[at] + rings[entry]
    grad = stack.astype(F32).T
    spread = [jnp.where(which == choice, grad, jnp.zeros_like(grad)) for choice in range(4)]
    ends = product(jnp.concatenate(spread, axis=0).astype(BF16), block)
    sums = [None] * 9
    for choice in range(4):
        rows = slice(choice * 128, choice * 128 + 128)
        found = [(tap, edges[rows, step * 128 : step * 128 + 128]) for step, tap in enumerate(STRIP_TAPS[choice])]
        found.append((CORNER_TAPS[choice], ends[rows]))
        for (up, across), value in found:
            old = sums[up * 3 + across]
            sums[up * 3 + across] = value if old is None else old + value
    return sums


def halves(value):
    return value.astype(F32).reshape(value.shape[0], value.shape[1] * 2, 8, 128)


def shifted_up(upper, lower):
    low = lax.broadcasted_iota(jnp.int32, upper.shape, upper.ndim - 2) < 4
    mixed = jnp.where(low, lower, upper)
    return jnp.concatenate([mixed[..., 4:, :], mixed[..., :4, :]], axis=mixed.ndim - 2)


def gelu_parts(value):
    root = math.sqrt(2.0 / math.pi)
    square = value * value
    bent = jnp.tanh(root * (value + 0.044715 * (value * square)))
    half = 0.5 * (1.0 + bent)
    slope = half + 0.5 * value * (1.0 - bent * bent) * (root * (1.0 + 3 * 0.044715 * square))
    return (value * half, slope)


UNITS = 72
HALF = 37
CHUNK = 3


def chunk_start(index):
    return (index * (HALF - CHUNK)) // 15


class Swap:
    def __init__(self, me, send, arrived, sems, corner_units=CORNER_CAP, strip_units=8):
        core = me % 2
        far, mate, other = 5 - 5 * core, 3 - core, 2 + core
        self.copies = []
        for where, offset, strips, send_at, recv_at in (
            (other, 2 * core - 1, 1, 2, 2),
            (1, -2, 2, 1, 4),
            (4, 2, 2, 4, 1),
            (far, 3 - 6 * core, 1, 0, 0),
            (mate, 1 - 2 * core, 2, 3, 3),
        ):
            size = corner_units + strip_units * strips
            self.copies.append(
                pltpu.make_async_remote_copy(
                    src_ref=send.at[where, pl.ds(0, size)],
                    dst_ref=arrived.at[5 - where, pl.ds(0, size)],
                    send_sem=sems.at[0, send_at],
                    recv_sem=sems.at[1, recv_at],
                    device_id={"space": lax.rem(me + offset + SPAN, SPAN)},
                    device_id_type=MESH_ID,
                )
            )

    def start(self):
        for copy in self.copies:
            copy.start()

    def wait(self):
        for copy in self.copies:
            copy.wait()


class Place:
    def __init__(self):
        me = lax.axis_index("space")
        self.me = me
        self.core, self.y, self.z, self.x_lo = me % 2, me // 2 % 4, me // 8 % 8, me // 64
        self.plane = (lax.axis_index("dp") * 2 + self.x_lo) * 4 + self.y
        self.mate = {"space": me + 1 - 2 * self.core}

    def at_plane(self, index):
        return {
            "dp": index // 8,
            "space": ((index // 4 % 2) * 8 + self.z) * 8 + index % 4 * 2 + self.core,
        }

    def at_line(self, index):
        return {"space": (self.x_lo * 8 + index) * 8 + self.y * 2 + self.core}


class Sum:
    def __init__(self, place, buffers, sems):
        self.place = place
        self.half_send, self.half_in, self.plane_send, self.plane_in, self.line_in = buffers[:5]
        self.wide_in, self.pair_send, self.pair_in, self.acc = buffers[5:]
        self.sems = sems
        self.copies = []

    def copy(self, source, target, index, where):
        one = pltpu.make_async_remote_copy(
            src_ref=source,
            dst_ref=target,
            send_sem=self.sems.at[0, index],
            recv_sem=self.sems.at[1, index],
            device_id=where,
            device_id_type=MESH_ID,
        )
        one.start()
        self.copies.append(one)

    def put(self, terms):
        for tap, term in enumerate(terms):
            value = blocks(term.astype(BF16))
            for part in range(2):
                half, at = divmod(tap * 8 + part * 4, 36)
                self.half_send[half, at : at + 4] = value[part * 4 : part * 4 + 4]

    def wait(self):
        for one in self.copies:
            one.wait()
        self.copies = []

    def one(self):
        place = self.place
        self.copy(self.half_send.at[1 - place.core], self.half_in, 0, place.mate)

    def two(self):
        place = self.place
        self.wait()
        self.acc[...] = self.half_send[place.core].astype(F32) + self.half_in[...].astype(F32)
        self.plane_send[...] = self.acc[...].astype(BF16)
        for step in range(1, 16):
            peer = lax.rem(place.plane + step, 16)
            source = self.plane_send.at[pl.ds(chunk_start(peer), CHUNK)]
            self.copy(source, self.plane_in.at[step - 1], step, place.at_plane(peer))

    def three(self):
        place = self.place
        self.wait()
        total = self.acc[pl.ds(chunk_start(place.plane), CHUNK)]
        for step in range(15):
            total = total + self.plane_in[step].astype(F32)
        self.line_in[place.z] = total.astype(BF16)
        for step in range(1, 8):
            peer = lax.rem(place.z + step, 8)
            self.copy(self.line_in.at[place.z], self.line_in.at[place.z], 15 + step, place.at_line(peer))

    def four(self):
        place = self.place
        self.wait()
        total = self.line_in[0].astype(F32)
        for index in range(1, 8):
            total = total + self.line_in[index].astype(F32)
        self.wide_in[place.plane] = total.astype(BF16)
        for step in range(1, 16):
            peer = lax.rem(place.plane + step, 16)
            here = self.wide_in.at[place.plane]
            self.copy(here, here, 22 + step, place.at_plane(peer))

    def five(self):
        self.wait()
        for index in range(16):
            at = chunk_start(index)
            self.pair_send[at : at + CHUNK] = self.wide_in[index]
        self.copy(self.pair_send, self.pair_in, 38, self.place.mate)

    def end(self, out, layer, over):
        self.wait()
        core = self.place.core
        mine, other = self.pair_send[...], self.pair_in[...]
        out[layer, :36] = jnp.where(core == 0, mine[:36], other[:36])
        out[layer, 36:] = jnp.where(core == 0, other[:36], mine[:36])
        if over is not None:
            over[0] = jnp.where(jnp.max(mine[36].astype(F32)) > 0.0, 1, 0)


def columns(value, first, count):
    rows, wide = value.shape[:2]
    paired = value.reshape(rows, wide // 2, 2, 16, 128)
    return [
        cells(paired[:, (first + step) // 2 : (first + step) // 2 + count, (first + step) % 2])
        for step in range(4)
    ]


def split_pairs(result, rows, count):
    wide = result.reshape(rows, count, 16, 256)
    return jnp.stack([wide[..., :128], wide[..., 128:]], axis=2).reshape(rows, count * 2, 16, 128)


def paired_conv(sources, first, count, weight):
    taps = [tap for value in sources for tap in columns(value, first, count)]
    result = product(jnp.concatenate(taps, axis=1), weight)
    return split_pairs(result, sources[0].shape[0], count)


def gradient_terms(turned, windows, extra=None):
    total = None
    for at, taps in windows:
        part = product(turned[:, at : at + taps[0].shape[0]], jnp.concatenate(taps, axis=1))
        total = part if total is None else total + part
    terms = [total[:, tap * 128 : tap * 128 + 128] for tap in range(9)]
    if extra is not None:
        terms = [term if more is None else term + more for term, more in zip(terms, extra)]
    return [term.T for term in terms]


def whole(
    slot_ref, near_ref, turn_ref, flag_ref, order_ref,
    state_far, cotangent_far, kernels_far, turns_far, unpack_far, pack, pack_corners, unpack_corners,
    fresh_far, summed_far, sums, over,
    fresh, summed, edge_weights, corner_weights, table, state, cotangent, kernels, turns, unpack, load_sems, thin_strips, thin_corners, state_blocks, grad_blocks, hidden_blocks, strips, corners, given_strips, given_corners,
    grad_strips, grad_corners,
    send_a, send_c, send_d, send_e, in_a, in_c, in_d, in_e,
    forward, flipped, grad_wide, wide, total, padded, widened, even, odd, slope, grad_even, grad_odd,
    turned_one, turned_two, masked, *rest,
):
    swap_sems, one_sems, two_sems = rest[18:]
    loads = []
    pairs = (
        (turns_far, turns), (state_far, state), (cotangent_far, cotangent), (kernels_far, kernels),
        (unpack_far, unpack),
    )
    for index, (source, target) in enumerate(pairs):
        loads.append(pltpu.make_async_copy(source, target, load_sems.at[index]))
        loads[index].start()
    place = Place()
    me = place.me
    barrier = pltpu.get_barrier_semaphore()

    def greet(where):
        pl.semaphore_signal(barrier, inc=1, device_id=where, device_id_type=MESH_ID)

    for offset in OFFSETS:
        greet({"space": lax.rem(me + offset + SPAN, SPAN)})
    greet(place.mate)
    for step in range(1, 16):
        greet(place.at_plane(lax.rem(place.plane + step, 16)))
    for step in range(1, 8):
        greet(place.at_line(lax.rem(place.z + step, 8)))

    rims_one = Swap(me, send_a, in_a, swap_sems.at[0], 1, 4)
    rims_two = Swap(me, send_c, in_c, swap_sems.at[1])
    back_one = Swap(me, send_d, in_d, swap_sems.at[2])
    rims_grad = Swap(me, send_e, in_e, swap_sems.at[3])
    reduce_one = Sum(place, rest[:9], one_sems)
    reduce_two = Sum(place, rest[9:18], two_sems)

    tile_in, found, over_count = plan_sends(me, order_ref, slot_ref, near_ref, turn_ref, table)
    loads[0].wait()
    loads[1].wait()
    for slot in range(2):
        for row in range(8):
            moved = product(turns[0], state[slot, row])
            state_blocks[slot, row] = blocks(moved.astype(BF16))
    take_rims(state_blocks, strips, corners)
    thin_rims(strips, corners, pack, pack_corners, thin_strips, thin_corners)
    send_thin(table, thin_strips, thin_corners, send_a)
    pl.semaphore_wait(barrier, 29)
    rims_one.start()
    plan_pieces(me, tile_in, found, slot_ref, near_ref, turn_ref, flag_ref, table)

    grad_wide[...] = jnp.zeros_like(grad_wide)
    loads[2].wait()
    for slot in range(2):
        present = jnp.where(table[T_PRESENT + slot] > 0, 1.0, 0.0)
        for row in range(8):
            moved = blocks((product(turns[0], cotangent[slot, row]) * present).astype(BF16))
            grad_blocks[slot, row] = moved
            grad_wide[slot, 2 + row, 2:10] = moved
    take_rims(grad_blocks, grad_strips, grad_corners)
    for slot in range(2):
        for side in range(4):
            keep = jnp.where(piece_of(table, slot, 4 + side)[5] > 0, 1.0, 0.0).astype(BF16)
            at = slot * 4 + side
            grad_corners[at] = grad_corners[at] * keep
    send_rims(table, grad_strips, grad_corners, send_e, T_GIVE_STRIP, T_GIVE_CORNER)
    rims_grad.start()
    plan_sums(found, over_count, table)

    loads[3].wait()

    def build_forward(layer):
        forward[layer] = jnp.zeros(forward.shape[1:], BF16)
        for up in range(3):
            for across in range(3):
                for side in range(2):
                    at = (up * 4 + side + across) * 128
                    forward[layer, at : at + 128, side * 128 : side * 128 + 128] = kernels[layer, up, across]

    def build_flipped(layer):
        flipped[layer] = jnp.zeros(flipped.shape[1:], BF16)
        for up in range(3):
            for across in range(3):
                turned = kernels[layer, up, across].T
                for side in range(2):
                    at = (up * 4 + side + 2 - across) * 128
                    flipped[layer, at : at + 128, side * 128 : side * 128 + 128] = turned
                if layer == 1:
                    for edge in range(4):
                        for step, tap in enumerate(STRIP_TAPS[edge]):
                            if tap == (up, across):
                                edge_weights[edge, step * 128 : step * 128 + 128] = turned
                        if CORNER_TAPS[edge] == (up, across):
                            corner_weights[:, edge * 128 : edge * 128 + 128] = turned

    build_forward(0)
    build_flipped(1)
    for slot in range(2):
        for row in (0, 4):
            sources = [grad_wide[slot, row + 3 - up : row + 7 - up] for up in range(3)]
            total[slot, row : row + 4] = paired_conv(sources, 1, 4, flipped[1])

    for slot in range(2):
        for step in range(4):
            at = slot * 1024 + step * 256
            turned_two[:, at : at + 256] = cells(grad_blocks[slot, step * 2 : step * 2 + 2]).T
    widened[...] = jnp.zeros_like(widened)
    grad_even[...] = jnp.zeros_like(grad_even)
    grad_odd[...] = jnp.zeros_like(grad_odd)
    for slot in range(2):
        padded[slot, 1:9, 1:9] = state_blocks[slot]

    def arrange(rows_even, rows_odd, span):
        def half_rows(slot, row):
            return halves(padded[slot, row : row + 1, span])[0]

        at = slice(span.start * 2, span.stop * 2)
        for row in rows_even:
            both = [half_rows(slot, row) for slot in range(2)]
            even[row, at] = jnp.concatenate(both, axis=1).astype(BF16)
        for row in rows_odd:
            both = [shifted_up(half_rows(slot, row), half_rows(slot, row + 1)) for slot in range(2)]
            odd[row, at] = jnp.concatenate(both, axis=1).astype(BF16)

    arrange(range(1, 9), range(1, 8), slice(1, 9))
    loads[4].wait()
    rims_one.wait()
    widen_thin(table, thin_strips, thin_corners, in_a, unpack, unpack_corners, padded)
    arrange(range(1, 9), range(1, 8), slice(0, 1))
    arrange(range(1, 9), range(1, 8), slice(9, 10))
    arrange((), (0, 8), slice(0, 10))
    for row in (0, 4):
        sources = [odd[row : row + 4], even[row + 1 : row + 5], odd[row + 1 : row + 5]]
        result = paired_conv(sources, 1, 8, forward[0])
        hidden, slopes = gelu_parts(result)
        slope[row : row + 4] = slopes
        for slot in range(2):
            part = hidden[:, :, slot * 8 : slot * 8 + 8].reshape(4, 8, 16, 128).astype(BF16)
            hidden_blocks[slot, row : row + 4] = part
            widened[slot, row + 1 : row + 5, 1:9] = part
    take_rims(hidden_blocks, strips, corners)
    send_rims(table, strips, corners, send_c)
    rims_two.start()

    rims_grad.wait()
    extra = rim_terms(
        table, in_e, grad_strips, grad_corners, strips, corners, turns,
        edge_weights, corner_weights, masked, total,
    )
    windows = []
    for slot in range(2):
        for row in (0, 4):
            taps = [
                cells(widened[slot, row + up : row + up + 4, across : across + 8])
                for up in range(3)
                for across in range(3)
            ]
            windows.append((slot * 1024 + row * 128, taps))
    reduce_two.put(gradient_terms(turned_two, windows, extra))
    broken = jnp.zeros((1, 16, 128), F32) + table[T_OVER].astype(F32)
    for half in range(2):
        reduce_one.half_send[half, 36:37] = jnp.zeros((1, 16, 128), BF16)
        reduce_two.half_send[half, 36:37] = broken.astype(BF16)
    reduce_two.one()

    for row in range(8):
        both = [total[slot, row].astype(BF16).astype(F32).reshape(16, 8, 128) for slot in range(2)]
        grad = (jnp.concatenate(both, axis=1) * slope[row]).astype(BF16)
        grad_even[row + 1, 2:18] = grad
        turned_one[:, row * 256 : row * 256 + 256] = cells(grad).T
    reduce_two.two()
    windows = []
    for row in range(0, 8, 2):
        taps = []
        for source, at in ((odd, row), (even, row + 1), (odd, row + 1)):
            for across in range(3):
                taps.append(cells(source[at : at + 2, 1 + across : 17 + across]))
        windows.append((row * 256, taps))
    reduce_one.put(gradient_terms(turned_one, windows))
    reduce_one.one()

    build_flipped(0)
    build_forward(1)
    for row in range(9):
        low = grad_even[row, 2:18].astype(F32)
        high = grad_even[row + 1, 2:18].astype(F32)
        both = [
            shifted_up(low[:, slot * 8 : slot * 8 + 8], high[:, slot * 8 : slot * 8 + 8])
            for slot in range(2)
        ]
        grad_odd[row + 1, 2:18] = jnp.concatenate(both, axis=1).astype(BF16)
    reduce_one.two()

    def returned(row):
        sources = [grad_odd[row + 1 : row + 6], grad_even[row : row + 5], grad_odd[row : row + 5]]
        result = paired_conv(sources, 0, 9, flipped[0])
        blank = jnp.zeros((5, 1, 8, 128), F32)
        for slot in range(2):
            part = jnp.concatenate([blank, result[:, :, slot * 8 : slot * 8 + 8], blank], axis=1)
            wide[slot, row : row + 5] = part.reshape(5, 10, 16, 128)

    def finish(slot):
        present = jnp.where(table[T_PRESENT + slot] > 0, 1.0, 0.0)
        for row in (0, 4):
            sources = [widened[slot, row + up : row + up + 4] for up in range(3)]
            result = paired_conv(sources, 0, 4, forward[1])
            value = state_blocks[slot, row : row + 4].astype(F32) + result
            fresh[slot, row : row + 4] = (value * present).astype(BF16)

    returned(0)
    returned(5)
    give_back(table, wide, turns, send_d, given_strips, given_corners)
    back_one.start()
    for slot in range(2):
        total[slot] = wide[slot, 1:9, 1:9]
    reduce_two.three()
    reduce_one.three()
    rims_two.wait()
    widen(table, hidden_blocks, strips, corners, in_c, turns, widened)
    finish(0)
    finish(1)
    stores = [pltpu.make_async_copy(fresh, fresh_far, load_sems.at[5])]
    stores[0].start()
    reduce_two.four()
    reduce_one.four()
    back_one.wait()
    take_back(table, in_d, given_strips, given_corners, total)
    for slot in range(2):
        present = jnp.where(table[T_PRESENT + slot] > 0, 1.0, 0.0)
        value = grad_blocks[slot].astype(F32) + total[slot]
        summed[slot] = (value * present).astype(BF16)
    stores.append(pltpu.make_async_copy(summed, summed_far, load_sems.at[6]))
    stores[1].start()
    reduce_two.five()
    reduce_one.five()
    reduce_two.end(sums, 1, over)
    reduce_one.end(sums, 0, None)
    for store in stores:
        store.wait()


def settle(scale, fresh, summed, sums, back, next_state, cell_grad, kernel_grads):
    for row in range(fresh.shape[0]):
        next_state[row] = product(back[...], cells(fresh[row])).astype(BF16)
        cell_grad[row] = product(back[...], cells(summed[row])).astype(BF16)
    kernel_grads[...] = sums[...].astype(F32) * scale


def vmem(shape, kind):
    return pltpu.VMEM(shape, kind)


def specs(kinds):
    spaces = {"s": pltpu.SMEM, "v": pltpu.VMEM, "a": pl.ANY}
    return [pl.BlockSpec(memory_space=spaces[kind]) for kind in kinds]


def shape(dims, kind):
    return jax.ShapeDtypeStruct(dims, kind)


TILES = (2, 8, 8, 16, 128)
STRIPS = (8, 8, 16, 128)
CORNERS = (8, 16, 128)
SENT = (6, PART, 16, 128)
THIN_SENT = (6, THIN, 16, 128)
NATURAL = (2, 8, 128, 128)


def sum_buffers():
    return [
        vmem((2, HALF, 16, 128), BF16), vmem((HALF, 16, 128), BF16), vmem((HALF, 16, 128), BF16),
        vmem((15, CHUNK, 16, 128), BF16), vmem((8, CHUNK, 16, 128), BF16), vmem((16, CHUNK, 16, 128), BF16),
        vmem((HALF, 16, 128), BF16), vmem((HALF, 16, 128), BF16), vmem((HALF, 16, 128), F32),
    ]


def finished(scale, fresh, summed, sums, back):
    def rows(count, *tail):
        return pl.BlockSpec((count,) + tail, lambda step: (step,) + (0,) * len(tail))

    return pl.pallas_call(
        functools.partial(settle, scale),
        grid=(2,),
        out_shape=[
            shape((16, 128, 128), BF16), shape((16, 128, 128), BF16), shape((2 * UNITS, 16, 128), F32)
        ],
        in_specs=[
            rows(8, 8, 16, 128), rows(8, 8, 16, 128), rows(UNITS, 16, 128),
            pl.BlockSpec((128, 128), lambda step: (0, 0)),
        ],
        out_specs=[rows(8, 128, 128), rows(8, 128, 128), rows(UNITS, 16, 128)],
        compiler_params=pltpu.CompilerParams(vmem_limit_bytes=10 * 1024 * 1024),
    )(
        fresh.reshape(16, 8, 16, 128), summed.reshape(16, 8, 16, 128),
        sums.reshape(2 * UNITS, 16, 128), back,
    )


def routed(cell_state, cotangent, kernels, slot_of_tile, neighbours, rotations, corner_flags):
    scale = 1.0 / math.sqrt(
        cell_state.shape[0] * lax.axis_size("dp") * slot_of_tile.shape[0] * cell_state.shape[2] ** 2
    )
    turns = permutations()
    pack, pack_corners, unpack, unpack_corners = packings()
    fresh, summed, sums, over = pl.pallas_call(
        whole,
        out_shape=[
            shape(TILES, BF16), shape(TILES, BF16), shape((2, UNITS, 16, 128), BF16), shape((1,), jnp.int32)
        ],
        in_specs=specs("ssssvaaaaavvv"),
        out_specs=specs("aavs"),
        scratch_shapes=[
            vmem(TILES, BF16), vmem(TILES, BF16), vmem((4, 384, 128), BF16), vmem((128, 512), BF16),
            pltpu.SMEM((T_SIZE,), jnp.int32),
            vmem(NATURAL, BF16), vmem(NATURAL, BF16), vmem(kernels.shape, BF16), vmem(turns.shape, BF16),
            vmem((16, 128, 128), BF16), pltpu.SemaphoreType.DMA((7,)), vmem((8, 4, 16, 128), BF16), vmem(CORNERS, F32),
            vmem(TILES, BF16), vmem(TILES, BF16), vmem(TILES, BF16),
            vmem(STRIPS, BF16), vmem(CORNERS, BF16), vmem(STRIPS, BF16), vmem(CORNERS, BF16),
            vmem(STRIPS, BF16), vmem(CORNERS, BF16),
        ]
        + [vmem(THIN_SENT, BF16)]
        + [vmem(SENT, BF16)] * 3
        + [vmem(THIN_SENT, BF16)]
        + [vmem(SENT, BF16)] * 3
        + [
            vmem((2, 1536, 256), BF16), vmem((2, 1536, 256), BF16),
            vmem((2, 12, 12, 16, 128), BF16), vmem((2, 10, 10, 16, 128), F32), vmem(TILES, F32),
            vmem((2, 10, 10, 16, 128), BF16), vmem((2, 10, 10, 16, 128), BF16),
            vmem((10, 20, 16, 128), BF16), vmem((9, 20, 16, 128), BF16),
            vmem((8, 16, 16, 128), F32), vmem((10, 20, 16, 128), BF16), vmem((11, 20, 16, 128), BF16),
            vmem((128, 2048), BF16), vmem((128, 2048), BF16), vmem((512, 1024), BF16),
        ]
        + sum_buffers()
        + sum_buffers()
        + [
            pltpu.SemaphoreType.DMA((4, 2, 6)),
            pltpu.SemaphoreType.DMA((2, 39)),
            pltpu.SemaphoreType.DMA((2, 39)),
        ],
        compiler_params=pltpu.CompilerParams(
            vmem_limit_bytes=VMEM_BYTES, collective_id=1, has_side_effects=True
        ),
    )(
        slot_of_tile, neighbours.T, rotations.T, corner_flags.T, slot_of_tile.reshape(1, -1),
        cell_state.reshape(NATURAL), cotangent.reshape(NATURAL), kernels, jnp.asarray(turns, BF16),
        *(jnp.asarray(part, BF16) for part in (unpack, pack, pack_corners, unpack_corners)),
    )
    back = jnp.asarray(turns[1], BF16)
    arrays = (cell_state, cotangent, kernels, slot_of_tile, neighbours, rotations, corner_flags)

    def fast(*_):
        outs = finished(scale, fresh, summed, sums, back)
        return tuple(out.reshape(like) for out, like in zip(outs, (cell_state.shape, cell_state.shape, kernels.shape)))

    return lax.cond(over[0] == 0, fast, shards, *arrays)


def solution(mesh):
    in_specs = (
        P("dp", "space", None, None, None),
        P("dp", "space", None, None, None),
        P(),
        P(),
        P(),
        P(),
        P(),
    )
    out_specs = (P("dp", "space", None, None, None), P("dp", "space", None, None, None), P())
    return jax.shard_map(routed, mesh=mesh, in_specs=in_specs, out_specs=out_specs, check_vma=False)
```
